32 devices in a mesh: dp: 4 (over y, x), chan: 8 (over z, core).
Axes of the slice: x: 2, y: 2, z: 4, core: 2. Of those that a mesh axis runs over, the one named last changes fastest.
Arguments:
- images: bfloat16 [4, 768, 128, 128], P('dp', 'chan'), may hold values from -6 to 6
- cotangent: bfloat16 [4, 768, 128, 128], P('dp', 'chan'), may hold values from -6 to 6
- image_sizes: int32 [4, 2], replicated, may hold values from 64 to 128
- slot_image: int32 [4], replicated, may hold values from 0 to 3, each once
- rows_rate: float32 [768, 32], P('chan'), may hold values from 0.01 to 0.3
- rows_freq: float32 [768, 32], P('chan'), may hold values from 0 to 1.5
- rows_real: float32 [768, 32], P('chan'), may hold values from -0.36 to 0.36
- rows_imag: float32 [768, 32], P('chan'), may hold values from -0.36 to 0.36
- cols_rate: float32 [768, 32], P('chan'), may hold values from 0.01 to 0.3
- cols_freq: float32 [768, 32], P('chan'), may hold values from 0 to 1.5
- cols_real: float32 [768, 32], P('chan'), may hold values from -0.36 to 0.36
- cols_imag: float32 [768, 32], P('chan'), may hold values from -0.36 to 0.36
- skip_gain: float32 [768], P('chan'), may hold values from 0.25 to 1.75
- norm_gain: float32 [768], replicated, may hold values from 0.5 to 1.5
- norm_bias: float32 [768], replicated, may hold values from -1.8 to 1.8
- weight_in: bfloat16 [768, 3072], P(None, 'chan'), may hold values from -0.21875 to 0.21875
- bias_in: bfloat16 [3072], P('chan'), may hold values from -1.796875 to 1.796875
- weight_out: bfloat16 [3072, 768], P('chan'), may hold values from -0.15625 to 0.15625
- bias_out: float32 [768], P('chan'), may hold values from -3 to 3
- layer_scale: float32 [768], P('chan'), may hold values from 0.5 to 1.5
Outputs:
- output: bfloat16 [4, 768, 128, 128], P('dp', 'chan')
- input_grad: float32 [4, 768, 128, 128], P('dp', 'chan')
- rows_rate_grad: float32 [768, 32], P('chan')
- rows_freq_grad: float32 [768, 32], P('chan')
- rows_real_grad: float32 [768, 32], P('chan')
- rows_imag_grad: float32 [768, 32], P('chan')
- cols_rate_grad: float32 [768, 32], P('chan')
- cols_freq_grad: float32 [768, 32], P('chan')
- cols_real_grad: float32 [768, 32], P('chan')
- cols_imag_grad: float32 [768, 32], P('chan')
- skip_gain_grad: float32 [768], P('chan')
- norm_gain_grad: float32 [768], replicated
- norm_bias_grad: float32 [768], replicated
- weight_in_grad: float32 [768, 3072], P(None, 'chan')
- bias_in_grad: float32 [3072], P('chan')
- weight_out_grad: float32 [3072, 768], P('chan')
- bias_out_grad: float32 [768], P('chan')
- layer_scale_grad: float32 [768], P('chan')
The draws below stay inside these ranges and needn't reach their ends.
Inputs may be any that keep to these rules, and one draw needn't show every extreme that they name: `image_sizes`: heights (column 0) and widths (column 1) of the images, in list order. Slot s of the batch holds image slot_image[s] of the list; each image once.
All inputs are finite; a program needn't handle non-finite values.
Results may differ from the reference program's by a relative error of at most 0.0074.
Values may be sent and summed in bfloat16 or wider, within the bound.
A program may use at most 640 MiB of HBM per device.

```python
import math
import jax
import jax.numpy as jnp
from jax import lax

C = 768
FF = 3072
MODES = 32
SIDE = 128
IMAGES = 4


def place_ends(values, rng, low, top_value):
    place = [jax.random.randint(jax.random.fold_in(rng, axis), (), 0, length) for axis, length in enumerate(values.shape)]
    widest = values.shape.index(max(values.shape))
    next_to = place[:widest] + [(place[widest] + 1) % values.shape[widest]] + place[widest + 1:]
    return values.at[tuple(place)].set(low).at[tuple(next_to)].set(top_value)


def level_of(rng, shape, pieces, least, top_value):
    factor_of = 1.0
    for axis_at, parts in pieces:
        steps = jax.random.uniform(jax.random.fold_in(jax.random.fold_in(rng, 6), axis_at), (parts,), jnp.float32, least / len(pieces), top_value / len(pieces))
        factor_of = factor_of * jnp.repeat(jnp.exp(steps), shape[axis_at] // parts).reshape((-1,) + (1,) * (len(shape) - 1 - axis_at))
    return factor_of


def normal_values(key, shape, scale, limit, shards=(), kind=jnp.bfloat16):
    factor_of = level_of(key, shape, shards, -0.22, 0.18) if shards else 1.0
    entries = jax.random.normal(key, shape, jnp.float32) * scale * factor_of
    return jnp.minimum(jnp.maximum(entries, -limit), limit).astype(kind)


def setup_inputs(seed: int = 0) -> dict:
    arg_keys = jax.random.split(jax.random.key(seed), 21)
    images = normal_values(arg_keys[0], (IMAGES, C, SIDE, SIDE), 1.0, 6.0, ((0, 4), (1, 8)))
    cotangent = normal_values(arg_keys[1], (IMAGES, C, SIDE, SIDE), 1.0, 6.0, ((0, 4), (1, 8)))
    image_sizes = place_ends(jax.random.randint(arg_keys[2], (IMAGES, 2), SIDE // 2, SIDE + 1), jax.random.fold_in(arg_keys[2], 1), SIDE // 2, SIDE).astype(jnp.int32)
    slot_image = jax.random.permutation(arg_keys[3], IMAGES).astype(jnp.int32)
    rows_rate = jnp.clip(jnp.exp(math.log(0.3) - 3.4011974 * jax.random.uniform(arg_keys[4], (C, MODES), jnp.float32) ** level_of(arg_keys[4], (C, MODES), ((0, 8),), -0.2, 0.2)), 0.01, 0.3)
    rows_freq = jnp.clip(1.5 * jax.random.uniform(arg_keys[5], (C, MODES), jnp.float32) ** level_of(arg_keys[5], (C, MODES), ((0, 8),), -0.2, 0.2), 0.0, 1.5)
    rows_real = normal_values(arg_keys[6], (C, MODES), 0.06, 0.36, ((0, 8),), jnp.float32)
    rows_imag = normal_values(arg_keys[7], (C, MODES), 0.06, 0.36, ((0, 8),), jnp.float32)
    cols_rate = jnp.clip(jnp.exp(math.log(0.3) - 3.4011974 * jax.random.uniform(arg_keys[8], (C, MODES), jnp.float32) ** level_of(arg_keys[8], (C, MODES), ((0, 8),), -0.2, 0.2)), 0.01, 0.3)
    cols_freq = jnp.clip(1.5 * jax.random.uniform(arg_keys[9], (C, MODES), jnp.float32) ** level_of(arg_keys[9], (C, MODES), ((0, 8),), -0.2, 0.2), 0.0, 1.5)
    cols_real = normal_values(arg_keys[10], (C, MODES), 0.06, 0.36, ((0, 8),), jnp.float32)
    cols_imag = normal_values(arg_keys[11], (C, MODES), 0.06, 0.36, ((0, 8),), jnp.float32)
    skip_gain = jnp.clip(1.0 + 0.15 * jax.random.normal(arg_keys[12], (C,), jnp.float32), 0.25, 1.75)
    norm_gain = jnp.clip(1.0 + 0.1 * jax.random.normal(arg_keys[13], (C,), jnp.float32), 0.5, 1.5)
    norm_bias = normal_values(arg_keys[14], (C,), 0.3, 1.8, (), jnp.float32)
    weight_in = normal_values(arg_keys[15], (C, FF), C ** -0.5, 0.21875, ((1, 8),))
    bias_in = normal_values(arg_keys[16], (FF,), 0.3, 1.796875, ((0, 8),))
    weight_out = normal_values(arg_keys[17], (FF, C), (FF // 2) ** -0.5, 0.15625, ((0, 8),))
    bias_out = normal_values(arg_keys[18], (C,), 0.5, 3.0, ((0, 8),), jnp.float32)
    layer_scale = jnp.clip(1.0 + 0.1 * jax.random.normal(arg_keys[19], (C,), jnp.float32), 0.5, 1.5)
    return dict(images=images, cotangent=cotangent, image_sizes=image_sizes, slot_image=slot_image, rows_rate=rows_rate, rows_freq=rows_freq, rows_real=rows_real, rows_imag=rows_imag, cols_rate=cols_rate, cols_freq=cols_freq, cols_real=cols_real, cols_imag=cols_imag, skip_gain=skip_gain, norm_gain=norm_gain, norm_bias=norm_bias, weight_in=weight_in, bias_in=bias_in, weight_out=weight_out, bias_out=bias_out, layer_scale=layer_scale)


eps_norm = 1e-06
highest = lax.Precision.HIGHEST

@jax.custom_vjp
def low(v):
    return lax.optimization_barrier(v.astype(jnp.bfloat16)).astype(jnp.float32)

@jax.custom_vjp
def low_back(v):
    return v

def low_keep(v):
    return (low(v), None)

def low_pass(kept, grad):
    return (grad,)

def back_keep(v):
    return (v, None)

def back_low(kept, grad):
    return (low(grad),)
low.defvjp(low_keep, low_pass)
low_back.defvjp(back_keep, back_low)

def kernel_taps(rate_vals, freq_vals, real_part, imag_part, length):
    offsets = jnp.arange(length, dtype=jnp.float32)
    decays = jnp.exp(-rate_vals[:, :, None] * offsets)
    angles = freq_vals[:, :, None] * offsets
    return lax.optimization_barrier(jnp.sum(decays * (real_part[:, :, None] * jnp.cos(angles) - imag_part[:, :, None] * jnp.sin(angles)), axis=1))

def toeplitz(filter_taps):
    length = filter_taps.shape[1]
    offsets = jnp.arange(length, dtype=jnp.int32)
    lag_index = offsets[:, None] - offsets[None, :]
    return jnp.where(lag_index[None] >= 0, filter_taps[:, jnp.maximum(lag_index, 0)], 0.0)

def forward(image, inside, weights_all):
    rows_rate, rows_freq, rows_real, rows_imag, cols_rate, cols_freq, cols_real, cols_imag, skip_gain, norm_gain, norm_bias, weight_in, bias_in, weight_out, bias_out, layer_scale = weights_all
    channels = image.shape[0]
    length = image.shape[1]
    masked_in = image * inside[None]
    rows_op = toeplitz(kernel_taps(rows_rate, rows_freq, rows_real, rows_imag, length))
    cols_op = toeplitz(kernel_taps(cols_rate, cols_freq, cols_real, cols_imag, length))
    along_rows = jnp.einsum('chi,cij->chj', rows_op, masked_in, precision=highest)
    mixed_out = jnp.einsum('chj,cwj->chw', along_rows, cols_op, precision=highest) + skip_gain[:, None, None] * masked_in
    mixed_low = low(mixed_out).reshape(channels, length * length)
    center = mixed_low - lax.optimization_barrier(jnp.mean(mixed_low, axis=0, keepdims=True))
    inverse = lax.rsqrt(lax.optimization_barrier(jnp.mean(center * center, axis=0, keepdims=True)) + eps_norm)
    normed = low(center * inverse * norm_gain[:, None] + norm_bias[:, None])
    before = low_back(jnp.einsum('cf,cp->fp', weight_in, normed, precision=highest) + bias_in[:, None])
    active = low(jax.nn.gelu(before, approximate=False))
    branch = low_back(jnp.einsum('fc,fp->cp', weight_out, active, precision=highest))
    result = image.reshape(channels, length * length) + layer_scale[:, None] * (branch + bias_out[:, None])
    return (inside.reshape(1, length * length) * result).reshape(image.shape)

def reference(images, cotangent, image_sizes, slot_image, rows_rate, rows_freq, rows_real, rows_imag, cols_rate, cols_freq, cols_real, cols_imag, skip_gain, norm_gain, norm_bias, weight_in, bias_in, weight_out, bias_out, layer_scale):
    weights_all = (rows_rate.astype(jnp.float32), rows_freq.astype(jnp.float32), rows_real.astype(jnp.float32), rows_imag.astype(jnp.float32), cols_rate.astype(jnp.float32), cols_freq.astype(jnp.float32), cols_real.astype(jnp.float32), cols_imag.astype(jnp.float32), skip_gain.astype(jnp.float32), norm_gain.astype(jnp.float32), norm_bias.astype(jnp.float32), weight_in.astype(jnp.float32), bias_in.astype(jnp.float32), weight_out.astype(jnp.float32), bias_out.astype(jnp.float32), layer_scale.astype(jnp.float32))
    slot_sizes = image_sizes[slot_image]
    offsets = jnp.arange(images.shape[2], dtype=jnp.int32)
    inside_all = ((offsets[None, :, None] < slot_sizes[:, 0, None, None]) & (offsets[None, None, :] < slot_sizes[:, 1, None, None])).astype(jnp.float32)

    def step_image(totals, entry):
        image, grad_image, inside = entry
        result, pullback = jax.vjp(lambda xval, wval: forward(xval, inside, wval), image.astype(jnp.float32), weights_all)
        image_grad, weight_grads = pullback(grad_image.astype(jnp.float32))
        totals = jax.tree.map(lambda left, right: left + right, totals, weight_grads)
        return (totals, (result.astype(jnp.bfloat16), image_grad))
    zeros_all = tuple((jnp.zeros_like(weight) for weight in weights_all))
    totals, (outputs, input_grads) = lax.scan(step_image, zeros_all, (images, cotangent, inside_all))
    return (outputs, input_grads, totals[0], totals[1], totals[2], totals[3], totals[4], totals[5], totals[6], totals[7], totals[8], totals[9], totals[10], totals[11], totals[12], totals[13], totals[14], totals[15])
```

```python
import functools

import jax
import jax.numpy as jnp
from jax import lax
from jax.experimental import pallas as pl
from jax.experimental.pallas import tpu as pltpu
from jax.sharding import PartitionSpec as P

eps_norm = 1e-06
highest = lax.Precision.HIGHEST


def kernel_taps(rate_vals, freq_vals, real_part, imag_part, length):
    offsets = jnp.arange(length, dtype=jnp.float32)
    decays = jnp.exp(-rate_vals[:, :, None] * offsets)
    angles = freq_vals[:, :, None] * offsets
    return jnp.sum(
        decays
        * (real_part[:, :, None] * jnp.cos(angles) - imag_part[:, :, None] * jnp.sin(angles)),
        axis=1,
    )


def toeplitz(filter_taps):
    length = filter_taps.shape[1]
    offsets = jnp.arange(length, dtype=jnp.int32)
    lag_index = offsets[:, None] - offsets[None, :]
    return jnp.where(lag_index[None] >= 0, filter_taps[:, jnp.maximum(lag_index, 0)], 0.0)


def mixer(
    masked_in,
    rows_rate,
    rows_freq,
    rows_real,
    rows_imag,
    cols_rate,
    cols_freq,
    cols_real,
    cols_imag,
    skip_gain,
):
    rows_op = toeplitz(kernel_taps(rows_rate, rows_freq, rows_real, rows_imag, masked_in.shape[2]))
    cols_op = toeplitz(kernel_taps(cols_rate, cols_freq, cols_real, cols_imag, masked_in.shape[3]))
    along_rows = jnp.einsum("chi,ncij->nchj", rows_op, masked_in, precision=highest)
    return (
        jnp.einsum("nchj,cwj->nchw", along_rows, cols_op, precision=highest)
        + skip_gain[None, :, None, None] * masked_in
    )


def normalize(values, norm_gain, norm_bias):
    center = values - jnp.mean(values, axis=-2, keepdims=True)
    inverse = lax.rsqrt(jnp.mean(center * center, axis=-2, keepdims=True) + eps_norm)
    scaled = center * inverse
    return (scaled * norm_gain[:, None] + norm_bias[:, None], scaled, inverse)


def gelu_exact(values):
    return jax.nn.gelu(values, approximate=False)


def plain_body(
    images,
    cotangent,
    image_sizes,
    slot_image,
    rows_rate,
    rows_freq,
    rows_real,
    rows_imag,
    cols_rate,
    cols_freq,
    cols_real,
    cols_imag,
    skip_gain,
    norm_gain,
    norm_bias,
    weight_in,
    bias_in,
    weight_out,
    bias_out,
    layer_scale,
):
    slot_count, chan_count, length = (images.shape[0], images.shape[1], images.shape[2])
    pixels = length * length
    image_count = slot_image.shape[0]
    slot_ids = lax.axis_index("dp") * slot_count + jnp.arange(slot_count, dtype=jnp.int32)
    choose = (slot_ids[:, None] == jnp.arange(image_count, dtype=jnp.int32)[None, :]).astype(
        jnp.int32
    )
    picked = jnp.sum(choose * slot_image[None, :], axis=1)
    owners = (picked[:, None] == jnp.arange(image_count, dtype=jnp.int32)[None, :]).astype(
        jnp.int32
    )
    heights = jnp.sum(owners * image_sizes[None, :, 0], axis=1)
    widths = jnp.sum(owners * image_sizes[None, :, 1], axis=1)
    offsets = jnp.arange(length, dtype=jnp.int32)
    inside = (
        (offsets[None, :, None] < heights[:, None, None])
        & (offsets[None, None, :] < widths[:, None, None])
    ).astype(jnp.float32)
    masked_in = images.astype(jnp.float32) * inside[:, None]
    mixed_out, mixer_pull = jax.vjp(
        mixer,
        masked_in,
        rows_rate,
        rows_freq,
        rows_real,
        rows_imag,
        cols_rate,
        cols_freq,
        cols_real,
        cols_imag,
        skip_gain,
    )
    mixed_low = mixed_out.astype(jnp.bfloat16).reshape(slot_count, chan_count, pixels)
    mask_flat = inside.reshape(slot_count, 1, pixels)
    residual = images.astype(jnp.float32).reshape(slot_count, chan_count, pixels)
    grad_out = cotangent.astype(jnp.float32).reshape(slot_count, chan_count, pixels) * mask_flat
    chan_offset = lax.axis_index("chan") * chan_count
    all_channels = norm_gain.shape[0]
    slot_item = 0
    gathered = lax.all_gather(mixed_low[slot_item], "chan", axis=0, tiled=True)
    normed, scaled, inverse = normalize(gathered.astype(jnp.float32), norm_gain, norm_bias)
    normed_low = normed.astype(jnp.bfloat16)
    before = (
        jnp.einsum("cf,cp->fp", weight_in, normed_low, preferred_element_type=jnp.float32)
        + bias_in.astype(jnp.float32)[:, None]
    )
    active = gelu_exact(before).astype(jnp.bfloat16)

    def project(first_row, row_count, active=active):
        return jnp.einsum("fc,fp->cp", weight_out, active, preferred_element_type=jnp.float32)

    branch_list = [
        lax.psum_scatter(
            project(jnp.int32(0), chan_count * lax.axis_size("chan")),
            "chan",
            scatter_dimension=0,
            tiled=True,
        )
    ]
    scaled_part = lax.dynamic_slice_in_dim(scaled, chan_offset, chan_count, 0)
    stored = [(normed_low, before, active, scaled_part, inverse)]
    branch_all = jnp.stack(branch_list)
    shifted = branch_all + bias_out[None, :, None]
    output = (
        (mask_flat * (residual + layer_scale[None, :, None] * shifted))
        .astype(jnp.bfloat16)
        .reshape(images.shape)
    )
    scale_grad = jnp.sum(grad_out * shifted, axis=(0, 2))
    branch_grad = layer_scale[None, :, None] * grad_out
    bias_out_grad = jnp.sum(branch_grad, axis=(0, 2))
    branch_low = branch_grad.astype(jnp.bfloat16)
    hidden_count = weight_in.shape[1]
    out_weight_grad = jnp.zeros((hidden_count, all_channels), jnp.float32)
    gain_shard = lax.dynamic_slice_in_dim(norm_gain, chan_offset, chan_count, 0)
    slot_item = 0
    normed_low, before, active, scaled_part, inverse = stored[slot_item]

    def absorb(totals, shard_rows, first_row, active=active):
        hidden_grad = jnp.einsum(
            "fc,cp->fp", weight_out, shard_rows, preferred_element_type=jnp.float32
        )
        product_part = jnp.einsum(
            "fp,cp->fc", active, shard_rows, preferred_element_type=jnp.float32
        )
        return (hidden_grad, product_part)

    hidden_start = jnp.zeros((hidden_count, pixels), jnp.float32)
    hidden_grad, out_weight_grad = absorb(
        (hidden_start, out_weight_grad),
        lax.all_gather(branch_low[slot_item], "chan", axis=0, tiled=True),
        jnp.int32(0),
    )
    gelu_pull = jax.vjp(gelu_exact, before)[1]
    before_grad = gelu_pull(hidden_grad)[0].astype(jnp.bfloat16)
    in_weight_grad = jnp.einsum(
        "cp,fp->cf", normed_low, before_grad, preferred_element_type=jnp.float32
    )
    in_bias_grad = jnp.sum(before_grad.astype(jnp.float32), axis=1)

    def spread_back(first_row, row_count, before_grad=before_grad):
        return jnp.einsum("cf,fp->cp", weight_in, before_grad, preferred_element_type=jnp.float32)

    normed_grad = lax.psum_scatter(
        spread_back(jnp.int32(0), chan_count * lax.axis_size("chan")),
        "chan",
        scatter_dimension=0,
        tiled=True,
    )
    weighted = normed_grad * gain_shard[:, None]
    pixel_sums = (
        lax.psum(jnp.sum(weighted, axis=0).astype(jnp.bfloat16), "chan").astype(jnp.float32),
        lax.psum(jnp.sum(weighted * scaled_part, axis=0).astype(jnp.bfloat16), "chan").astype(
            jnp.float32
        ),
    )
    mixed_grads = [
        inverse
        * (
            weighted
            - pixel_sums[0][None, :] / all_channels
            - scaled_part * pixel_sums[1][None, :] / all_channels
        )
    ]
    gain_part = jnp.sum(normed_grad * scaled_part, axis=1)
    shift_part = jnp.sum(normed_grad, axis=1)
    mixed_grad_all = jnp.stack(mixed_grads)
    gain_grad = lax.dynamic_update_slice_in_dim(
        jnp.zeros((all_channels,), jnp.float32), gain_part, chan_offset, 0
    )
    shift_grad = lax.dynamic_update_slice_in_dim(
        jnp.zeros((all_channels,), jnp.float32), shift_part, chan_offset, 0
    )
    pulled = mixer_pull(mixed_grad_all.reshape(images.shape))
    input_grad = inside[:, None] * (cotangent.astype(jnp.float32) + pulled[0])
    summed = lax.psum(
        (
            in_weight_grad,
            out_weight_grad,
            in_bias_grad,
            bias_out_grad,
            scale_grad,
            pulled[1],
            pulled[2],
            pulled[3],
            pulled[4],
            pulled[5],
            pulled[6],
            pulled[7],
            pulled[8],
            pulled[9],
        ),
        "dp",
    )
    norm_sums = lax.psum((gain_grad, shift_grad), ("dp", "chan"))
    return (
        output,
        input_grad,
        summed[5],
        summed[6],
        summed[7],
        summed[8],
        summed[9],
        summed[10],
        summed[11],
        summed[12],
        summed[13],
        norm_sums[0],
        norm_sums[1],
        summed[0],
        summed[2],
        summed[1],
        summed[3],
        summed[4],
    )


MESH = pl.DeviceIdType.MESH
GROUP = 16
LINES = 4
STEP_HIDDEN = 512
mebi = 1024 * 1024


def dot_nn(left, right):
    return lax.dot_general(left, right, (((1,), (0,)), ((), ())), preferred_element_type=jnp.float32)


def dot_nt(left, right):
    return lax.dot_general(left, right, (((1,), (1,)), ((), ())), preferred_element_type=jnp.float32)


def split_low(values):
    high = values.astype(jnp.bfloat16)
    return high, (values - high.astype(jnp.float32)).astype(jnp.bfloat16)


def lag_matrix(line, side, keep):
    spread = pltpu.roll(jnp.broadcast_to(line, (side, side)), 0, 1, stride=1, stride_axis=0)
    return jnp.where(keep, spread, 0.0)


def lag_sums(matrix, side, keep):
    turned = pltpu.roll(jnp.where(keep, matrix, 0.0), 0, 1, stride=1, stride_axis=0)
    return jnp.sum(turned, axis=0, keepdims=True)


def meet(n):
    me = lax.axis_index("chan")
    barrier = pltpu.get_barrier_semaphore()
    for shift in range(1, n):
        pl.semaphore_signal(
            barrier, inc=1, device_id={"chan": lax.rem(me + shift, n)}, device_id_type=MESH
        )
    pl.semaphore_wait(barrier, n - 1)
    return me


def send_part(stage, target, me, peer, part, send_sem, recv_sem, shift):
    return pltpu.make_async_remote_copy(
        src_ref=stage.at[peer, part],
        dst_ref=target.at[me, part],
        send_sem=send_sem.at[shift],
        recv_sem=recv_sem.at[shift],
        device_id={"chan": peer},
        device_id_type=MESH,
    )


def wait_parts(stage, target, me, n, send_sem, recv_sem):
    for shift in range(1, n):
        peer = lax.rem(me + shift, n)
        origin = lax.rem(me + n - shift, n)
        pltpu.make_async_remote_copy(
            src_ref=stage.at[peer],
            dst_ref=target.at[origin],
            send_sem=send_sem.at[shift],
            recv_sem=recv_sem.at[shift],
            device_id={"chan": peer},
            device_id_type=MESH,
        ).wait()


def mixer_kernel(
    n,
    sizes_ref,
    image_ref,
    cot_ref,
    rows_ref,
    cols_ref,
    skip_ref,
    scale_ref,
    mixed_ref,
    back_ref,
    sums_ref,
    mixed_stage,
    back_stage,
    wide,
    send_m,
    recv_m,
    send_b,
    recv_b,
    own_sem,
):
    count, side, _ = image_ref.shape
    parts = count // GROUP
    block = side // n
    me = meet(n)
    row_at = lax.broadcasted_iota(jnp.int32, (side, side), 0)
    col_at = lax.broadcasted_iota(jnp.int32, (side, side), 1)
    inside = (row_at < sizes_ref[0]) & (col_at < sizes_ref[1])
    lower = row_at >= col_at
    upper = row_at <= col_at

    def turn(stage, part):
        @pl.loop(0, n)
        def _(owner):
            for line in range(block):
                tile = wide[pl.ds(owner * block + line, GROUP, stride=side), :]
                stage[owner, part, line] = tile.astype(jnp.bfloat16)

    def send(stage, target, part, send_sem, recv_sem):
        for shift in range(1, n):
            send_part(stage, target, me, lax.rem(me + shift, n), part, send_sem, recv_sem, shift).start()

    @pl.loop(0, parts)
    def _(part):
        @pl.loop(0, GROUP)
        def _(item):
            chan = part * GROUP + item
            grad_out = jnp.where(inside, cot_ref[chan].astype(jnp.float32), 0.0)
            scaled = grad_out * scale_ref[pl.ds(chan, 1), :]
            sums_ref[pl.ds(chan, 1), :] = jnp.sum(scaled, axis=0, keepdims=True)
            wide[pl.ds(pl.multiple_of(item * side, side), side), :] = scaled

        turn(back_stage, part)
        send(back_stage, back_ref, part, send_b, recv_b)

    @pl.loop(0, parts)
    def _(part):
        @pl.loop(0, GROUP)
        def _(item):
            chan = part * GROUP + item
            masked = jnp.where(inside, image_ref[chan].astype(jnp.float32), 0.0)
            masked_low = masked.astype(jnp.bfloat16)
            rows_high, rows_low = split_low(lag_matrix(rows_ref[pl.ds(chan, 1), 0, :], side, lower))
            cols_high, cols_low = split_low(lag_matrix(cols_ref[pl.ds(chan, 1), 1, :], side, upper))
            along = dot_nn(
                jnp.concatenate([rows_high, rows_low], axis=1),
                jnp.concatenate([masked_low, masked_low], axis=0),
            )
            along_high, along_low = split_low(along)
            mixed = dot_nn(
                jnp.concatenate([along_high, along_low], axis=1),
                jnp.concatenate([cols_high, cols_high], axis=0),
            ) + dot_nn(along_high, cols_low)
            mixed = mixed + skip_ref[pl.ds(chan, 1), :] * masked
            wide[pl.ds(pl.multiple_of(item * side, side), side), :] = mixed

        turn(mixed_stage, part)
        send(mixed_stage, mixed_ref, part, send_m, recv_m)

    own_b = pltpu.make_async_copy(back_stage.at[me], back_ref.at[me], own_sem.at[0])
    own_m = pltpu.make_async_copy(mixed_stage.at[me], mixed_ref.at[me], own_sem.at[1])
    own_b.start()
    own_m.start()
    own_b.wait()
    own_m.wait()
    wait_parts(back_stage, back_ref, me, n, send_b, recv_b)
    wait_parts(mixed_stage, mixed_ref, me, n, send_m, recv_m)


def mixer_forward(n, sizes, images, cotangent, rows_pair, cols_pair, skip_wide, scale_wide):
    count, side, _ = images.shape
    shape = (n, count // GROUP, side // n, GROUP, side)
    vmem = pl.BlockSpec(memory_space=pltpu.VMEM)
    hbm = pl.BlockSpec(memory_space=pl.ANY)
    return pl.pallas_call(
        functools.partial(mixer_kernel, n),
        out_shape=(
            jax.ShapeDtypeStruct(shape, jnp.bfloat16),
            jax.ShapeDtypeStruct(shape, jnp.bfloat16),
            jax.ShapeDtypeStruct((count, side), jnp.float32),
        ),
        in_specs=[pl.BlockSpec(memory_space=pltpu.SMEM)] + [vmem] * 6,
        out_specs=(hbm, hbm, vmem),
        scratch_shapes=[
            pltpu.VMEM(shape, jnp.bfloat16),
            pltpu.VMEM(shape, jnp.bfloat16),
            pltpu.VMEM((GROUP * side, side), jnp.float32),
            pltpu.SemaphoreType.DMA((n,)),
            pltpu.SemaphoreType.DMA((n,)),
            pltpu.SemaphoreType.DMA((n,)),
            pltpu.SemaphoreType.DMA((n,)),
            pltpu.SemaphoreType.DMA((2,)),
        ],
        compiler_params=pltpu.CompilerParams(
            collective_id=0, has_side_effects=True, vmem_limit_bytes=40 * mebi
        ),
        name="mixer_forward",
    )(sizes, images, cotangent, rows_pair, cols_pair, skip_wide, scale_wide)


def gelu_parts(value):
    bell = jnp.exp(-0.5 * value * value)
    inner = 1.0 / (1.0 + (0.3275911 * 0.7071067811865476) * jnp.abs(value))
    series = 1.061405429 * inner - 1.453152027
    series = series * inner + 1.421413741
    series = series * inner - 0.284496736
    series = series * inner + 0.254829592
    tail = (0.5 * inner) * series * bell
    return jnp.where(value < 0.0, tail, 1.0 - tail), bell * 0.3989422804014327


def mlp_kernel(
    n,
    mixed_ref,
    back_ref,
    in_turned_ref,
    in_ref,
    out_ref,
    out_turned_ref,
    gain_ref,
    shift_ref,
    bias_ref,
    grad_ref,
    branch_ref,
    active_ref,
    before_grad_ref,
    normed_ref,
    cots_ref,
    gain_grad_ref,
    shift_grad_ref,
    grad_stage,
    branch_stage,
    active_keep,
    before_keep,
    normed_keep,
    cots_keep,
    scaled_keep,
    inverse_keep,
    branch_sum,
    grad_sum,
    send_g,
    recv_g,
    send_r,
    recv_r,
    own_sem,
    keep_sem,
):
    side = mixed_ref.shape[-1]
    groups = mixed_ref.shape[1]
    block = mixed_ref.shape[2]
    hidden, channels = out_ref.shape
    local = channels // n
    steps = block // LINES
    width = LINES * side
    me = meet(n)
    gain_grad_ref[...] = jnp.zeros_like(gain_grad_ref)
    shift_grad_ref[...] = jnp.zeros_like(shift_grad_ref)

    def keeps(slot, step):
        span = pl.ds(pl.multiple_of(step * width, width), width)
        pairs = (
            (active_keep, active_ref),
            (before_keep, before_grad_ref),
            (normed_keep, normed_ref),
            (cots_keep, cots_ref),
        )
        return [
            pltpu.make_async_copy(kept.at[slot], whole.at[:, span], keep_sem.at[slot, at])
            for at, (kept, whole) in enumerate(pairs)
        ]

    @pl.loop(0, steps)
    def _(step):
        slot = lax.rem(step, 2)

        @pl.when(step >= 2)
        def _():
            for copy in keeps(slot, step - 2):
                copy.wait()

        for line in range(LINES):
            row = step * LINES + line
            lanes = pl.ds(line * side, side)
            order = [(owner, group) for owner in range(n) for group in range(groups)]
            mixed = jnp.concatenate(
                [mixed_ref[owner, group, row].astype(jnp.float32) for owner, group in order], axis=0
            )
            mean = jnp.sum(mixed, axis=0, keepdims=True) * (1.0 / channels)
            center = mixed - mean
            var = jnp.sum(center * center, axis=0, keepdims=True) * (1.0 / channels)
            inverse = lax.rsqrt(var + eps_norm)
            scaled = center * inverse
            normed_keep[slot, :, lanes] = (scaled * gain_ref[...] + shift_ref[...]).astype(jnp.bfloat16)
            scaled_keep[:, lanes] = scaled
            inverse_keep[:, lanes] = inverse
            cots_keep[slot, :, lanes] = jnp.concatenate(
                [back_ref[owner, group, row] for owner, group in order], axis=0
            )

        @pl.loop(0, hidden // STEP_HIDDEN)
        def _(part):
            span = pl.ds(pl.multiple_of(part * STEP_HIDDEN, STEP_HIDDEN), STEP_HIDDEN)
            before = dot_nn(in_turned_ref[span, :], normed_keep[slot]) + bias_ref[span, :]
            inside, bell = gelu_parts(before)
            active = (before * inside).astype(jnp.bfloat16)
            active_grad = dot_nn(out_ref[span, :], cots_keep[slot])
            before_grad = (active_grad * (inside + before * bell)).astype(jnp.bfloat16)
            active_keep[slot, span, :] = active
            before_keep[slot, span, :] = before_grad
            branch = dot_nn(out_turned_ref[:, span], active)
            grad = dot_nn(in_ref[:, span], before_grad)

            @pl.when(part == 0)
            def _():
                branch_sum[...] = branch
                grad_sum[...] = grad

            @pl.when(part > 0)
            def _():
                branch_sum[...] += branch
                grad_sum[...] += grad

        for copy in keeps(slot, step):
            copy.start()

        for line in range(LINES):
            lanes = pl.ds(line * side, side)
            grad = grad_sum[:, lanes]
            scaled = scaled_keep[:, lanes]
            gain_grad_ref[...] += grad * scaled
            shift_grad_ref[...] += grad
            weighted = grad * gain_ref[...]
            first = jnp.sum(weighted, axis=0, keepdims=True) * (1.0 / channels)
            second = jnp.sum(weighted * scaled, axis=0, keepdims=True) * (1.0 / channels)
            mixed_grad = (inverse_keep[:, lanes] * (weighted - first - scaled * second)).astype(jnp.bfloat16)
            branch = branch_sum[:, lanes].astype(jnp.bfloat16)
            for owner in range(n):
                grad_stage[owner, step, line] = mixed_grad[owner * local : (owner + 1) * local]
                branch_stage[owner, step, line] = branch[owner * local : (owner + 1) * local]

        for shift in range(1, n):
            send_part(grad_stage, grad_ref, me, lax.rem(me + shift, n), step, send_g, recv_g, shift).start()
        for shift in range(1, n):
            send_part(branch_stage, branch_ref, me, lax.rem(me + shift, n), step, send_r, recv_r, shift).start()

    own_g = pltpu.make_async_copy(grad_stage.at[me], grad_ref.at[me], own_sem.at[0])
    own_r = pltpu.make_async_copy(branch_stage.at[me], branch_ref.at[me], own_sem.at[1])
    own_g.start()
    own_r.start()
    own_g.wait()
    own_r.wait()
    for step in range(max(steps - 2, 0), steps):
        for copy in keeps(step % 2, step):
            copy.wait()
    wait_parts(grad_stage, grad_ref, me, n, send_g, recv_g)
    wait_parts(branch_stage, branch_ref, me, n, send_r, recv_r)


def mlp(n, mixed, back, in_turned, in_full, out_full, out_turned, gain, shift, bias):
    _, groups, block, group, side = mixed.shape
    hidden, channels = out_full.shape
    local = channels // n
    pixels = block * side
    width = LINES * side
    shape = (n, block // LINES, LINES, local, side)
    vmem = pl.BlockSpec(memory_space=pltpu.VMEM)
    hbm = pl.BlockSpec(memory_space=pl.ANY)
    return pl.pallas_call(
        functools.partial(mlp_kernel, n),
        out_shape=(
            jax.ShapeDtypeStruct(shape, jnp.bfloat16),
            jax.ShapeDtypeStruct(shape, jnp.bfloat16),
            jax.ShapeDtypeStruct((hidden, pixels), jnp.bfloat16),
            jax.ShapeDtypeStruct((hidden, pixels), jnp.bfloat16),
            jax.ShapeDtypeStruct((channels, pixels), jnp.bfloat16),
            jax.ShapeDtypeStruct((channels, pixels), jnp.bfloat16),
            jax.ShapeDtypeStruct((channels, side), jnp.float32),
            jax.ShapeDtypeStruct((channels, side), jnp.float32),
        ),
        in_specs=[vmem] * 9,
        out_specs=(hbm,) * 6 + (vmem, vmem),
        scratch_shapes=[
            pltpu.VMEM(shape, jnp.bfloat16),
            pltpu.VMEM(shape, jnp.bfloat16),
            pltpu.VMEM((2, hidden, width), jnp.bfloat16),
            pltpu.VMEM((2, hidden, width), jnp.bfloat16),
            pltpu.VMEM((2, channels, width), jnp.bfloat16),
            pltpu.VMEM((2, channels, width), jnp.bfloat16),
            pltpu.VMEM((channels, width), jnp.float32),
            pltpu.VMEM((1, width), jnp.float32),
            pltpu.VMEM((channels, width), jnp.float32),
            pltpu.VMEM((channels, width), jnp.float32),
            pltpu.SemaphoreType.DMA((n,)),
            pltpu.SemaphoreType.DMA((n,)),
            pltpu.SemaphoreType.DMA((n,)),
            pltpu.SemaphoreType.DMA((n,)),
            pltpu.SemaphoreType.DMA((2,)),
            pltpu.SemaphoreType.DMA((2, 4)),
        ],
        compiler_params=pltpu.CompilerParams(
            collective_id=1, has_side_effects=True, vmem_limit_bytes=63 * mebi
        ),
        name="mlp",
    )(mixed, back, in_turned, in_full, out_full, out_turned, gain, shift, bias)


def back_kernel(
    sizes_ref,
    image_ref,
    cot_ref,
    grad_ref,
    branch_ref,
    rows_ref,
    cols_ref,
    skip_ref,
    scale_ref,
    bias_ref,
    output_ref,
    input_grad_ref,
    rows_sums_ref,
    cols_sums_ref,
    skip_sums_ref,
    scale_sums_ref,
    grad_wide,
    branch_wide,
):
    count, side, _ = image_ref.shape
    row_at = lax.broadcasted_iota(jnp.int32, (side, side), 0)
    col_at = lax.broadcasted_iota(jnp.int32, (side, side), 1)
    inside = (row_at < sizes_ref[0]) & (col_at < sizes_ref[1])
    lower = row_at >= col_at
    upper = row_at <= col_at
    flip = (row_at + col_at == side - 1).astype(jnp.bfloat16)

    @pl.loop(0, side)
    def _(row):
        span = pl.ds(pl.multiple_of(row * count, count), count)
        grad_wide[span, :] = grad_ref[row].astype(jnp.float32)
        branch_wide[span, :] = branch_ref[row].astype(jnp.float32)

    @pl.loop(0, count)
    def _(chan):
        one = pl.ds(chan, 1)
        grad = grad_wide[pl.ds(chan, side, stride=count), :]
        branch = branch_wide[pl.ds(chan, side, stride=count), :]
        image = image_ref[chan].astype(jnp.float32)
        grad_out = jnp.where(inside, cot_ref[chan].astype(jnp.float32), 0.0)
        shifted = branch + bias_ref[one, :]
        output_ref[chan] = jnp.where(inside, image + scale_ref[one, :] * shifted, 0.0).astype(jnp.bfloat16)
        scale_sums_ref[one, :] = jnp.sum(grad_out * shifted, axis=0, keepdims=True)
        masked = jnp.where(inside, image, 0.0)
        skip_sums_ref[one, :] = jnp.sum(grad * masked, axis=0, keepdims=True)
        masked_low = masked.astype(jnp.bfloat16)
        grad_low = grad.astype(jnp.bfloat16)
        grad_turned = dot_nt(flip, grad_low).astype(jnp.bfloat16)
        masked_turned = dot_nn(flip, masked_low).astype(jnp.bfloat16)
        rows_high, rows_low = split_low(lag_matrix(rows_ref[one, 0, :], side, lower))
        turned_high, turned_low = split_low(lag_matrix(rows_ref[one, 1, :], side, upper))
        cols_high, cols_low = split_low(lag_matrix(cols_ref[one, 0, :], side, lower))
        along = dot_nn(
            jnp.concatenate([rows_high, rows_low], axis=1),
            jnp.concatenate([masked_low, masked_low], axis=0),
        )
        along_grad = dot_nn(
            jnp.concatenate([grad_low, grad_low], axis=1),
            jnp.concatenate([cols_high, cols_low], axis=0),
        )
        along_high, along_low = split_low(along)
        grad_high, grad_rest = split_low(along_grad)
        cols_grad = dot_nn(
            jnp.concatenate([grad_turned, grad_turned], axis=1),
            jnp.concatenate([along_high, along_low], axis=0),
        )
        rows_grad = dot_nt(
            jnp.concatenate([grad_high, grad_rest], axis=1),
            jnp.concatenate([masked_turned, masked_turned], axis=1),
        )
        masked_grad = dot_nn(
            jnp.concatenate([turned_high, turned_low], axis=1),
            jnp.concatenate([grad_high, grad_high], axis=0),
        ) + dot_nn(turned_high, grad_rest)
        masked_grad = masked_grad + skip_ref[one, :] * grad
        input_grad_ref[chan] = jnp.where(inside, grad_out + masked_grad, 0.0)
        rows_sums_ref[one, :] = lag_sums(rows_grad, side, row_at + col_at >= side - 1)
        cols_sums_ref[one, :] = lag_sums(cols_grad, side, row_at + col_at <= side - 1)


def mixer_back(sizes, images, cotangent, grad, branch, rows_pair, cols_pair, skip_wide, scale_wide, bias_wide):
    count, side, _ = images.shape
    line = jax.ShapeDtypeStruct((count, side), jnp.float32)
    vmem = pl.BlockSpec(memory_space=pltpu.VMEM)
    return pl.pallas_call(
        back_kernel,
        out_shape=(
            jax.ShapeDtypeStruct(images.shape, jnp.bfloat16),
            jax.ShapeDtypeStruct(images.shape, jnp.float32),
            line,
            line,
            line,
            line,
        ),
        in_specs=[pl.BlockSpec(memory_space=pltpu.SMEM)] + [vmem] * 9,
        out_specs=(vmem,) * 6,
        scratch_shapes=[
            pltpu.VMEM((count * side, side), jnp.float32),
            pltpu.VMEM((count * side, side), jnp.float32),
        ],
        compiler_params=pltpu.CompilerParams(vmem_limit_bytes=60 * mebi),
        name="mixer_back",
    )(sizes, images, cotangent, grad, branch, rows_pair, cols_pair, skip_wide, scale_wide, bias_wide)


def lag_pair(taps):
    return jnp.stack([jnp.roll(taps[:, ::-1], 1, axis=1), taps], axis=1)


def pixel_body(
    n,
    images,
    cotangent,
    image_sizes,
    slot_image,
    rows_rate,
    rows_freq,
    rows_real,
    rows_imag,
    cols_rate,
    cols_freq,
    cols_real,
    cols_imag,
    skip_gain,
    norm_gain,
    norm_bias,
    weight_in,
    bias_in,
    weight_out,
    bias_out,
    layer_scale,
):
    _, count, side, _ = images.shape
    channels = norm_gain.shape[0]
    picked = slot_image[lax.axis_index("dp")]
    sizes = image_sizes[picked]
    image, cot = images[0], cotangent[0]

    def both_taps(*params):
        return kernel_taps(*params[:4], side), kernel_taps(*params[4:], side)

    (rows_taps, cols_taps), taps_pull = jax.vjp(
        both_taps,
        rows_rate,
        rows_freq,
        rows_real,
        rows_imag,
        cols_rate,
        cols_freq,
        cols_real,
        cols_imag,
    )
    rows_pair, cols_pair = lag_pair(rows_taps), lag_pair(cols_taps)
    skip_wide = jnp.broadcast_to(skip_gain[:, None], (count, side))
    scale_wide = jnp.broadcast_to(layer_scale[:, None], (count, side))
    bias_wide = jnp.broadcast_to(bias_out[:, None], (count, side))

    in_turned = lax.all_gather(weight_in.T, "chan", axis=0, tiled=True)
    out_full = lax.all_gather(weight_out, "chan", axis=0, tiled=True)
    bias_full = lax.all_gather(bias_in, "chan", axis=0, tiled=True).astype(jnp.float32)

    mixed, back, bias_out_sums = mixer_forward(
        n, sizes, image, cot, rows_pair, cols_pair, skip_wide, scale_wide
    )
    grad, branch, active, before_grad, normed, cots, gain_sums, shift_sums = mlp(
        n,
        mixed,
        back,
        in_turned,
        in_turned.T,
        out_full,
        out_full.T,
        jnp.broadcast_to(norm_gain[:, None], (channels, side)),
        jnp.broadcast_to(norm_bias[:, None], (channels, side)),
        bias_full[:, None],
    )
    out_weight_grad = lax.psum_scatter(dot_nt(active, cots), "chan", scatter_dimension=0, tiled=True)
    in_weight_grad = lax.psum_scatter(dot_nt(before_grad, normed), "chan", scatter_dimension=0, tiled=True)
    in_bias_grad = lax.psum_scatter(
        jnp.sum(before_grad.astype(jnp.float32), axis=1), "chan", scatter_dimension=0, tiled=True
    )
    output, input_grad, rows_sums, cols_sums, skip_sums, scale_sums = mixer_back(
        sizes,
        image,
        cot,
        grad.reshape(side, count, side),
        branch.reshape(side, count, side),
        rows_pair,
        cols_pair,
        skip_wide,
        scale_wide,
        bias_wide,
    )
    params_grad = taps_pull(
        (jnp.roll(rows_sums, 1, axis=1), cols_sums[:, ::-1])
    )
    in_weight_grad, out_weight_grad = lax.psum((in_weight_grad, out_weight_grad), "dp")
    small = lax.psum(
        (
            *params_grad,
            jnp.sum(skip_sums, axis=1),
            in_bias_grad,
            jnp.sum(bias_out_sums, axis=1),
            jnp.sum(scale_sums, axis=1),
        ),
        "dp",
    )
    norm_sums = lax.psum((jnp.sum(gain_sums, axis=1), jnp.sum(shift_sums, axis=1)), ("dp", "chan"))
    return (
        output[None],
        input_grad[None],
        *small[:9],
        *norm_sums,
        in_weight_grad.T,
        small[9],
        out_weight_grad,
        small[10],
        small[11],
    )


def choose_body(n, images, *rest):
    slots, count, side, _ = images.shape
    fits = (
        slots == 1
        and side == 128
        and count % GROUP == 0
        and side % (n * LINES) == 0
        and (rest[15].shape[0] * n) % STEP_HIDDEN == 0
    )
    return pixel_body(n, images, *rest) if fits else plain_body(images, *rest)


def solution(mesh):
    in_specs = (
        P("dp", "chan", None, None),
        P("dp", "chan", None, None),
        P(),
        P(),
        P("chan", None),
        P("chan", None),
        P("chan", None),
        P("chan", None),
        P("chan", None),
        P("chan", None),
        P("chan", None),
        P("chan", None),
        P("chan"),
        P(),
        P(),
        P(None, "chan"),
        P("chan"),
        P("chan", None),
        P("chan"),
        P("chan"),
    )
    out_specs = (
        P("dp", "chan", None, None),
        P("dp", "chan", None, None),
        P("chan", None),
        P("chan", None),
        P("chan", None),
        P("chan", None),
        P("chan", None),
        P("chan", None),
        P("chan", None),
        P("chan", None),
        P("chan"),
        P(),
        P(),
        P(None, "chan"),
        P("chan"),
        P("chan", None),
        P("chan"),
        P("chan"),
    )
    return jax.shard_map(functools.partial(choose_body, mesh.shape["chan"]), mesh=mesh, in_specs=in_specs, out_specs=out_specs, check_vma=False)
```

```python
import functools

import jax
import jax.numpy as jnp
from jax import lax
from jax.experimental import pallas as pl
from jax.experimental.pallas import tpu as pltpu
from jax.sharding import PartitionSpec as P

eps_norm = 1e-06
highest = lax.Precision.HIGHEST


def kernel_taps(rate_vals, freq_vals, real_part, imag_part, length):
    offsets = jnp.arange(length, dtype=jnp.float32)
    decays = jnp.exp(-rate_vals[:, :, None] * offsets)
    angles = freq_vals[:, :, None] * offsets
    return jnp.sum(
        decays
        * (real_part[:, :, None] * jnp.cos(angles) - imag_part[:, :, None] * jnp.sin(angles)),
        axis=1,
    )


def toeplitz(filter_taps):
    length = filter_taps.shape[1]
    offsets = jnp.arange(length, dtype=jnp.int32)
    lag_index = offsets[:, None] - offsets[None, :]
    return jnp.where(lag_index[None] >= 0, filter_taps[:, jnp.maximum(lag_index, 0)], 0.0)


def mixer(
    masked_in,
    rows_rate,
    rows_freq,
    rows_real,
    rows_imag,
    cols_rate,
    cols_freq,
    cols_real,
    cols_imag,
    skip_gain,
):
    rows_op = toeplitz(kernel_taps(rows_rate, rows_freq, rows_real, rows_imag, masked_in.shape[2]))
    cols_op = toeplitz(kernel_taps(cols_rate, cols_freq, cols_real, cols_imag, masked_in.shape[3]))
    along_rows = jnp.einsum("chi,ncij->nchj", rows_op, masked_in, precision=highest)
    return (
        jnp.einsum("nchj,cwj->nchw", along_rows, cols_op, precision=highest)
        + skip_gain[None, :, None, None] * masked_in
    )


def normalize(values, norm_gain, norm_bias):
    center = values - jnp.mean(values, axis=-2, keepdims=True)
    inverse = lax.rsqrt(jnp.mean(center * center, axis=-2, keepdims=True) + eps_norm)
    scaled = center * inverse
    return (scaled * norm_gain[:, None] + norm_bias[:, None], scaled, inverse)


def gelu_exact(values):
    return jax.nn.gelu(values, approximate=False)


def plain_body(
    images,
    cotangent,
    image_sizes,
    slot_image,
    rows_rate,
    rows_freq,
    rows_real,
    rows_imag,
    cols_rate,
    cols_freq,
    cols_real,
    cols_imag,
    skip_gain,
    norm_gain,
    norm_bias,
    weight_in,
    bias_in,
    weight_out,
    bias_out,
    layer_scale,
):
    slot_count, chan_count, length = (images.shape[0], images.shape[1], images.shape[2])
    pixels = length * length
    image_count = slot_image.shape[0]
    slot_ids = lax.axis_index("dp") * slot_count + jnp.arange(slot_count, dtype=jnp.int32)
    choose = (slot_ids[:, None] == jnp.arange(image_count, dtype=jnp.int32)[None, :]).astype(
        jnp.int32
    )
    picked = jnp.sum(choose * slot_image[None, :], axis=1)
    owners = (picked[:, None] == jnp.arange(image_count, dtype=jnp.int32)[None, :]).astype(
        jnp.int32
    )
    heights = jnp.sum(owners * image_sizes[None, :, 0], axis=1)
    widths = jnp.sum(owners * image_sizes[None, :, 1], axis=1)
    offsets = jnp.arange(length, dtype=jnp.int32)
    inside = (
        (offsets[None, :, None] < heights[:, None, None])
        & (offsets[None, None, :] < widths[:, None, None])
    ).astype(jnp.float32)
    masked_in = images.astype(jnp.float32) * inside[:, None]
    mixed_out, mixer_pull = jax.vjp(
        mixer,
        masked_in,
        rows_rate,
        rows_freq,
        rows_real,
        rows_imag,
        cols_rate,
        cols_freq,
        cols_real,
        cols_imag,
        skip_gain,
    )
    mixed_low = mixed_out.astype(jnp.bfloat16).reshape(slot_count, chan_count, pixels)
    mask_flat = inside.reshape(slot_count, 1, pixels)
    residual = images.astype(jnp.float32).reshape(slot_count, chan_count, pixels)
    grad_out = cotangent.astype(jnp.float32).reshape(slot_count, chan_count, pixels) * mask_flat
    chan_offset = lax.axis_index("chan") * chan_count
    all_channels = norm_gain.shape[0]
    slot_item = 0
    gathered = lax.all_gather(mixed_low[slot_item], "chan", axis=0, tiled=True)
    normed, scaled, inverse = normalize(gathered.astype(jnp.float32), norm_gain, norm_bias)
    normed_low = normed.astype(jnp.bfloat16)
    before = (
        jnp.einsum("cf,cp->fp", weight_in, normed_low, preferred_element_type=jnp.float32)
        + bias_in.astype(jnp.float32)[:, None]
    )
    active = gelu_exact(before).astype(jnp.bfloat16)

    def project(first_row, row_count, active=active):
        return jnp.einsum("fc,fp->cp", weight_out, active, preferred_element_type=jnp.float32)

    branch_list = [
        lax.psum_scatter(
            project(jnp.int32(0), chan_count * lax.axis_size("chan")),
            "chan",
            scatter_dimension=0,
            tiled=True,
        )
    ]
    scaled_part = lax.dynamic_slice_in_dim(scaled, chan_offset, chan_count, 0)
    stored = [(normed_low, before, active, scaled_part, inverse)]
    branch_all = jnp.stack(branch_list)
    shifted = branch_all + bias_out[None, :, None]
    output = (
        (mask_flat * (residual + layer_scale[None, :, None] * shifted))
        .astype(jnp.bfloat16)
        .reshape(images.shape)
    )
    scale_grad = jnp.sum(grad_out * shifted, axis=(0, 2))
    branch_grad = layer_scale[None, :, None] * grad_out
    bias_out_grad = jnp.sum(branch_grad, axis=(0, 2))
    branch_low = branch_grad.astype(jnp.bfloat16)
    hidden_count = weight_in.shape[1]
    out_weight_grad = jnp.zeros((hidden_count, all_channels), jnp.float32)
    gain_shard = lax.dynamic_slice_in_dim(norm_gain, chan_offset, chan_count, 0)
    slot_item = 0
    normed_low, before, active, scaled_part, inverse = stored[slot_item]

    def absorb(totals, shard_rows, first_row, active=active):
        hidden_grad = jnp.einsum(
            "fc,cp->fp", weight_out, shard_rows, preferred_element_type=jnp.float32
        )
        product_part = jnp.einsum(
            "fp,cp->fc", active, shard_rows, preferred_element_type=jnp.float32
        )
        return (hidden_grad, product_part)

    hidden_start = jnp.zeros((hidden_count, pixels), jnp.float32)
    hidden_grad, out_weight_grad = absorb(
        (hidden_start, out_weight_grad),
        lax.all_gather(branch_low[slot_item], "chan", axis=0, tiled=True),
        jnp.int32(0),
    )
    gelu_pull = jax.vjp(gelu_exact, before)[1]
    before_grad = gelu_pull(hidden_grad)[0].astype(jnp.bfloat16)
    in_weight_grad = jnp.einsum(
        "cp,fp->cf", normed_low, before_grad, preferred_element_type=jnp.float32
    )
    in_bias_grad = jnp.sum(before_grad.astype(jnp.float32), axis=1)

    def spread_back(first_row, row_count, before_grad=before_grad):
        return jnp.einsum("cf,fp->cp", weight_in, before_grad, preferred_element_type=jnp.float32)

    normed_grad = lax.psum_scatter(
        spread_back(jnp.int32(0), chan_count * lax.axis_size("chan")),
        "chan",
        scatter_dimension=0,
        tiled=True,
    )
    weighted = normed_grad * gain_shard[:, None]
    pixel_sums = (
        lax.psum(jnp.sum(weighted, axis=0).astype(jnp.bfloat16), "chan").astype(jnp.float32),
        lax.psum(jnp.sum(weighted * scaled_part, axis=0).astype(jnp.bfloat16), "chan").astype(
            jnp.float32
        ),
    )
    mixed_grads = [
        inverse
        * (
            weighted
            - pixel_sums[0][None, :] / all_channels
            - scaled_part * pixel_sums[1][None, :] / all_channels
        )
    ]
    gain_part = jnp.sum(normed_grad * scaled_part, axis=1)
    shift_part = jnp.sum(normed_grad, axis=1)
    mixed_grad_all = jnp.stack(mixed_grads)
    gain_grad = lax.dynamic_update_slice_in_dim(
        jnp.zeros((all_channels,), jnp.float32), gain_part, chan_offset, 0
    )
    shift_grad = lax.dynamic_update_slice_in_dim(
        jnp.zeros((all_channels,), jnp.float32), shift_part, chan_offset, 0
    )
    pulled = mixer_pull(mixed_grad_all.reshape(images.shape))
    input_grad = inside[:, None] * (cotangent.astype(jnp.float32) + pulled[0])
    summed = lax.psum(
        (
            in_weight_grad,
            out_weight_grad,
            in_bias_grad,
            bias_out_grad,
            scale_grad,
            pulled[1],
            pulled[2],
            pulled[3],
            pulled[4],
            pulled[5],
            pulled[6],
            pulled[7],
            pulled[8],
            pulled[9],
        ),
        "dp",
    )
    norm_sums = lax.psum((gain_grad, shift_grad), ("dp", "chan"))
    return (
        output,
        input_grad,
        summed[5],
        summed[6],
        summed[7],
        summed[8],
        summed[9],
        summed[10],
        summed[11],
        summed[12],
        summed[13],
        norm_sums[0],
        norm_sums[1],
        summed[0],
        summed[2],
        summed[1],
        summed[3],
        summed[4],
    )


MESH = pl.DeviceIdType.MESH
GROUP = 16
LINES = 4
STEP_HIDDEN = 512
mebi = 1024 * 1024


def dot_nn(left, right):
    return lax.dot_general(left, right, (((1,), (0,)), ((), ())), preferred_element_type=jnp.float32)


def dot_nt(left, right):
    return lax.dot_general(left, right, (((1,), (1,)), ((), ())), preferred_element_type=jnp.float32)


def dot_tn(left, right):
    return lax.dot_general(left, right, (((0,), (0,)), ((), ())), preferred_element_type=jnp.float32)


def split_low(values):
    high = values.astype(jnp.bfloat16)
    return high, (values - high.astype(jnp.float32)).astype(jnp.bfloat16)


def lag_matrix(line, side, keep):
    spread = pltpu.roll(jnp.broadcast_to(line, (side, side)), 0, 1, stride=1, stride_axis=0)
    return jnp.where(keep, spread, 0.0)


def lag_sums(matrix, side, keep):
    turned = pltpu.roll(jnp.where(keep, matrix, 0.0), 0, 1, stride=1, stride_axis=0)
    return jnp.sum(turned, axis=0, keepdims=True)


cos_terms = (
    1.0, -19.7392087, 64.9393891, -85.4566583, 60.242131, -26.4046662, 7.8001253, -1.45310477
)
sin_terms = (6.2831853, -41.3417004, 81.6051314, -76.703015, 42.0259236, -14.8998335, 3.23811835)


def polynomial(terms, at):
    value = terms[-1]
    for term in terms[-2::-1]:
        value = value * at + term
    return value


def taps_tile(rate, freq, real, imag, lag):
    turns = freq * 0.15915494309189535
    total = jnp.zeros((rate.shape[0], lag.shape[1]), jnp.float32)
    for mode in range(rate.shape[1]):
        one = slice(mode, mode + 1)
        angle = turns[:, one] * lag
        angle = angle - jnp.floor(angle + 0.5)
        square = angle * angle
        wave = real[:, one] * polynomial(cos_terms, square)
        wave = wave - (imag[:, one] * angle) * polynomial(sin_terms, square)
        total = total + jnp.exp(-rate[:, one] * lag) * wave
    return total


def meet(n, shares):
    me, share = lax.axis_index("chan"), lax.axis_index("dp")
    barrier = pltpu.get_barrier_semaphore()
    for shift in range(1, n):
        pl.semaphore_signal(
            barrier, inc=1, device_id={"chan": lax.rem(me + shift, n)}, device_id_type=MESH
        )
    for shift in range(1, shares):
        pl.semaphore_signal(
            barrier, inc=1, device_id={"dp": lax.rem(share + shift, shares)}, device_id_type=MESH
        )
    pl.semaphore_wait(barrier, n + shares - 2)
    return me, share


def push(source, target, send_sem, recv_sem, **peer):
    return pltpu.make_async_remote_copy(
        src_ref=source,
        dst_ref=target,
        send_sem=send_sem,
        recv_sem=recv_sem,
        device_id=peer,
        device_id_type=MESH,
    )


def weight_rounds(n, shares, me, share, pairs, sems):
    near, far = n // 2, me // 2
    core = lax.rem(me, 2)
    own_sem, send1, recv1, send2, recv2, send3, recv3 = sems

    def own(at):
        local, whole = pairs[at]
        return pltpu.make_async_copy(local, whole.at[core, :, far], own_sem.at[at])

    def first(at, shift, back=False):
        local, whole = pairs[at]
        origin = lax.rem(far + near - shift, near) if back else far
        return push(
            local.at[share],
            whole.at[core, share, origin],
            send1.at[at, shift],
            recv1.at[at, shift],
            chan=lax.rem(far + shift, near) * 2 + core,
        )

    def second(at, shift, turn, back=False):
        whole = pairs[at][1]
        origin = lax.rem(far + near - shift, near)
        holder = lax.rem(share + shares - turn, shares) if back else share
        return push(
            whole.at[core, share, origin],
            whole.at[core, holder, origin],
            send2.at[at, shift, turn],
            recv2.at[at, shift, turn],
            dp=lax.rem(share + turn, shares),
        )

    def third(at, back=False):
        whole = pairs[at][1]
        return push(
            whole.at[core], whole.at[1 - core if back else core], send3.at[at], recv3.at[at], chan=far * 2 + 1 - core
        )

    both = range(len(pairs))

    def start_first():
        for at in both:
            own(at).start()
            for shift in range(1, near):
                first(at, shift).start()

    def start_second():
        for at in both:
            for shift in range(1, near):
                first(at, shift, True).wait_recv()
                for turn in range(1, shares):
                    second(at, shift, turn).start()

    def start_third():
        for at in both:
            own(at).wait()
            for shift in range(1, near):
                for turn in range(1, shares):
                    second(at, shift, turn, True).wait_recv()
            third(at).start()

    def finish():
        for at in both:
            third(at, True).wait_recv()
            third(at).wait_send()
            for shift in range(1, near):
                first(at, shift).wait_send()
                for turn in range(1, shares):
                    second(at, shift, turn).wait_send()

    return start_first, start_second, start_third, finish


def send_part(stage, target, me, peer, part, send_sem, recv_sem, shift):
    return pltpu.make_async_remote_copy(
        src_ref=stage.at[peer, part],
        dst_ref=target.at[me, part],
        send_sem=send_sem.at[shift],
        recv_sem=recv_sem.at[shift],
        device_id={"chan": peer},
        device_id_type=MESH,
    )


def wait_parts(stage, target, me, n, send_sem, recv_sem):
    for shift in range(1, n):
        peer = lax.rem(me + shift, n)
        origin = lax.rem(me + n - shift, n)
        pltpu.make_async_remote_copy(
            src_ref=stage.at[peer],
            dst_ref=target.at[origin],
            send_sem=send_sem.at[shift],
            recv_sem=recv_sem.at[shift],
            device_id={"chan": peer},
            device_id_type=MESH,
        ).wait()


def mixer_kernel(
    n,
    shares,
    sizes_ref,
    image_ref,
    cot_ref,
    rate_ref,
    freq_ref,
    real_ref,
    imag_ref,
    cols_rate_ref,
    cols_freq_ref,
    cols_real_ref,
    cols_imag_ref,
    skip_ref,
    scale_ref,
    in_part_ref,
    out_part_ref,
    mixed_ref,
    back_ref,
    in_whole_ref,
    out_whole_ref,
    sums_ref,
    rows_back_ref,
    rows_ref,
    cols_back_ref,
    cols_ref,
    mixed_stage,
    back_stage,
    wide,
    send_m,
    recv_m,
    send_b,
    recv_b,
    own_sem,
    *weight_sems,
):
    count, side, _ = image_ref.shape
    parts = count // GROUP
    block = side // n
    me, share = meet(n, shares)
    start_first, start_second, start_third, finish = weight_rounds(
        n, shares, me, share, ((in_part_ref, in_whole_ref), (out_part_ref, out_whole_ref)), weight_sems
    )
    start_first()
    row_at = lax.broadcasted_iota(jnp.int32, (side, side), 0)
    col_at = lax.broadcasted_iota(jnp.int32, (side, side), 1)
    inside = (row_at < sizes_ref[0]) & (col_at < sizes_ref[1])
    lower = row_at >= col_at
    upper = row_at <= col_at

    def turn(stage, part):
        @pl.loop(0, n)
        def _(owner):
            for line in range(block):
                tile = wide[pl.ds(owner * block + line, GROUP, stride=side), :]
                stage[owner, part, line] = tile.astype(jnp.bfloat16)

    def send(stage, target, part, send_sem, recv_sem):
        for shift in range(1, n):
            send_part(stage, target, me, lax.rem(me + shift, n), part, send_sem, recv_sem, shift).start()

    @pl.loop(0, parts)
    def _(part):
        @pl.loop(0, GROUP)
        def _(item):
            chan = part * GROUP + item
            grad_out = jnp.where(inside, cot_ref[chan].astype(jnp.float32), 0.0)
            scaled = grad_out * scale_ref[pl.ds(chan, 1), :]
            sums_ref[pl.ds(chan, 1), :] = jnp.sum(scaled, axis=0, keepdims=True)
            wide[pl.ds(pl.multiple_of(item * side, side), side), :] = scaled

        turn(back_stage, part)
        send(back_stage, back_ref, part, send_b, recv_b)

    lag = lax.broadcasted_iota(jnp.int32, (1, side), 1)
    lag_back = jnp.where(lag == 0, 0, side - lag).astype(jnp.float32)
    lag = lag.astype(jnp.float32)

    @pl.loop(0, count // 8)
    def _(tile):
        few = pl.ds(pl.multiple_of(tile * 8, 8), 8)
        rows = (rate_ref[few, :], freq_ref[few, :], real_ref[few, :], imag_ref[few, :])
        cols = (cols_rate_ref[few, :], cols_freq_ref[few, :], cols_real_ref[few, :], cols_imag_ref[few, :])
        rows_back_ref[few, :] = taps_tile(*rows, lag_back)
        rows_ref[few, :] = taps_tile(*rows, lag)
        cols_back_ref[few, :] = taps_tile(*cols, lag_back)
        cols_ref[few, :] = taps_tile(*cols, lag)

    start_second()

    @pl.loop(0, parts)
    def _(part):
        @pl.loop(0, GROUP)
        def _(item):
            chan = part * GROUP + item
            masked = jnp.where(inside, image_ref[chan].astype(jnp.float32), 0.0)
            masked_low = masked.astype(jnp.bfloat16)
            rows_high, rows_low = split_low(lag_matrix(rows_back_ref[pl.ds(chan, 1), :], side, lower))
            cols_high, cols_low = split_low(lag_matrix(cols_ref[pl.ds(chan, 1), :], side, upper))
            along = dot_nn(
                jnp.concatenate([rows_high, rows_low], axis=1),
                jnp.concatenate([masked_low, masked_low], axis=0),
            )
            along_high, along_low = split_low(along)
            mixed = dot_nn(
                jnp.concatenate([along_high, along_low], axis=1),
                jnp.concatenate([cols_high, cols_high], axis=0),
            ) + dot_nn(along_high, cols_low)
            mixed = mixed + skip_ref[pl.ds(chan, 1), :] * masked
            wide[pl.ds(pl.multiple_of(item * side, side), side), :] = mixed

        turn(mixed_stage, part)
        send(mixed_stage, mixed_ref, part, send_m, recv_m)

    start_third()
    own_b = pltpu.make_async_copy(back_stage.at[me], back_ref.at[me], own_sem.at[0])
    own_m = pltpu.make_async_copy(mixed_stage.at[me], mixed_ref.at[me], own_sem.at[1])
    own_b.start()
    own_m.start()
    own_b.wait()
    own_m.wait()
    wait_parts(back_stage, back_ref, me, n, send_b, recv_b)
    wait_parts(mixed_stage, mixed_ref, me, n, send_m, recv_m)
    finish()


def mixer_forward(n, shares, sizes, images, cotangent, params, skip_wide, scale_wide, in_part, out_part):
    near = n // 2
    count, side, _ = images.shape
    line = jax.ShapeDtypeStruct((count, side), jnp.float32)
    shape = (n, count // GROUP, side // n, GROUP, side)
    vmem = pl.BlockSpec(memory_space=pltpu.VMEM)
    hbm = pl.BlockSpec(memory_space=pl.ANY)
    return pl.pallas_call(
        functools.partial(mixer_kernel, n, shares),
        out_shape=(
            jax.ShapeDtypeStruct(shape, jnp.bfloat16),
            jax.ShapeDtypeStruct(shape, jnp.bfloat16),
        )
        + tuple(
            jax.ShapeDtypeStruct((2, shares, near, *part.shape[1:]), jnp.bfloat16)
            for part in (in_part, out_part)
        )
        + (line,) * 5,
        in_specs=[pl.BlockSpec(memory_space=pltpu.SMEM)] + [vmem] * 12 + [hbm] * 2,
        out_specs=(hbm,) * 4 + (vmem,) * 5,
        scratch_shapes=[
            pltpu.VMEM(shape, jnp.bfloat16),
            pltpu.VMEM(shape, jnp.bfloat16),
            pltpu.VMEM((GROUP * side, side), jnp.float32),
            pltpu.SemaphoreType.DMA((n,)),
            pltpu.SemaphoreType.DMA((n,)),
            pltpu.SemaphoreType.DMA((n,)),
            pltpu.SemaphoreType.DMA((n,)),
            pltpu.SemaphoreType.DMA((2,)),
            pltpu.SemaphoreType.DMA((2,)),
            pltpu.SemaphoreType.DMA((2, near)),
            pltpu.SemaphoreType.DMA((2, near)),
            pltpu.SemaphoreType.DMA((2, near, shares)),
            pltpu.SemaphoreType.DMA((2, near, shares)),
            pltpu.SemaphoreType.DMA((2,)),
            pltpu.SemaphoreType.DMA((2,)),
        ],
        compiler_params=pltpu.CompilerParams(
            collective_id=0, has_side_effects=True, vmem_limit_bytes=40 * mebi
        ),
        name="mixer_forward",
    )(sizes, images, cotangent, *params, skip_wide, scale_wide, in_part, out_part)


def gelu_parts(value):
    bell = jnp.exp(-0.5 * value * value)
    inner = 1.0 / (1.0 + (0.3275911 * 0.7071067811865476) * jnp.abs(value))
    series = 1.061405429 * inner - 1.453152027
    series = series * inner + 1.421413741
    series = series * inner - 0.284496736
    series = series * inner + 0.254829592
    tail = (0.5 * inner) * series * bell
    return jnp.where(value < 0.0, tail, 1.0 - tail), bell * 0.3989422804014327


def mlp_kernel(
    n,
    shares,
    mixed_ref,
    back_ref,
    in_ref,
    out_ref,
    gain_ref,
    shift_ref,
    grad_ref,
    branch_ref,
    active_ref,
    before_grad_ref,
    out_own_ref,
    out_got_ref,
    in_own_ref,
    in_got_ref,
    gain_grad_ref,
    shift_grad_ref,
    grad_stage,
    branch_stage,
    active_ring,
    before_ring,
    normed_keep,
    cots_keep,
    scaled_keep,
    inverse_keep,
    branch_sum,
    grad_sum,
    hidden_sum,
    pieces,
    rows_stage,
    send_g,
    recv_g,
    own_sem,
    ring_sem,
    piece_sem,
    half_sem,
    send_h,
    recv_h,
):
    side = mixed_ref.shape[-1]
    groups = mixed_ref.shape[1]
    block = mixed_ref.shape[2]
    hidden, channels = out_ref.shape
    local = channels // n
    steps = block // LINES
    width = LINES * side
    parts = hidden // STEP_HIDDEN
    ring = active_ring.shape[0]
    me, _ = meet(n, shares)
    core = lax.rem(me, 2)
    sibling = me + 1 - 2 * core
    gain_grad_ref[...] = jnp.zeros_like(gain_grad_ref)
    shift_grad_ref[...] = jnp.zeros_like(shift_grad_ref)
    hidden_sum[...] = jnp.zeros_like(hidden_sum)

    def keeps(turn):
        slot = lax.rem(turn, ring)
        span = pl.ds(pl.multiple_of(lax.rem(turn, parts) * STEP_HIDDEN, STEP_HIDDEN), STEP_HIDDEN)
        return [
            pltpu.make_async_copy(kept.at[slot], whole.at[turn // parts, span], ring_sem.at[at, slot])
            for at, (kept, whole) in enumerate(((active_ring, active_ref), (before_ring, before_grad_ref)))
        ]

    @pl.loop(0, steps)
    def _(step):
        for line in range(LINES):
            row = step * LINES + line
            lanes = pl.ds(line * side, side)
            order = [(owner, group) for owner in range(n) for group in range(groups)]
            mixed = jnp.concatenate(
                [mixed_ref[owner, group, row].astype(jnp.float32) for owner, group in order], axis=0
            )
            mean = jnp.sum(mixed, axis=0, keepdims=True) * (1.0 / channels)
            center = mixed - mean
            var = jnp.sum(center * center, axis=0, keepdims=True) * (1.0 / channels)
            inverse = lax.rsqrt(var + eps_norm)
            scaled = center * inverse
            normed_keep[step, :, lanes] = (scaled * gain_ref[...] + shift_ref[...]).astype(jnp.bfloat16)
            scaled_keep[:, lanes] = scaled
            inverse_keep[:, lanes] = inverse
            cots_keep[step, :, lanes] = jnp.concatenate(
                [back_ref[owner, group, row] for owner, group in order], axis=0
            )

        @pl.loop(0, parts)
        def _(part):
            turn = step * parts + part
            slot = lax.rem(turn, ring)

            @pl.when(turn >= ring)
            def _():
                for copy in keeps(turn - ring):
                    copy.wait()

            span = pl.ds(pl.multiple_of(part * STEP_HIDDEN, STEP_HIDDEN), STEP_HIDDEN)
            bias = in_ref[span, channels:].astype(jnp.float32)[:, :1]
            before = dot_nn(in_ref[span, :channels], normed_keep[step]) + bias
            inside, bell = gelu_parts(before)
            active = (before * inside).astype(jnp.bfloat16)
            active_grad = dot_nn(out_ref[span, :], cots_keep[step])
            before_grad = (active_grad * (inside + before * bell)).astype(jnp.bfloat16)
            active_ring[slot] = active
            before_ring[slot] = before_grad
            hidden_sum[span, :] += sum(
                before_grad[:, line * side : (line + 1) * side].astype(jnp.float32) for line in range(LINES)
            )
            branch = dot_tn(out_ref[span, :], active)
            grad = dot_tn(in_ref[span, :channels], before_grad)

            @pl.when(part == 0)
            def _():
                branch_sum[...] = branch
                grad_sum[...] = grad

            @pl.when(part > 0)
            def _():
                branch_sum[...] += branch
                grad_sum[...] += grad

            for copy in keeps(turn):
                copy.start()

        for line in range(LINES):
            lanes = pl.ds(line * side, side)
            grad = grad_sum[:, lanes]
            scaled = scaled_keep[:, lanes]
            gain_grad_ref[...] += grad * scaled
            shift_grad_ref[...] += grad
            weighted = grad * gain_ref[...]
            first = jnp.sum(weighted, axis=0, keepdims=True) * (1.0 / channels)
            second = jnp.sum(weighted * scaled, axis=0, keepdims=True) * (1.0 / channels)
            mixed_grad = (inverse_keep[:, lanes] * (weighted - first - scaled * second)).astype(jnp.bfloat16)
            branch = branch_sum[:, lanes].astype(jnp.bfloat16)
            for owner in range(n):
                grad_stage[owner, step, line] = mixed_grad[owner * local : (owner + 1) * local]
                branch_stage[owner, step, line] = branch[owner * local : (owner + 1) * local]

        for shift in range(1, n):
            send_part(grad_stage, grad_ref, me, lax.rem(me + shift, n), step, send_g, recv_g, shift).start()

    own_g = pltpu.make_async_copy(grad_stage.at[me], grad_ref.at[me], own_sem.at[0])
    own_r = pltpu.make_async_copy(branch_stage, branch_ref, own_sem.at[1])
    own_g.start()
    own_r.start()
    turns = steps * parts
    for turn in range(turns - ring, turns):
        for copy in keeps(turn):
            copy.wait()

    half = parts // 2

    kinds = (
        (active_ref, cots_keep, out_own_ref, out_got_ref, channels),
        (before_grad_ref, normed_keep, in_own_ref, in_got_ref, channels + side),
    )

    def fetch(whole, job, slot):
        place = lax.rem((1 - core) * half + job, parts)
        span = pl.ds(pl.multiple_of(place * STEP_HIDDEN, STEP_HIDDEN), STEP_HIDDEN)
        return pltpu.make_async_copy(whole.at[:, span], pieces.at[slot], piece_sem.at[slot])

    def give(kind, job):
        _, _, _, got, wide = kinds[kind]
        return push(
            rows_stage.at[job, :, pl.ds(0, wide)],
            got.at[pl.ds(job * STEP_HIDDEN, STEP_HIDDEN)],
            send_h.at[kind, job],
            recv_h.at[kind, job],
            chan=sibling,
        )

    def keep(kind, job):
        _, _, own, _, wide = kinds[kind]
        return pltpu.make_async_copy(
            rows_stage.at[job, :, pl.ds(0, wide)],
            own.at[pl.ds((job - half) * STEP_HIDDEN, STEP_HIDDEN)],
            half_sem.at[kind, job],
        )

    jobs = [(kind, job) for kind in range(2) for job in range(parts)]
    fetch(kinds[0][0], 0, 0).start()
    for at, (kind, job) in enumerate(jobs):
        whole, right = kinds[kind][:2]
        slot = at % 2
        if at + 1 < len(jobs):
            fetch(kinds[jobs[at + 1][0]][0], jobs[at + 1][1], (at + 1) % 2).start()
        fetch(whole, job, slot).wait()
        if kind == 1:
            (give if job < half else keep)(0, job).wait()
        total = dot_nt(pieces[slot, 0], right[0])
        for step in range(1, steps):
            total = total + dot_nt(pieces[slot, step], right[step])
        rows_stage[job, :, :channels] = total.astype(jnp.bfloat16)
        if kind == 1:
            place = lax.rem((1 - core) * half + job, parts)
            span = pl.ds(pl.multiple_of(place * STEP_HIDDEN, STEP_HIDDEN), STEP_HIDDEN)
            rows_stage[job, :, channels:] = hidden_sum[span, :].astype(jnp.bfloat16)
        (give if job < half else keep)(kind, job).start()
    for job in range(parts):
        (give if job < half else keep)(1, job).wait()
    own_g.wait()
    own_r.wait()
    wait_parts(grad_stage, grad_ref, me, n, send_g, recv_g)


def mlp(n, shares, mixed, back, in_full, out_full, gain, shift):
    _, groups, block, group, side = mixed.shape
    hidden, channels = out_full.shape
    local = channels // n
    steps = block // LINES
    width = LINES * side
    parts = hidden // STEP_HIDDEN
    shape = (n, steps, LINES, local, side)
    ring = 4
    low = functools.partial(jax.ShapeDtypeStruct, dtype=jnp.bfloat16)
    vmem = pl.BlockSpec(memory_space=pltpu.VMEM)
    hbm = pl.BlockSpec(memory_space=pl.ANY)
    return pl.pallas_call(
        functools.partial(mlp_kernel, n, shares),
        out_shape=(
            low(shape),
            low(shape),
            low((steps, hidden, width)),
            low((steps, hidden, width)),
            low((hidden // 2, channels)),
            low((hidden // 2, channels)),
            low((hidden // 2, channels + side)),
            low((hidden // 2, channels + side)),
            jax.ShapeDtypeStruct((channels, side), jnp.float32),
            jax.ShapeDtypeStruct((channels, side), jnp.float32),
        ),
        in_specs=[vmem] * 6,
        out_specs=(hbm,) * 8 + (vmem, vmem),
        scratch_shapes=[
            pltpu.VMEM(shape, jnp.bfloat16),
            pltpu.VMEM(shape, jnp.bfloat16),
            pltpu.VMEM((ring, STEP_HIDDEN, width), jnp.bfloat16),
            pltpu.VMEM((ring, STEP_HIDDEN, width), jnp.bfloat16),
            pltpu.VMEM((steps, channels, width), jnp.bfloat16),
            pltpu.VMEM((steps, channels, width), jnp.bfloat16),
            pltpu.VMEM((channels, width), jnp.float32),
            pltpu.VMEM((1, width), jnp.float32),
            pltpu.VMEM((channels, width), jnp.float32),
            pltpu.VMEM((channels, width), jnp.float32),
            pltpu.VMEM((hidden, side), jnp.float32),
            pltpu.VMEM((2, steps, STEP_HIDDEN, width), jnp.bfloat16),
            pltpu.VMEM((parts, STEP_HIDDEN, channels + side), jnp.bfloat16),
            pltpu.SemaphoreType.DMA((n,)),
            pltpu.SemaphoreType.DMA((n,)),
            pltpu.SemaphoreType.DMA((2,)),
            pltpu.SemaphoreType.DMA((2, ring)),
            pltpu.SemaphoreType.DMA((2,)),
            pltpu.SemaphoreType.DMA((2, parts)),
            pltpu.SemaphoreType.DMA((2, parts)),
            pltpu.SemaphoreType.DMA((2, parts)),
        ],
        compiler_params=pltpu.CompilerParams(
            collective_id=1, has_side_effects=True, vmem_limit_bytes=63 * mebi
        ),
        name="mlp",
    )(mixed, back, in_full, out_full, gain, shift)


def sum_rounds(n, shares, me, share, own, got, final, stage2, take2, stage3, take3, keep3, sems):
    near, far = n // 2, me // 2
    core = lax.rem(me, 2)
    send2, recv2, send3, recv3, send4, recv4, own_sem = sems
    rows = keep3.shape[0]
    block = near * rows

    def second(turn):
        peer = lax.rem(share + turn, shares)
        return push(stage2.at[peer], take2.at[turn], send2.at[turn], recv2.at[turn], dp=peer)

    def third(turn):
        peer = lax.rem(far + turn, near)
        return push(stage3.at[peer], take3.at[turn], send3.at[turn], recv3.at[turn], chan=peer * 2 + core)

    def fourth(turn, back=False):
        holder = lax.rem(share + shares - turn, shares) if back else share
        peer = lax.rem(share + turn, shares)
        return push(keep3, final.at[holder], send4.at[turn], recv4.at[turn], dp=peer)

    def mine():
        return pltpu.make_async_copy(keep3, final.at[share], own_sem.at[0])

    def start_second():
        for at in range(shares):
            span = slice(at * block, (at + 1) * block)
            stage2[at] = (own[span].astype(jnp.float32) + got[span].astype(jnp.float32)).astype(jnp.bfloat16)
        for turn in range(1, shares):
            second(turn).start()

    def start_third():
        for turn in range(1, shares):
            second(turn).wait()
        for at in range(near):
            base = pl.ds(pl.multiple_of(share * block + at * rows, rows), rows)
            span = slice(at * rows, (at + 1) * rows)
            total = own[base, :].astype(jnp.float32) + got[base, :].astype(jnp.float32)
            for turn in range(1, shares):
                total = total + take2[turn, span].astype(jnp.float32)
            stage3[at] = total.astype(jnp.bfloat16)

            @pl.when(far == at)
            def _():
                keep3[...] = total

        for turn in range(1, near):
            third(turn).start()

    def start_fourth():
        for turn in range(1, near):
            third(turn).wait()
        total = keep3[...]
        for turn in range(1, near):
            total = total + take3[turn].astype(jnp.float32)
        keep3[...] = total
        mine().start()
        for turn in range(1, shares):
            fourth(turn).start()

    def finish():
        mine().wait()
        for turn in range(1, shares):
            fourth(turn, True).wait_recv()
            fourth(turn).wait_send()

    return start_second, start_third, start_fourth, finish


def back_kernel(
    n,
    shares,
    sizes_ref,
    image_ref,
    cot_ref,
    grad_ref,
    branch_ref,
    rows_back_ref,
    rows_ref,
    cols_back_ref,
    skip_ref,
    scale_ref,
    bias_ref,
    out_own_ref,
    out_got_ref,
    in_own_ref,
    in_got_ref,
    output_ref,
    input_grad_ref,
    rows_sums_ref,
    cols_sums_ref,
    skip_sums_ref,
    scale_sums_ref,
    out_final_ref,
    in_final_ref,
    wide,
    branch_got,
    send_sem,
    recv_sem,
    own_sem,
    *rest,
):
    count, side, _ = image_ref.shape
    steps, lines = branch_ref.shape[1], branch_ref.shape[2]
    me, share = meet(n, shares)
    out_rounds = sum_rounds(
        n, shares, me, share, out_own_ref, out_got_ref, out_final_ref, *rest[:5], rest[10:17]
    )
    in_rounds = sum_rounds(
        n, shares, me, share, in_own_ref, in_got_ref, in_final_ref, *rest[5:10], rest[17:24]
    )
    out_rounds[0]()
    for shift in range(1, n):
        peer = lax.rem(me + shift, n)
        pltpu.make_async_remote_copy(
            src_ref=branch_ref.at[peer],
            dst_ref=branch_got.at[me],
            send_sem=send_sem.at[shift],
            recv_sem=recv_sem.at[shift],
            device_id={"chan": peer},
            device_id_type=MESH,
        ).start()
    own = pltpu.make_async_copy(branch_ref.at[me], branch_got.at[me], own_sem.at[0])
    own.start()
    in_rounds[0]()
    row_at = lax.broadcasted_iota(jnp.int32, (side, side), 0)
    col_at = lax.broadcasted_iota(jnp.int32, (side, side), 1)
    inside = (row_at < sizes_ref[0]) & (col_at < sizes_ref[1])
    lower = row_at >= col_at
    upper = row_at <= col_at
    flip = (row_at + col_at == side - 1).astype(jnp.bfloat16)

    @pl.loop(0, side)
    def _(row):
        span = pl.ds(pl.multiple_of(row * count, count), count)
        wide[span, :] = grad_ref[row].astype(jnp.float32)

    @pl.loop(0, count)
    def _(chan):
        pl.when(chan == count // 2)(out_rounds[1])
        pl.when(chan == count * 3 // 4)(out_rounds[2])
        pl.when(chan == count * 15 // 16)(in_rounds[1])
        one = pl.ds(chan, 1)
        grad = wide[pl.ds(chan, side, stride=count), :]
        image = image_ref[chan].astype(jnp.float32)
        grad_out = jnp.where(inside, cot_ref[chan].astype(jnp.float32), 0.0)
        masked = jnp.where(inside, image, 0.0)
        skip_sums_ref[one, :] = jnp.sum(grad * masked, axis=0, keepdims=True)
        masked_low = masked.astype(jnp.bfloat16)
        grad_low = grad.astype(jnp.bfloat16)
        grad_turned = dot_nt(flip, grad_low).astype(jnp.bfloat16)
        masked_turned = dot_nn(flip, masked_low).astype(jnp.bfloat16)
        rows_high, rows_low = split_low(lag_matrix(rows_back_ref[one, :], side, lower))
        turned_high, turned_low = split_low(lag_matrix(rows_ref[one, :], side, upper))
        cols_high, cols_low = split_low(lag_matrix(cols_back_ref[one, :], side, lower))
        along = dot_nn(
            jnp.concatenate([rows_high, rows_low], axis=1),
            jnp.concatenate([masked_low, masked_low], axis=0),
        )
        along_grad = dot_nn(
            jnp.concatenate([grad_low, grad_low], axis=1),
            jnp.concatenate([cols_high, cols_low], axis=0),
        )
        along_high, along_low = split_low(along)
        grad_high, grad_rest = split_low(along_grad)
        cols_grad = dot_nn(
            jnp.concatenate([grad_turned, grad_turned], axis=1),
            jnp.concatenate([along_high, along_low], axis=0),
        )
        rows_grad = dot_nt(
            jnp.concatenate([grad_high, grad_rest], axis=1),
            jnp.concatenate([masked_turned, masked_turned], axis=1),
        )
        masked_grad = dot_nn(
            jnp.concatenate([turned_high, turned_low], axis=1),
            jnp.concatenate([grad_high, grad_high], axis=0),
        ) + dot_nn(turned_high, grad_rest)
        masked_grad = masked_grad + skip_ref[one, :] * grad
        input_grad_ref[chan] = jnp.where(inside, grad_out + masked_grad, 0.0)
        rows_sums_ref[one, :] = lag_sums(rows_grad, side, row_at + col_at >= side - 1)
        cols_sums_ref[one, :] = lag_sums(cols_grad, side, row_at + col_at <= side - 1)

    own.wait()
    for shift in range(1, n):
        peer = lax.rem(me + shift, n)
        pltpu.make_async_remote_copy(
            src_ref=branch_ref.at[peer],
            dst_ref=branch_got.at[lax.rem(me + n - shift, n)],
            send_sem=send_sem.at[shift],
            recv_sem=recv_sem.at[shift],
            device_id={"chan": peer},
            device_id_type=MESH,
        ).wait()

    @pl.loop(0, n * steps)
    def _(step):
        for line in range(lines):
            span = pl.ds(pl.multiple_of((step * lines + line) * count, count), count)
            wide[span, :] = branch_got[step // steps, lax.rem(step, steps), line].astype(jnp.float32)

    @pl.loop(0, count)
    def _(chan):
        one = pl.ds(chan, 1)
        shifted = wide[pl.ds(chan, side, stride=count), :] + bias_ref[one, :]
        image = image_ref[chan].astype(jnp.float32)
        grad_out = jnp.where(inside, cot_ref[chan].astype(jnp.float32), 0.0)
        output_ref[chan] = jnp.where(inside, image + scale_ref[one, :] * shifted, 0.0).astype(jnp.bfloat16)
        scale_sums_ref[one, :] = jnp.sum(grad_out * shifted, axis=0, keepdims=True)

    in_rounds[2]()
    out_rounds[3]()
    in_rounds[3]()


def mixer_back(n, shares, sizes, images, cotangent, grad, branch, lines, halves):
    count, side, _ = images.shape
    near = n // 2
    rows = halves[0].shape[0] // (shares * near)
    wides = (halves[0].shape[1], halves[2].shape[1])
    hbm = pl.BlockSpec(memory_space=pl.ANY)
    line = jax.ShapeDtypeStruct((count, side), jnp.float32)
    vmem = pl.BlockSpec(memory_space=pltpu.VMEM)
    return pl.pallas_call(
        functools.partial(back_kernel, n, shares),
        out_shape=(
            jax.ShapeDtypeStruct(images.shape, jnp.bfloat16),
            jax.ShapeDtypeStruct(images.shape, jnp.float32),
            line,
            line,
            line,
            line,
        )
        + tuple(jax.ShapeDtypeStruct((shares, rows, wide), jnp.float32) for wide in wides),
        in_specs=[pl.BlockSpec(memory_space=pltpu.SMEM)] + [vmem] * 3 + [hbm] + [vmem] * 10,
        out_specs=(vmem,) * 6 + (hbm,) * 2,
        scratch_shapes=[
            pltpu.VMEM((count * side, side), jnp.float32),
            pltpu.VMEM(branch.shape, jnp.bfloat16),
            pltpu.SemaphoreType.DMA((n,)),
            pltpu.SemaphoreType.DMA((n,)),
            pltpu.SemaphoreType.DMA((1,)),
        ]
        + [
            kind
            for wide in wides
            for kind in (
                pltpu.VMEM((shares, near * rows, wide), jnp.bfloat16),
                pltpu.VMEM((shares, near * rows, wide), jnp.bfloat16),
                pltpu.VMEM((near, rows, wide), jnp.bfloat16),
                pltpu.VMEM((near, rows, wide), jnp.bfloat16),
                pltpu.VMEM((rows, wide), jnp.float32),
            )
        ]
        + [
            pltpu.SemaphoreType.DMA((size,))
            for _ in wides
            for size in (shares, shares, near, near, shares, shares, 1)
        ],
        compiler_params=pltpu.CompilerParams(
            collective_id=2, has_side_effects=True, vmem_limit_bytes=62 * mebi
        ),
        name="mixer_back",
    )(sizes, images, cotangent, grad, branch, *lines, *halves)


def pixel_body(
    n,
    images,
    cotangent,
    image_sizes,
    slot_image,
    rows_rate,
    rows_freq,
    rows_real,
    rows_imag,
    cols_rate,
    cols_freq,
    cols_real,
    cols_imag,
    skip_gain,
    norm_gain,
    norm_bias,
    weight_in,
    bias_in,
    weight_out,
    bias_out,
    layer_scale,
):
    _, count, side, _ = images.shape
    channels = norm_gain.shape[0]
    picked = slot_image[lax.axis_index("dp")]
    sizes = image_sizes[picked]
    image, cot = images[0], cotangent[0]

    params = (
        rows_rate,
        rows_freq,
        rows_real,
        rows_imag,
        cols_rate,
        cols_freq,
        cols_real,
        cols_imag,
    )

    def both_taps(*params):
        return kernel_taps(*params[:4], side), kernel_taps(*params[4:], side)

    skip_wide = jnp.broadcast_to(skip_gain[:, None], (count, side))
    scale_wide = jnp.broadcast_to(layer_scale[:, None], (count, side))
    bias_wide = jnp.broadcast_to(bias_out[:, None], (count, side))

    shares = lax.axis_size("dp")
    hidden = weight_out.shape[0]
    spread = jnp.broadcast_to(bias_in[:, None], (hidden, side))
    in_part = jnp.concatenate([weight_in.T, spread], axis=1).reshape(shares, -1, channels + side)
    out_part = weight_out.reshape(shares, -1, channels)
    mixed, back, in_whole, out_whole, bias_out_sums, rows_back, rows, cols_back, _ = mixer_forward(
        n, shares, sizes, image, cot, params, skip_wide, scale_wide, in_part, out_part
    )
    grad, branch, _, _, *halves, gain_sums, shift_sums = mlp(
        n,
        shares,
        mixed,
        back,
        in_whole.reshape(-1, channels + side),
        out_whole.reshape(-1, channels),
        jnp.broadcast_to(norm_gain[:, None], (channels, side)),
        jnp.broadcast_to(norm_bias[:, None], (channels, side)),
    )
    output, input_grad, rows_sums, cols_sums, skip_sums, scale_sums, out_final, in_final = mixer_back(
        n,
        shares,
        sizes,
        image,
        cot,
        grad.reshape(side, count, side),
        branch,
        (rows_back, rows, cols_back, skip_wide, scale_wide, bias_wide),
        halves,
    )
    in_final = in_final.reshape(hidden, channels + side)
    params_grad = jax.vjp(both_taps, *params)[1](
        (jnp.roll(rows_sums, 1, axis=1), cols_sums[:, ::-1])
    )
    small = lax.psum(
        (
            *params_grad,
            jnp.sum(skip_sums, axis=1),
            jnp.sum(bias_out_sums, axis=1),
            jnp.sum(scale_sums, axis=1),
        ),
        "dp",
    )
    gain_grad, shift_grad = lax.psum(
        (jnp.sum(gain_sums, axis=1), jnp.sum(shift_sums, axis=1)), ("dp", "chan")
    )
    return (
        output[None],
        input_grad[None],
        *small[:9],
        gain_grad,
        shift_grad,
        in_final[:, :channels].T,
        jnp.sum(in_final[:, channels:], axis=1),
        out_final.reshape(hidden, channels),
        small[9],
        small[10],
    )


def choose_body(n, images, *rest):
    slots, count, side, _ = images.shape
    fits = (
        slots == 1
        and side == 128
        and count % GROUP == 0
        and side % (n * LINES) == 0
        and n % 2 == 0
        and (rest[15].shape[0] * n) % (2 * STEP_HIDDEN) == 0
        and rest[15].shape[0] % (16 * lax.axis_size("dp")) == 0
    )
    return pixel_body(n, images, *rest) if fits else plain_body(images, *rest)


def solution(mesh):
    in_specs = (
        P("dp", "chan", None, None),
        P("dp", "chan", None, None),
        P(),
        P(),
        P("chan", None),
        P("chan", None),
        P("chan", None),
        P("chan", None),
        P("chan", None),
        P("chan", None),
        P("chan", None),
        P("chan", None),
        P("chan"),
        P(),
        P(),
        P(None, "chan"),
        P("chan"),
        P("chan", None),
        P("chan"),
        P("chan"),
    )
    out_specs = (
        P("dp", "chan", None, None),
        P("dp", "chan", None, None),
        P("chan", None),
        P("chan", None),
        P("chan", None),
        P("chan", None),
        P("chan", None),
        P("chan", None),
        P("chan", None),
        P("chan", None),
        P("chan"),
        P(),
        P(),
        P(None, "chan"),
        P("chan"),
        P("chan", None),
        P("chan"),
        P("chan"),
    )
    return jax.shard_map(functools.partial(choose_body, mesh.shape["chan"]), mesh=mesh, in_specs=in_specs, out_specs=out_specs, check_vma=False)
```

```python
import functools

import jax
import jax.numpy as jnp
from jax import lax
from jax.experimental import pallas as pl
from jax.experimental.pallas import tpu as pltpu
from jax.sharding import PartitionSpec as P

eps_norm = 1e-06
highest = lax.Precision.HIGHEST


def kernel_taps(rate_vals, freq_vals, real_part, imag_part, length):
    offsets = jnp.arange(length, dtype=jnp.float32)
    decays = jnp.exp(-rate_vals[:, :, None] * offsets)
    angles = freq_vals[:, :, None] * offsets
    return jnp.sum(
        decays
        * (real_part[:, :, None] * jnp.cos(angles) - imag_part[:, :, None] * jnp.sin(angles)),
        axis=1,
    )


def toeplitz(filter_taps):
    length = filter_taps.shape[1]
    offsets = jnp.arange(length, dtype=jnp.int32)
    lag_index = offsets[:, None] - offsets[None, :]
    return jnp.where(lag_index[None] >= 0, filter_taps[:, jnp.maximum(lag_index, 0)], 0.0)


def mixer(
    masked_in,
    rows_rate,
    rows_freq,
    rows_real,
    rows_imag,
    cols_rate,
    cols_freq,
    cols_real,
    cols_imag,
    skip_gain,
):
    rows_op = toeplitz(kernel_taps(rows_rate, rows_freq, rows_real, rows_imag, masked_in.shape[2]))
    cols_op = toeplitz(kernel_taps(cols_rate, cols_freq, cols_real, cols_imag, masked_in.shape[3]))
    along_rows = jnp.einsum("chi,ncij->nchj", rows_op, masked_in, precision=highest)
    return (
        jnp.einsum("nchj,cwj->nchw", along_rows, cols_op, precision=highest)
        + skip_gain[None, :, None, None] * masked_in
    )


def normalize(values, norm_gain, norm_bias):
    center = values - jnp.mean(values, axis=-2, keepdims=True)
    inverse = lax.rsqrt(jnp.mean(center * center, axis=-2, keepdims=True) + eps_norm)
    scaled = center * inverse
    return (scaled * norm_gain[:, None] + norm_bias[:, None], scaled, inverse)


def gelu_exact(values):
    return jax.nn.gelu(values, approximate=False)


def plain_body(
    images,
    cotangent,
    image_sizes,
    slot_image,
    rows_rate,
    rows_freq,
    rows_real,
    rows_imag,
    cols_rate,
    cols_freq,
    cols_real,
    cols_imag,
    skip_gain,
    norm_gain,
    norm_bias,
    weight_in,
    bias_in,
    weight_out,
    bias_out,
    layer_scale,
):
    slot_count, chan_count, length = (images.shape[0], images.shape[1], images.shape[2])
    pixels = length * length
    image_count = slot_image.shape[0]
    slot_ids = lax.axis_index("dp") * slot_count + jnp.arange(slot_count, dtype=jnp.int32)
    choose = (slot_ids[:, None] == jnp.arange(image_count, dtype=jnp.int32)[None, :]).astype(
        jnp.int32
    )
    picked = jnp.sum(choose * slot_image[None, :], axis=1)
    owners = (picked[:, None] == jnp.arange(image_count, dtype=jnp.int32)[None, :]).astype(
        jnp.int32
    )
    heights = jnp.sum(owners * image_sizes[None, :, 0], axis=1)
    widths = jnp.sum(owners * image_sizes[None, :, 1], axis=1)
    offsets = jnp.arange(length, dtype=jnp.int32)
    inside = (
        (offsets[None, :, None] < heights[:, None, None])
        & (offsets[None, None, :] < widths[:, None, None])
    ).astype(jnp.float32)
    masked_in = images.astype(jnp.float32) * inside[:, None]
    mixed_out, mixer_pull = jax.vjp(
        mixer,
        masked_in,
        rows_rate,
        rows_freq,
        rows_real,
        rows_imag,
        cols_rate,
        cols_freq,
        cols_real,
        cols_imag,
        skip_gain,
    )
    mixed_low = mixed_out.astype(jnp.bfloat16).reshape(slot_count, chan_count, pixels)
    mask_flat = inside.reshape(slot_count, 1, pixels)
    residual = images.astype(jnp.float32).reshape(slot_count, chan_count, pixels)
    grad_out = cotangent.astype(jnp.float32).reshape(slot_count, chan_count, pixels) * mask_flat
    chan_offset = lax.axis_index("chan") * chan_count
    all_channels = norm_gain.shape[0]
    slot_item = 0
    gathered = lax.all_gather(mixed_low[slot_item], "chan", axis=0, tiled=True)
    normed, scaled, inverse = normalize(gathered.astype(jnp.float32), norm_gain, norm_bias)
    normed_low = normed.astype(jnp.bfloat16)
    before = (
        jnp.einsum("cf,cp->fp", weight_in, normed_low, preferred_element_type=jnp.float32)
        + bias_in.astype(jnp.float32)[:, None]
    )
    active = gelu_exact(before).astype(jnp.bfloat16)

    def project(first_row, row_count, active=active):
        return jnp.einsum("fc,fp->cp", weight_out, active, preferred_element_type=jnp.float32)

    branch_list = [
        lax.psum_scatter(
            project(jnp.int32(0), chan_count * lax.axis_size("chan")),
            "chan",
            scatter_dimension=0,
            tiled=True,
        )
    ]
    scaled_part = lax.dynamic_slice_in_dim(scaled, chan_offset, chan_count, 0)
    stored = [(normed_low, before, active, scaled_part, inverse)]
    branch_all = jnp.stack(branch_list)
    shifted = branch_all + bias_out[None, :, None]
    output = (
        (mask_flat * (residual + layer_scale[None, :, None] * shifted))
        .astype(jnp.bfloat16)
        .reshape(images.shape)
    )
    scale_grad = jnp.sum(grad_out * shifted, axis=(0, 2))
    branch_grad = layer_scale[None, :, None] * grad_out
    bias_out_grad = jnp.sum(branch_grad, axis=(0, 2))
    branch_low = branch_grad.astype(jnp.bfloat16)
    hidden_count = weight_in.shape[1]
    out_weight_grad = jnp.zeros((hidden_count, all_channels), jnp.float32)
    gain_shard = lax.dynamic_slice_in_dim(norm_gain, chan_offset, chan_count, 0)
    slot_item = 0
    normed_low, before, active, scaled_part, inverse = stored[slot_item]

    def absorb(totals, shard_rows, first_row, active=active):
        hidden_grad = jnp.einsum(
            "fc,cp->fp", weight_out, shard_rows, preferred_element_type=jnp.float32
        )
        product_part = jnp.einsum(
            "fp,cp->fc", active, shard_rows, preferred_element_type=jnp.float32
        )
        return (hidden_grad, product_part)

    hidden_start = jnp.zeros((hidden_count, pixels), jnp.float32)
    hidden_grad, out_weight_grad = absorb(
        (hidden_start, out_weight_grad),
        lax.all_gather(branch_low[slot_item], "chan", axis=0, tiled=True),
        jnp.int32(0),
    )
    gelu_pull = jax.vjp(gelu_exact, before)[1]
    before_grad = gelu_pull(hidden_grad)[0].astype(jnp.bfloat16)
    in_weight_grad = jnp.einsum(
        "cp,fp->cf", normed_low, before_grad, preferred_element_type=jnp.float32
    )
    in_bias_grad = jnp.sum(before_grad.astype(jnp.float32), axis=1)

    def spread_back(first_row, row_count, before_grad=before_grad):
        return jnp.einsum("cf,fp->cp", weight_in, before_grad, preferred_element_type=jnp.float32)

    normed_grad = lax.psum_scatter(
        spread_back(jnp.int32(0), chan_count * lax.axis_size("chan")),
        "chan",
        scatter_dimension=0,
        tiled=True,
    )
    weighted = normed_grad * gain_shard[:, None]
    pixel_sums = (
        lax.psum(jnp.sum(weighted, axis=0).astype(jnp.bfloat16), "chan").astype(jnp.float32),
        lax.psum(jnp.sum(weighted * scaled_part, axis=0).astype(jnp.bfloat16), "chan").astype(
            jnp.float32
        ),
    )
    mixed_grads = [
        inverse
        * (
            weighted
            - pixel_sums[0][None, :] / all_channels
            - scaled_part * pixel_sums[1][None, :] / all_channels
        )
    ]
    gain_part = jnp.sum(normed_grad * scaled_part, axis=1)
    shift_part = jnp.sum(normed_grad, axis=1)
    mixed_grad_all = jnp.stack(mixed_grads)
    gain_grad = lax.dynamic_update_slice_in_dim(
        jnp.zeros((all_channels,), jnp.float32), gain_part, chan_offset, 0
    )
    shift_grad = lax.dynamic_update_slice_in_dim(
        jnp.zeros((all_channels,), jnp.float32), shift_part, chan_offset, 0
    )
    pulled = mixer_pull(mixed_grad_all.reshape(images.shape))
    input_grad = inside[:, None] * (cotangent.astype(jnp.float32) + pulled[0])
    summed = lax.psum(
        (
            in_weight_grad,
            out_weight_grad,
            in_bias_grad,
            bias_out_grad,
            scale_grad,
            pulled[1],
            pulled[2],
            pulled[3],
            pulled[4],
            pulled[5],
            pulled[6],
            pulled[7],
            pulled[8],
            pulled[9],
        ),
        "dp",
    )
    norm_sums = lax.psum((gain_grad, shift_grad), ("dp", "chan"))
    return (
        output,
        input_grad,
        summed[5],
        summed[6],
        summed[7],
        summed[8],
        summed[9],
        summed[10],
        summed[11],
        summed[12],
        summed[13],
        norm_sums[0],
        norm_sums[1],
        summed[0],
        summed[2],
        summed[1],
        summed[3],
        summed[4],
    )


MESH = pl.DeviceIdType.MESH
GROUP = 16
LINES = 4
STEP_HIDDEN = 512
mebi = 1024 * 1024


def dot_nn(left, right):
    return lax.dot_general(left, right, (((1,), (0,)), ((), ())), preferred_element_type=jnp.float32)


def dot_nt(left, right):
    return lax.dot_general(left, right, (((1,), (1,)), ((), ())), preferred_element_type=jnp.float32)


def dot_tn(left, right):
    return lax.dot_general(left, right, (((0,), (0,)), ((), ())), preferred_element_type=jnp.float32)


def split_low(values):
    high = values.astype(jnp.bfloat16)
    return high, (values - high.astype(jnp.float32)).astype(jnp.bfloat16)


def lag_matrix(line, side, keep):
    spread = pltpu.roll(jnp.broadcast_to(line, (side, side)), 0, 1, stride=1, stride_axis=0)
    return jnp.where(keep, spread, 0.0)


def lag_sums(matrix, side, keep):
    turned = pltpu.roll(jnp.where(keep, matrix, 0.0), 0, 1, stride=1, stride_axis=0)
    return jnp.sum(turned, axis=0, keepdims=True)


cos_terms = (
    1.0, -19.7392087, 64.9393891, -85.4566583, 60.242131, -26.4046662, 7.8001253, -1.45310477
)
sin_terms = (6.2831853, -41.3417004, 81.6051314, -76.703015, 42.0259236, -14.8998335, 3.23811835)


def polynomial(terms, at):
    value = terms[-1]
    for term in terms[-2::-1]:
        value = value * at + term
    return value


TILE = 16


def power(rate, freq, lag):
    angle = freq * 0.15915494309189535 * lag
    angle = angle - jnp.floor(angle + 0.5)
    square = angle * angle
    decay = jnp.exp(-rate * lag)
    return decay * polynomial(cos_terms, square), decay * (angle * polynomial(sin_terms, square))


def product(left, right):
    return left[0] * right[0] - left[1] * right[1], left[0] * right[1] + left[1] * right[0]


def taps_lines(rate, freq, real, imag, side, store):
    first = power(rate, freq, 1.0)

    @pl.loop(0, side // TILE)
    def _(tile):
        state = product((real, imag), power(rate, freq, (tile * TILE).astype(jnp.float32)))
        for step in range(TILE):
            store(tile * TILE + step, jnp.sum(state[0], axis=0, keepdims=True))
            state = product(state, first)


def taps_adjoint(rate, freq, real, imag, side, load):
    first = power(rate, freq, 1.0)

    def tile_sums(tile, totals):
        state = power(rate, freq, (tile * TILE).astype(jnp.float32))
        even, odd, even_lag, odd_lag = totals
        for step in range(TILE):
            grad = load(tile * TILE + step)
            late = grad * (tile * TILE + step).astype(jnp.float32)
            even = even + grad * state[0]
            odd = odd + grad * state[1]
            even_lag = even_lag + late * state[0]
            odd_lag = odd_lag + late * state[1]
            state = product(state, first)
        return even, odd, even_lag, odd_lag

    zero = jnp.zeros_like(rate)
    even, odd, even_lag, odd_lag = lax.fori_loop(0, side // TILE, tile_sums, (zero,) * 4)
    return imag * odd_lag - real * even_lag, -real * odd_lag - imag * even_lag, even, -odd


def lane_sums(values):
    ones = jnp.ones((8, values.shape[1]), jnp.bfloat16)
    high, rest = split_low(values)
    low = (values - high.astype(jnp.float32) - rest.astype(jnp.float32)).astype(jnp.bfloat16)
    return dot_nt(ones, high) + dot_nt(ones, rest) + dot_nt(ones, low)


def meet(n, shares):
    me, share = lax.axis_index("chan"), lax.axis_index("dp")
    barrier = pltpu.get_barrier_semaphore()
    for shift in range(1, n):
        pl.semaphore_signal(
            barrier, inc=1, device_id={"chan": lax.rem(me + shift, n)}, device_id_type=MESH
        )
    for shift in range(1, shares):
        pl.semaphore_signal(
            barrier, inc=1, device_id={"dp": lax.rem(share + shift, shares)}, device_id_type=MESH
        )
    pl.semaphore_wait(barrier, n + shares - 2)
    return me, share


def push(source, target, send_sem, recv_sem, **peer):
    return pltpu.make_async_remote_copy(
        src_ref=source,
        dst_ref=target,
        send_sem=send_sem,
        recv_sem=recv_sem,
        device_id=peer,
        device_id_type=MESH,
    )


def weight_rounds(n, shares, me, share, pairs, sems):
    near, far = n // 2, me // 2
    core = lax.rem(me, 2)
    own_sem, send1, recv1, send2, recv2, send3, recv3 = sems

    def own(at):
        local, whole = pairs[at]
        return pltpu.make_async_copy(local, whole.at[core, :, far], own_sem.at[at])

    def first(at, shift, back=False):
        local, whole = pairs[at]
        origin = lax.rem(far + near - shift, near) if back else far
        return push(
            local.at[share],
            whole.at[core, share, origin],
            send1.at[at, shift],
            recv1.at[at, shift],
            chan=lax.rem(far + shift, near) * 2 + core,
        )

    def second(at, shift, turn, back=False):
        whole = pairs[at][1]
        origin = lax.rem(far + near - shift, near)
        holder = lax.rem(share + shares - turn, shares) if back else share
        return push(
            whole.at[core, share, origin],
            whole.at[core, holder, origin],
            send2.at[at, shift, turn],
            recv2.at[at, shift, turn],
            dp=lax.rem(share + turn, shares),
        )

    def third(at, back=False):
        whole = pairs[at][1]
        return push(
            whole.at[core], whole.at[1 - core if back else core], send3.at[at], recv3.at[at], chan=far * 2 + 1 - core
        )

    both = range(len(pairs))

    def start_first():
        for at in both:
            own(at).start()
            for shift in range(1, near):
                first(at, shift).start()

    def start_second():
        for at in both:
            for shift in range(1, near):
                first(at, shift, True).wait_recv()
                for turn in range(1, shares):
                    second(at, shift, turn).start()

    def start_third():
        for at in both:
            own(at).wait()
            for shift in range(1, near):
                for turn in range(1, shares):
                    second(at, shift, turn, True).wait_recv()
            third(at).start()

    def finish():
        for at in both:
            third(at, True).wait_recv()
            third(at).wait_send()
            for shift in range(1, near):
                first(at, shift).wait_send()
                for turn in range(1, shares):
                    second(at, shift, turn).wait_send()

    return start_first, start_second, start_third, finish


def send_part(stage, target, me, peer, part, send_sem, recv_sem, shift):
    return pltpu.make_async_remote_copy(
        src_ref=stage.at[peer, part],
        dst_ref=target.at[me, part],
        send_sem=send_sem.at[shift],
        recv_sem=recv_sem.at[shift],
        device_id={"chan": peer},
        device_id_type=MESH,
    )


def wait_parts(stage, target, me, n, send_sem, recv_sem):
    for shift in range(1, n):
        peer = lax.rem(me + shift, n)
        origin = lax.rem(me + n - shift, n)
        pltpu.make_async_remote_copy(
            src_ref=stage.at[peer],
            dst_ref=target.at[origin],
            send_sem=send_sem.at[shift],
            recv_sem=recv_sem.at[shift],
            device_id={"chan": peer},
            device_id_type=MESH,
        ).wait()


def mixer_kernel(
    n,
    shares,
    sizes_ref,
    image_ref,
    cot_ref,
    rate_ref,
    freq_ref,
    real_ref,
    imag_ref,
    cols_rate_ref,
    cols_freq_ref,
    cols_real_ref,
    cols_imag_ref,
    skip_ref,
    scale_ref,
    in_part_ref,
    out_part_ref,
    mixed_ref,
    back_ref,
    in_whole_ref,
    out_whole_ref,
    sums_ref,
    rows_back_ref,
    rows_ref,
    cols_back_ref,
    cols_ref,
    mixed_stage,
    back_stage,
    wide,
    taps,
    send_m,
    recv_m,
    send_b,
    recv_b,
    own_sem,
    *weight_sems,
):
    count, side, _ = image_ref.shape
    parts = count // GROUP
    block = side // n
    me, share = meet(n, shares)
    start_first, start_second, start_third, finish = weight_rounds(
        n, shares, me, share, ((in_part_ref, in_whole_ref), (out_part_ref, out_whole_ref)), weight_sems
    )
    start_first()
    taps[...] = jnp.zeros_like(taps)
    row_at = lax.broadcasted_iota(jnp.int32, (side, side), 0)
    col_at = lax.broadcasted_iota(jnp.int32, (side, side), 1)
    inside = (row_at < sizes_ref[0]) & (col_at < sizes_ref[1])
    lower = row_at >= col_at
    upper = row_at <= col_at

    def turn(stage, part):
        @pl.loop(0, n)
        def _(owner):
            for line in range(block):
                tile = wide[pl.ds(owner * block + line, GROUP, stride=side), :]
                stage[owner, part, line] = tile.astype(jnp.bfloat16)

    def send(stage, target, part, send_sem, recv_sem):
        for shift in range(1, n):
            send_part(stage, target, me, lax.rem(me + shift, n), part, send_sem, recv_sem, shift).start()

    @pl.loop(0, parts)
    def _(part):
        @pl.loop(0, GROUP)
        def _(item):
            chan = part * GROUP + item
            grad_out = jnp.where(inside, cot_ref[chan].astype(jnp.float32), 0.0)
            scaled = grad_out * scale_ref[pl.ds(chan, 1), :]
            sums_ref[pl.ds(chan, 1), :] = jnp.sum(scaled, axis=0, keepdims=True)
            wide[pl.ds(pl.multiple_of(item * side, side), side), :] = scaled

        turn(back_stage, part)
        send(back_stage, back_ref, part, send_b, recv_b)

    for (rate, freq, real, imag), back_out, out in (
        ((rate_ref, freq_ref, real_ref, imag_ref), rows_back_ref, rows_ref),
        ((cols_rate_ref, cols_freq_ref, cols_real_ref, cols_imag_ref), cols_back_ref, cols_ref),
    ):

        def store(lag, line):
            taps[0, pl.ds(lax.rem(side - lag, side), 1), :count] = line
            taps[1, pl.ds(lag, 1), :count] = line

        taps_lines(rate[...], freq[...], real[...], imag[...], side, store)
        back_out[...] = taps[0].T[:count]
        out[...] = taps[1].T[:count]

    start_second()

    @pl.loop(0, parts)
    def _(part):
        @pl.loop(0, GROUP)
        def _(item):
            chan = part * GROUP + item
            masked = jnp.where(inside, image_ref[chan].astype(jnp.float32), 0.0)
            masked_low = masked.astype(jnp.bfloat16)
            rows_high, rows_low = split_low(lag_matrix(rows_back_ref[pl.ds(chan, 1), :], side, lower))
            cols_high, cols_low = split_low(lag_matrix(cols_ref[pl.ds(chan, 1), :], side, upper))
            along = dot_nn(
                jnp.concatenate([rows_high, rows_low], axis=1),
                jnp.concatenate([masked_low, masked_low], axis=0),
            )
            along_high, along_low = split_low(along)
            mixed = dot_nn(
                jnp.concatenate([along_high, along_low], axis=1),
                jnp.concatenate([cols_high, cols_high], axis=0),
            ) + dot_nn(along_high, cols_low)
            mixed = mixed + skip_ref[pl.ds(chan, 1), :] * masked
            wide[pl.ds(pl.multiple_of(item * side, side), side), :] = mixed

        turn(mixed_stage, part)
        send(mixed_stage, mixed_ref, part, send_m, recv_m)

    start_third()
    own_b = pltpu.make_async_copy(back_stage.at[me], back_ref.at[me], own_sem.at[0])
    own_m = pltpu.make_async_copy(mixed_stage.at[me], mixed_ref.at[me], own_sem.at[1])
    own_b.start()
    own_m.start()
    own_b.wait()
    own_m.wait()
    wait_parts(back_stage, back_ref, me, n, send_b, recv_b)
    wait_parts(mixed_stage, mixed_ref, me, n, send_m, recv_m)
    finish()


def mixer_forward(n, shares, sizes, images, cotangent, params, skip_wide, scale_wide, in_part, out_part):
    near = n // 2
    count, side, _ = images.shape
    line = jax.ShapeDtypeStruct((count, side), jnp.float32)
    shape = (n, count // GROUP, side // n, GROUP, side)
    vmem = pl.BlockSpec(memory_space=pltpu.VMEM)
    hbm = pl.BlockSpec(memory_space=pl.ANY)
    return pl.pallas_call(
        functools.partial(mixer_kernel, n, shares),
        out_shape=(
            jax.ShapeDtypeStruct(shape, jnp.bfloat16),
            jax.ShapeDtypeStruct(shape, jnp.bfloat16),
        )
        + tuple(
            jax.ShapeDtypeStruct((2, shares, near, *part.shape[1:]), jnp.bfloat16)
            for part in (in_part, out_part)
        )
        + (line,) * 5,
        in_specs=[pl.BlockSpec(memory_space=pltpu.SMEM)] + [vmem] * 12 + [hbm] * 2,
        out_specs=(hbm,) * 4 + (vmem,) * 5,
        scratch_shapes=[
            pltpu.VMEM(shape, jnp.bfloat16),
            pltpu.VMEM(shape, jnp.bfloat16),
            pltpu.VMEM((GROUP * side, side), jnp.float32),
            pltpu.VMEM((2, side, side), jnp.float32),
            pltpu.SemaphoreType.DMA((n,)),
            pltpu.SemaphoreType.DMA((n,)),
            pltpu.SemaphoreType.DMA((n,)),
            pltpu.SemaphoreType.DMA((n,)),
            pltpu.SemaphoreType.DMA((2,)),
            pltpu.SemaphoreType.DMA((2,)),
            pltpu.SemaphoreType.DMA((2, near)),
            pltpu.SemaphoreType.DMA((2, near)),
            pltpu.SemaphoreType.DMA((2, near, shares)),
            pltpu.SemaphoreType.DMA((2, near, shares)),
            pltpu.SemaphoreType.DMA((2,)),
            pltpu.SemaphoreType.DMA((2,)),
        ],
        compiler_params=pltpu.CompilerParams(
            collective_id=0, has_side_effects=True, vmem_limit_bytes=40 * mebi
        ),
        name="mixer_forward",
    )(sizes, images, cotangent, *params, skip_wide, scale_wide, in_part, out_part)


def gelu_parts(value):
    bell = jnp.exp(-0.5 * value * value)
    inner = 1.0 / (1.0 + (0.3275911 * 0.7071067811865476) * jnp.abs(value))
    series = 1.061405429 * inner - 1.453152027
    series = series * inner + 1.421413741
    series = series * inner - 0.284496736
    series = series * inner + 0.254829592
    tail = (0.5 * inner) * series * bell
    return jnp.where(value < 0.0, tail, 1.0 - tail), bell * 0.3989422804014327


def mlp_kernel(
    n,
    shares,
    mixed_ref,
    back_ref,
    in_ref,
    out_ref,
    gain_ref,
    shift_ref,
    grad_ref,
    branch_ref,
    active_ref,
    before_grad_ref,
    out_take_ref,
    in_own_ref,
    in_got_ref,
    gain_grad_ref,
    shift_grad_ref,
    grad_stage,
    branch_stage,
    active_ring,
    before_ring,
    normed_keep,
    cots_keep,
    scaled_keep,
    inverse_keep,
    branch_sum,
    grad_sum,
    hidden_sum,
    pieces,
    rows_stage,
    out_got,
    send_g,
    recv_g,
    own_sem,
    ring_sem,
    piece_sem,
    half_sem,
    send_h,
    recv_h,
    send_2,
    recv_2,
):
    side = mixed_ref.shape[-1]
    groups = mixed_ref.shape[1]
    block = mixed_ref.shape[2]
    hidden, channels = out_ref.shape
    local = channels // n
    steps = block // LINES
    width = LINES * side
    parts = hidden // STEP_HIDDEN
    ring = active_ring.shape[0]
    me, share = meet(n, shares)
    core = lax.rem(me, 2)
    sibling = me + 1 - 2 * core
    gain_grad_ref[...] = jnp.zeros_like(gain_grad_ref)
    shift_grad_ref[...] = jnp.zeros_like(shift_grad_ref)
    hidden_sum[...] = jnp.zeros_like(hidden_sum)

    def keeps(turn):
        slot = lax.rem(turn, ring)
        span = pl.ds(pl.multiple_of(lax.rem(turn, parts) * STEP_HIDDEN, STEP_HIDDEN), STEP_HIDDEN)
        return [
            pltpu.make_async_copy(kept.at[slot], whole.at[turn // parts, span], ring_sem.at[at, slot])
            for at, (kept, whole) in enumerate(((active_ring, active_ref), (before_ring, before_grad_ref)))
        ]

    @pl.loop(0, steps)
    def _(step):
        for line in range(LINES):
            row = step * LINES + line
            lanes = pl.ds(line * side, side)
            order = [(owner, group) for owner in range(n) for group in range(groups)]
            mixed = jnp.concatenate(
                [mixed_ref[owner, group, row].astype(jnp.float32) for owner, group in order], axis=0
            )
            mean = jnp.sum(mixed, axis=0, keepdims=True) * (1.0 / channels)
            center = mixed - mean
            var = jnp.sum(center * center, axis=0, keepdims=True) * (1.0 / channels)
            inverse = lax.rsqrt(var + eps_norm)
            scaled = center * inverse
            normed_keep[step, :, lanes] = (scaled * gain_ref[...] + shift_ref[...]).astype(jnp.bfloat16)
            scaled_keep[:, lanes] = scaled
            inverse_keep[:, lanes] = inverse
            cots_keep[step, :, lanes] = jnp.concatenate(
                [back_ref[owner, group, row] for owner, group in order], axis=0
            )

        @pl.loop(0, parts)
        def _(part):
            turn = step * parts + part
            slot = lax.rem(turn, ring)

            @pl.when(turn >= ring)
            def _():
                for copy in keeps(turn - ring):
                    copy.wait()

            span = pl.ds(pl.multiple_of(part * STEP_HIDDEN, STEP_HIDDEN), STEP_HIDDEN)
            bias = in_ref[span, channels:].astype(jnp.float32)[:, :1]
            before = dot_nn(in_ref[span, :channels], normed_keep[step]) + bias
            inside, bell = gelu_parts(before)
            active = (before * inside).astype(jnp.bfloat16)
            active_grad = dot_nn(out_ref[span, :], cots_keep[step])
            before_grad = (active_grad * (inside + before * bell)).astype(jnp.bfloat16)
            active_ring[slot] = active
            before_ring[slot] = before_grad
            hidden_sum[span, :] += sum(
                before_grad[:, line * side : (line + 1) * side].astype(jnp.float32) for line in range(LINES)
            )
            branch = dot_tn(out_ref[span, :], active)
            grad = dot_tn(in_ref[span, :channels], before_grad)

            @pl.when(part == 0)
            def _():
                branch_sum[...] = branch
                grad_sum[...] = grad

            @pl.when(part > 0)
            def _():
                branch_sum[...] += branch
                grad_sum[...] += grad

            for copy in keeps(turn):
                copy.start()

        for line in range(LINES):
            lanes = pl.ds(line * side, side)
            grad = grad_sum[:, lanes]
            scaled = scaled_keep[:, lanes]
            gain_grad_ref[...] += grad * scaled
            shift_grad_ref[...] += grad
            weighted = grad * gain_ref[...]
            first = jnp.sum(weighted, axis=0, keepdims=True) * (1.0 / channels)
            second = jnp.sum(weighted * scaled, axis=0, keepdims=True) * (1.0 / channels)
            mixed_grad = (inverse_keep[:, lanes] * (weighted - first - scaled * second)).astype(jnp.bfloat16)
            branch = branch_sum[:, lanes].astype(jnp.bfloat16)
            for owner in range(n):
                grad_stage[owner, step, line] = mixed_grad[owner * local : (owner + 1) * local]
                branch_stage[owner, step, line] = branch[owner * local : (owner + 1) * local]

        for shift in range(1, n):
            send_part(grad_stage, grad_ref, me, lax.rem(me + shift, n), step, send_g, recv_g, shift).start()

    own_g = pltpu.make_async_copy(grad_stage.at[me], grad_ref.at[me], own_sem.at[0])
    own_r = pltpu.make_async_copy(branch_stage, branch_ref, own_sem.at[1])
    own_g.start()
    own_r.start()
    turns = steps * parts
    for turn in range(turns - ring, turns):
        for copy in keeps(turn):
            copy.wait()

    half = parts // 2
    kinds = (
        (active_ref, cots_keep, None, out_got, channels),
        (before_grad_ref, normed_keep, in_own_ref, in_got_ref, channels + side),
    )

    def place(job):
        at = lax.rem((1 - core) * half + job, parts)
        return pl.ds(pl.multiple_of(at * STEP_HIDDEN, STEP_HIDDEN), STEP_HIDDEN)

    def fetch(kind, job, slot):
        return pltpu.make_async_copy(kinds[kind][0].at[:, place(job)], pieces.at[slot], piece_sem.at[slot])

    def give(kind, job):
        _, _, _, got, wide = kinds[kind]
        return push(
            rows_stage.at[job, :, pl.ds(0, wide)],
            got.at[pl.ds(job * STEP_HIDDEN, STEP_HIDDEN)],
            send_h.at[kind, job],
            recv_h.at[kind, job],
            chan=sibling,
        )

    def keep(job):
        return pltpu.make_async_copy(
            rows_stage.at[job],
            in_own_ref.at[pl.ds((job - half) * STEP_HIDDEN, STEP_HIDDEN)],
            half_sem.at[job],
        )

    block_rows = hidden // 2 // shares

    def second(turn):
        peer = lax.rem(share + turn, shares)
        span = pl.ds(pl.multiple_of(peer * block_rows, block_rows), block_rows)
        if turn == 0:
            return pltpu.make_async_copy(out_got.at[span], out_take_ref.at[0], send_2.at[0])
        return push(out_got.at[span], out_take_ref.at[turn], send_2.at[turn], recv_2.at[turn], dp=peer)

    jobs = [(kind, job) for kind in range(2) for job in range(parts)]
    fetch(0, 0, 0).start()
    for at, (kind, job) in enumerate(jobs):
        slot = at % 2
        if at + 1 < len(jobs):
            fetch(*jobs[at + 1], (at + 1) % 2).start()
        if at == parts:
            for done in range(half):
                give(0, done).wait()
                span = pl.ds(done * STEP_HIDDEN, STEP_HIDDEN)
                mine = rows_stage[half + done, :, :channels].astype(jnp.float32)
                out_got[span, :] = (mine + out_got[span, :].astype(jnp.float32)).astype(jnp.bfloat16)
            for turn in range(shares):
                second(turn).start()
        fetch(kind, job, slot).wait()
        right = kinds[kind][1]
        total = dot_nt(pieces[slot, 0], right[0])
        for step in range(1, steps):
            total = total + dot_nt(pieces[slot, step], right[step])
        rows_stage[job, :, :channels] = total.astype(jnp.bfloat16)
        if kind == 1:
            rows_stage[job, :, channels:] = hidden_sum[place(job), :].astype(jnp.bfloat16)
        if job < half:
            give(kind, job).start()
        elif kind == 1:
            keep(job).start()
    for job in range(parts):
        (give(1, job) if job < half else keep(job)).wait()
    for turn in range(shares):
        second(turn).wait()
    own_g.wait()
    own_r.wait()
    wait_parts(grad_stage, grad_ref, me, n, send_g, recv_g)


def mlp(n, shares, mixed, back, in_full, out_full, gain, shift):
    _, groups, block, group, side = mixed.shape
    hidden, channels = out_full.shape
    local = channels // n
    steps = block // LINES
    width = LINES * side
    parts = hidden // STEP_HIDDEN
    shape = (n, steps, LINES, local, side)
    ring = 4
    low = functools.partial(jax.ShapeDtypeStruct, dtype=jnp.bfloat16)
    vmem = pl.BlockSpec(memory_space=pltpu.VMEM)
    hbm = pl.BlockSpec(memory_space=pl.ANY)
    return pl.pallas_call(
        functools.partial(mlp_kernel, n, shares),
        out_shape=(
            low(shape),
            low(shape),
            low((steps, hidden, width)),
            low((steps, hidden, width)),
            low((shares, hidden // 2 // shares, channels)),
            low((hidden // 2, channels + side)),
            low((hidden // 2, channels + side)),
            jax.ShapeDtypeStruct((channels, side), jnp.float32),
            jax.ShapeDtypeStruct((channels, side), jnp.float32),
        ),
        in_specs=[vmem] * 6,
        out_specs=(hbm,) * 7 + (vmem, vmem),
        scratch_shapes=[
            pltpu.VMEM(shape, jnp.bfloat16),
            pltpu.VMEM(shape, jnp.bfloat16),
            pltpu.VMEM((ring, STEP_HIDDEN, width), jnp.bfloat16),
            pltpu.VMEM((ring, STEP_HIDDEN, width), jnp.bfloat16),
            pltpu.VMEM((steps, channels, width), jnp.bfloat16),
            pltpu.VMEM((steps, channels, width), jnp.bfloat16),
            pltpu.VMEM((channels, width), jnp.float32),
            pltpu.VMEM((1, width), jnp.float32),
            pltpu.VMEM((channels, width), jnp.float32),
            pltpu.VMEM((channels, width), jnp.float32),
            pltpu.VMEM((hidden, side), jnp.float32),
            pltpu.VMEM((2, steps, STEP_HIDDEN, width), jnp.bfloat16),
            pltpu.VMEM((parts, STEP_HIDDEN, channels + side), jnp.bfloat16),
            pltpu.VMEM((hidden // 2, channels), jnp.bfloat16),
            pltpu.SemaphoreType.DMA((n,)),
            pltpu.SemaphoreType.DMA((n,)),
            pltpu.SemaphoreType.DMA((2,)),
            pltpu.SemaphoreType.DMA((2, ring)),
            pltpu.SemaphoreType.DMA((2,)),
            pltpu.SemaphoreType.DMA((parts,)),
            pltpu.SemaphoreType.DMA((2, parts)),
            pltpu.SemaphoreType.DMA((2, parts)),
            pltpu.SemaphoreType.DMA((shares,)),
            pltpu.SemaphoreType.DMA((shares,)),
        ],
        compiler_params=pltpu.CompilerParams(
            collective_id=1, has_side_effects=True, vmem_limit_bytes=63 * mebi
        ),
        name="mlp",
    )(mixed, back, in_full, out_full, gain, shift)


def sum_rounds(n, shares, me, share, part, final, stage3, take3, keep3, send3, recv3, send4, recv4, own_sem):
    near, far = n // 2, me // 2
    core = lax.rem(me, 2)

    def third(turn):
        peer = lax.rem(far + turn, near)
        return push(stage3.at[peer], take3.at[turn], send3.at[turn], recv3.at[turn], chan=peer * 2 + core)

    def fourth(turn, back=False):
        holder = lax.rem(share + shares - turn, shares) if back else share
        peer = lax.rem(share + turn, shares)
        return push(keep3, final.at[holder], send4.at[turn], recv4.at[turn], dp=peer)

    def mine():
        return pltpu.make_async_copy(keep3, final.at[share], own_sem.at[0])

    def start_third():
        for at in range(near):
            total = part(at)
            stage3[at] = total.astype(jnp.bfloat16)

            @pl.when(far == at)
            def _():
                keep3[...] = total

        for turn in range(1, near):
            third(turn).start()

    def start_fourth():
        for turn in range(1, near):
            third(turn).wait()
        total = keep3[...]
        for turn in range(1, near):
            total = total + take3[turn].astype(jnp.float32)
        keep3[...] = total
        mine().start()
        for turn in range(1, shares):
            fourth(turn).start()

    def finish():
        mine().wait()
        for turn in range(1, shares):
            fourth(turn, True).wait_recv()
            fourth(turn).wait_send()

    return start_third, start_fourth, finish


def back_kernel(
    n,
    shares,
    sizes_ref,
    image_ref,
    cot_ref,
    grad_ref,
    branch_ref,
    rows_back_ref,
    rows_ref,
    cols_back_ref,
    skip_ref,
    scale_ref,
    bias_ref,
    bias_sums_ref,
    gain_sums_ref,
    shift_sums_ref,
    out_take_ref,
    in_own_ref,
    in_got_ref,
    output_ref,
    input_grad_ref,
    small_ref,
    norm_ref,
    out_final_ref,
    in_final_ref,
    wide,
    branch_got,
    rows_sums,
    cols_sums,
    skip_sums,
    scale_sums,
    small_own,
    small_got,
    norm_own,
    norm_near,
    norm_mid,
    norm_far,
    stage2,
    take2,
    out_stage3,
    out_take3,
    out_keep3,
    in_stage3,
    in_take3,
    in_keep3,
    send_sem,
    recv_sem,
    own_sem,
    send_2,
    recv_2,
    send_s,
    recv_s,
    send_n,
    recv_n,
    send_f,
    recv_f,
    *round_sems,
):
    count, side, _ = image_ref.shape
    steps, lines = branch_ref.shape[1], branch_ref.shape[2]
    near = n // 2
    rows = in_keep3.shape[0]
    block = near * rows
    me, share = meet(n, shares)

    def out_part(at):
        span = slice(at * rows, (at + 1) * rows)
        return sum(out_take_ref[turn, span].astype(jnp.float32) for turn in range(shares))

    def in_part(at):
        base = pl.ds(pl.multiple_of(share * block + at * rows, rows), rows)
        total = in_own_ref[base, :].astype(jnp.float32) + in_got_ref[base, :].astype(jnp.float32)
        for turn in range(1, shares):
            total = total + take2[turn, at * rows : (at + 1) * rows].astype(jnp.float32)
        return total

    out_third, out_fourth, out_finish = sum_rounds(
        n, shares, me, share, out_part, out_final_ref, out_stage3, out_take3, out_keep3, *round_sems[:5]
    )
    in_third, in_fourth, in_finish = sum_rounds(
        n, shares, me, share, in_part, in_final_ref, in_stage3, in_take3, in_keep3, *round_sems[5:]
    )

    def in_second(turn):
        peer = lax.rem(share + turn, shares)
        return push(stage2.at[peer], take2.at[turn], send_2.at[turn], recv_2.at[turn], dp=peer)

    def norm_first(turn):
        peer = lax.rem(share + turn, shares)
        return push(norm_own, norm_near.at[turn], send_n.at[turn], recv_n.at[turn], dp=peer)

    def norm_second(turn):
        peer = lax.rem(me + turn, n)
        return push(norm_mid, norm_far.at[turn], send_f.at[turn], recv_f.at[turn], chan=peer)

    def small_push(turn):
        peer = lax.rem(share + turn, shares)
        return push(small_own, small_got.at[turn], send_s.at[turn], recv_s.at[turn], dp=peer)

    def norm_pass():
        total = norm_own[...]
        for turn in range(1, shares):
            norm_first(turn).wait()
            total = total + norm_near[turn]
        norm_mid[...] = total
        for turn in range(1, n):
            norm_second(turn).start()

    def in_pass():
        for turn in range(1, shares):
            in_second(turn).wait()
        in_third()

    out_third()
    for at in range(shares):
        span = slice(at * block, (at + 1) * block)
        stage2[at] = (in_own_ref[span].astype(jnp.float32) + in_got_ref[span].astype(jnp.float32)).astype(
            jnp.bfloat16
        )
    for turn in range(1, shares):
        in_second(turn).start()
    top = lax.broadcasted_iota(jnp.int32, norm_own.shape, 0) == 0
    norm_own[...] = jnp.where(top, lane_sums(gain_sums_ref[...]), lane_sums(shift_sums_ref[...]))
    for turn in range(1, shares):
        norm_first(turn).start()
    for shift in range(1, n):
        peer = lax.rem(me + shift, n)
        push(
            branch_ref.at[peer], branch_got.at[me], send_sem.at[shift], recv_sem.at[shift], chan=peer
        ).start()
    own = pltpu.make_async_copy(branch_ref.at[me], branch_got.at[me], own_sem.at[0])
    own.start()
    row_at = lax.broadcasted_iota(jnp.int32, (side, side), 0)
    col_at = lax.broadcasted_iota(jnp.int32, (side, side), 1)
    inside = (row_at < sizes_ref[0]) & (col_at < sizes_ref[1])
    lower = row_at >= col_at
    upper = row_at <= col_at
    flip = (row_at + col_at == side - 1).astype(jnp.bfloat16)

    @pl.loop(0, side)
    def _(row):
        span = pl.ds(pl.multiple_of(row * count, count), count)
        wide[span, :] = grad_ref[row].astype(jnp.float32)

    @pl.loop(0, count)
    def _(chan):
        pl.when(chan == count // 3)(out_fourth)
        pl.when(chan == count // 3)(norm_pass)
        pl.when(chan == count * 3 // 4)(in_pass)
        one = pl.ds(chan, 1)
        grad = wide[pl.ds(chan, side, stride=count), :]
        image = image_ref[chan].astype(jnp.float32)
        grad_out = jnp.where(inside, cot_ref[chan].astype(jnp.float32), 0.0)
        masked = jnp.where(inside, image, 0.0)
        skip_sums[one, :] = jnp.sum(grad * masked, axis=0, keepdims=True)
        masked_low = masked.astype(jnp.bfloat16)
        grad_low = grad.astype(jnp.bfloat16)
        grad_turned = dot_nt(flip, grad_low).astype(jnp.bfloat16)
        masked_turned = dot_nn(flip, masked_low).astype(jnp.bfloat16)
        rows_high, rows_low = split_low(lag_matrix(rows_back_ref[one, :], side, lower))
        turned_high, turned_low = split_low(lag_matrix(rows_ref[one, :], side, upper))
        cols_high, cols_low = split_low(lag_matrix(cols_back_ref[one, :], side, lower))
        along = dot_nn(
            jnp.concatenate([rows_high, rows_low], axis=1),
            jnp.concatenate([masked_low, masked_low], axis=0),
        )
        along_grad = dot_nn(
            jnp.concatenate([grad_low, grad_low], axis=1),
            jnp.concatenate([cols_high, cols_low], axis=0),
        )
        along_high, along_low = split_low(along)
        grad_high, grad_rest = split_low(along_grad)
        cols_grad = dot_nn(
            jnp.concatenate([grad_turned, grad_turned], axis=1),
            jnp.concatenate([along_high, along_low], axis=0),
        )
        rows_grad = dot_nt(
            jnp.concatenate([grad_high, grad_rest], axis=1),
            jnp.concatenate([masked_turned, masked_turned], axis=1),
        )
        masked_grad = dot_nn(
            jnp.concatenate([turned_high, turned_low], axis=1),
            jnp.concatenate([grad_high, grad_high], axis=0),
        ) + dot_nn(turned_high, grad_rest)
        masked_grad = masked_grad + skip_ref[one, :] * grad
        input_grad_ref[chan] = jnp.where(inside, grad_out + masked_grad, 0.0)
        rows_sums[one, :] = lag_sums(rows_grad, side, row_at + col_at >= side - 1)
        cols_sums[one, :] = lag_sums(cols_grad, side, row_at + col_at <= side - 1)

    small_own[:, :side] = rows_sums[...]
    small_own[:, side : 2 * side] = cols_sums[...]
    in_fourth()
    own.wait()
    for shift in range(1, n):
        peer = lax.rem(me + shift, n)
        pltpu.make_async_remote_copy(
            src_ref=branch_ref.at[peer],
            dst_ref=branch_got.at[lax.rem(me + n - shift, n)],
            send_sem=send_sem.at[shift],
            recv_sem=recv_sem.at[shift],
            device_id={"chan": peer},
            device_id_type=MESH,
        ).wait()

    @pl.loop(0, n * steps)
    def _(step):
        for line in range(lines):
            span = pl.ds(pl.multiple_of((step * lines + line) * count, count), count)
            wide[span, :] = branch_got[step // steps, lax.rem(step, steps), line].astype(jnp.float32)

    @pl.loop(0, count)
    def _(chan):
        one = pl.ds(chan, 1)
        shifted = wide[pl.ds(chan, side, stride=count), :] + bias_ref[one, :]
        image = image_ref[chan].astype(jnp.float32)
        grad_out = jnp.where(inside, cot_ref[chan].astype(jnp.float32), 0.0)
        output_ref[chan] = jnp.where(inside, image + scale_ref[one, :] * shifted, 0.0).astype(jnp.bfloat16)
        scale_sums[one, :] = jnp.sum(grad_out * shifted, axis=0, keepdims=True)

    lane = lax.broadcasted_iota(jnp.int32, (count, side), 1)
    last = jnp.zeros((count, side), jnp.float32)
    for at, sums in enumerate((skip_sums, bias_sums_ref, scale_sums)):
        last = jnp.where(lane == at, jnp.sum(sums[...], axis=1, keepdims=True), last)
    small_own[:, 2 * side :] = last
    for turn in range(1, shares):
        small_push(turn).start()
    total = norm_mid[...]
    for turn in range(1, n):
        norm_second(turn).wait()
        total = total + norm_far[turn]
    norm_ref[...] = total
    out_finish()
    in_finish()
    total = small_own[...]
    for turn in range(1, shares):
        small_push(turn).wait()
        total = total + small_got[turn]
    small_ref[...] = total


def mixer_back(n, shares, sizes, images, cotangent, grad, branch, lines, norms, sums):
    count, side, _ = images.shape
    near = n // 2
    out_take, in_own, _ = sums
    block, channels = out_take.shape[1:]
    rows = block // near
    wide = in_own.shape[1]
    line = pltpu.VMEM((count, side), jnp.float32)
    norm = pltpu.VMEM((8, channels), jnp.float32)
    vmem = pl.BlockSpec(memory_space=pltpu.VMEM)
    hbm = pl.BlockSpec(memory_space=pl.ANY)
    full = functools.partial(jax.ShapeDtypeStruct, dtype=jnp.float32)
    return pl.pallas_call(
        functools.partial(back_kernel, n, shares),
        out_shape=(
            jax.ShapeDtypeStruct(images.shape, jnp.bfloat16),
            full(images.shape),
            full((count, 3 * side)),
            full((8, channels)),
            full((shares, rows, channels)),
            full((shares, rows, wide)),
        ),
        in_specs=[pl.BlockSpec(memory_space=pltpu.SMEM)]
        + [vmem] * 3
        + [hbm]
        + [vmem] * (len(lines) + len(norms) + len(sums)),
        out_specs=(vmem,) * 4 + (hbm,) * 2,
        scratch_shapes=[
            pltpu.VMEM((count * side, side), jnp.float32),
            pltpu.VMEM(branch.shape, jnp.bfloat16),
            line,
            line,
            line,
            line,
            pltpu.VMEM((count, 3 * side), jnp.float32),
            pltpu.VMEM((shares, count, 3 * side), jnp.float32),
            norm,
            pltpu.VMEM((shares, 8, channels), jnp.float32),
            norm,
            pltpu.VMEM((n, 8, channels), jnp.float32),
            pltpu.VMEM((shares, block, wide), jnp.bfloat16),
            pltpu.VMEM((shares, block, wide), jnp.bfloat16),
        ]
        + [
            kind
            for columns in (channels, wide)
            for kind in (
                pltpu.VMEM((near, rows, columns), jnp.bfloat16),
                pltpu.VMEM((near, rows, columns), jnp.bfloat16),
                pltpu.VMEM((rows, columns), jnp.float32),
            )
        ]
        + [
            pltpu.SemaphoreType.DMA((size,))
            for size in (n, n, 1, shares, shares, shares, shares, shares, shares, n, n)
            + (near, near, shares, shares, 1) * 2
        ],
        compiler_params=pltpu.CompilerParams(
            collective_id=2, has_side_effects=True, vmem_limit_bytes=62 * mebi
        ),
        name="mixer_back",
    )(sizes, images, cotangent, grad, branch, *lines, *norms, *sums)


def taps_kernel(small_ref, *refs):
    params, (*grads, rest_ref), wide = refs[:8], refs[8:17], refs[17]
    count = small_ref.shape[0]
    side = wide.shape[0]
    wide[...] = jnp.zeros_like(wide)
    turned = refs[18]

    def turn(at):
        wide[:count, :] = small_ref[:, at * side : (at + 1) * side]
        turned[...] = wide[...].T

    def rows_load(lag):
        return turned[pl.ds(lax.rem(lag + side - 1, side), 1), :count]

    def cols_load(lag):
        return turned[pl.ds(side - 1 - lag, 1), :count]

    for at, load in enumerate((rows_load, cols_load)):
        turn(at)
        found = taps_adjoint(*(ref[...] for ref in params[4 * at : 4 * at + 4]), side, load)
        for ref, grad in zip(grads[4 * at : 4 * at + 4], found):
            ref[...] = grad
    turn(2)
    rest_ref[...] = turned[:8, :count]


def taps_back(small, params, side):
    modes, count = params[0].shape
    full = functools.partial(jax.ShapeDtypeStruct, dtype=jnp.float32)
    vmem = pl.BlockSpec(memory_space=pltpu.VMEM)
    return pl.pallas_call(
        taps_kernel,
        out_shape=(full((modes, count)),) * 8 + (full((8, count)),),
        in_specs=[vmem] * 9,
        out_specs=(vmem,) * 9,
        scratch_shapes=[pltpu.VMEM((side, side), jnp.float32), pltpu.VMEM((side, side), jnp.float32)],
        name="taps_back",
    )(small, *params)


def pixel_body(
    n,
    images,
    cotangent,
    image_sizes,
    slot_image,
    rows_rate,
    rows_freq,
    rows_real,
    rows_imag,
    cols_rate,
    cols_freq,
    cols_real,
    cols_imag,
    skip_gain,
    norm_gain,
    norm_bias,
    weight_in,
    bias_in,
    weight_out,
    bias_out,
    layer_scale,
):
    _, count, side, _ = images.shape
    channels = norm_gain.shape[0]
    picked = slot_image[lax.axis_index("dp")]
    sizes = image_sizes[picked]
    image, cot = images[0], cotangent[0]

    params = tuple(
        param.T
        for param in (
            rows_rate,
            rows_freq,
            rows_real,
            rows_imag,
            cols_rate,
            cols_freq,
            cols_real,
            cols_imag,
        )
    )
    skip_wide = jnp.broadcast_to(skip_gain[:, None], (count, side))
    scale_wide = jnp.broadcast_to(layer_scale[:, None], (count, side))
    bias_wide = jnp.broadcast_to(bias_out[:, None], (count, side))

    shares = lax.axis_size("dp")
    hidden = weight_out.shape[0]
    spread = jnp.broadcast_to(bias_in[:, None], (hidden, side))
    in_part = jnp.concatenate([weight_in.T, spread], axis=1).reshape(shares, -1, channels + side)
    out_part = weight_out.reshape(shares, -1, channels)
    mixed, back, in_whole, out_whole, bias_out_sums, rows_back, rows, cols_back, _ = mixer_forward(
        n, shares, sizes, image, cot, params, skip_wide, scale_wide, in_part, out_part
    )
    grad, branch, _, _, *sums, gain_sums, shift_sums = mlp(
        n,
        shares,
        mixed,
        back,
        in_whole.reshape(-1, channels + side),
        out_whole.reshape(-1, channels),
        jnp.broadcast_to(norm_gain[:, None], (channels, side)),
        jnp.broadcast_to(norm_bias[:, None], (channels, side)),
    )
    output, input_grad, small, norms, out_final, in_final = mixer_back(
        n,
        shares,
        sizes,
        image,
        cot,
        grad.reshape(side, count, side),
        branch,
        (rows_back, rows, cols_back, skip_wide, scale_wide, bias_wide),
        (bias_out_sums, gain_sums, shift_sums),
        sums,
    )
    *params_grad, rest = taps_back(small, params, side)
    in_final = in_final.reshape(hidden, channels + side)
    return (
        output[None],
        input_grad[None],
        *(grad.T for grad in params_grad),
        rest[0],
        norms[0],
        norms[1],
        in_final[:, :channels].T,
        jnp.sum(in_final[:, channels:], axis=1),
        out_final.reshape(hidden, channels),
        rest[1],
        rest[2],
    )


def choose_body(n, images, *rest):
    slots, count, side, _ = images.shape
    fits = (
        slots == 1
        and side == 128
        and count <= side
        and count % GROUP == 0
        and side % (n * LINES) == 0
        and n % 2 == 0
        and (rest[15].shape[0] * n) % (2 * STEP_HIDDEN) == 0
        and rest[15].shape[0] % (16 * lax.axis_size("dp")) == 0
    )
    return pixel_body(n, images, *rest) if fits else plain_body(images, *rest)


def solution(mesh):
    in_specs = (
        P("dp", "chan", None, None),
        P("dp", "chan", None, None),
        P(),
        P(),
        P("chan", None),
        P("chan", None),
        P("chan", None),
        P("chan", None),
        P("chan", None),
        P("chan", None),
        P("chan", None),
        P("chan", None),
        P("chan"),
        P(),
        P(),
        P(None, "chan"),
        P("chan"),
        P("chan", None),
        P("chan"),
        P("chan"),
    )
    out_specs = (
        P("dp", "chan", None, None),
        P("dp", "chan", None, None),
        P("chan", None),
        P("chan", None),
        P("chan", None),
        P("chan", None),
        P("chan", None),
        P("chan", None),
        P("chan", None),
        P("chan", None),
        P("chan"),
        P(),
        P(),
        P(None, "chan"),
        P("chan"),
        P("chan", None),
        P("chan"),
        P("chan"),
    )
    return jax.shard_map(functools.partial(choose_body, mesh.shape["chan"]), mesh=mesh, in_specs=in_specs, out_specs=out_specs, check_vma=False)
```

```python
import functools

import jax
import jax.numpy as jnp
from jax import lax
from jax.experimental import pallas as pl
from jax.experimental.pallas import tpu as pltpu
from jax.sharding import PartitionSpec as P

eps_norm = 1e-06
highest = lax.Precision.HIGHEST


def kernel_taps(rate_vals, freq_vals, real_part, imag_part, length):
    offsets = jnp.arange(length, dtype=jnp.float32)
    decays = jnp.exp(-rate_vals[:, :, None] * offsets)
    angles = freq_vals[:, :, None] * offsets
    return jnp.sum(
        decays
        * (real_part[:, :, None] * jnp.cos(angles) - imag_part[:, :, None] * jnp.sin(angles)),
        axis=1,
    )


def toeplitz(filter_taps):
    length = filter_taps.shape[1]
    offsets = jnp.arange(length, dtype=jnp.int32)
    lag_index = offsets[:, None] - offsets[None, :]
    return jnp.where(lag_index[None] >= 0, filter_taps[:, jnp.maximum(lag_index, 0)], 0.0)


def mixer(
    masked_in,
    rows_rate,
    rows_freq,
    rows_real,
    rows_imag,
    cols_rate,
    cols_freq,
    cols_real,
    cols_imag,
    skip_gain,
):
    rows_op = toeplitz(kernel_taps(rows_rate, rows_freq, rows_real, rows_imag, masked_in.shape[2]))
    cols_op = toeplitz(kernel_taps(cols_rate, cols_freq, cols_real, cols_imag, masked_in.shape[3]))
    along_rows = jnp.einsum("chi,ncij->nchj", rows_op, masked_in, precision=highest)
    return (
        jnp.einsum("nchj,cwj->nchw", along_rows, cols_op, precision=highest)
        + skip_gain[None, :, None, None] * masked_in
    )


def normalize(values, norm_gain, norm_bias):
    center = values - jnp.mean(values, axis=-2, keepdims=True)
    inverse = lax.rsqrt(jnp.mean(center * center, axis=-2, keepdims=True) + eps_norm)
    scaled = center * inverse
    return (scaled * norm_gain[:, None] + norm_bias[:, None], scaled, inverse)


def gelu_exact(values):
    return jax.nn.gelu(values, approximate=False)


def plain_body(
    images,
    cotangent,
    image_sizes,
    slot_image,
    rows_rate,
    rows_freq,
    rows_real,
    rows_imag,
    cols_rate,
    cols_freq,
    cols_real,
    cols_imag,
    skip_gain,
    norm_gain,
    norm_bias,
    weight_in,
    bias_in,
    weight_out,
    bias_out,
    layer_scale,
):
    slot_count, chan_count, length = (images.shape[0], images.shape[1], images.shape[2])
    pixels = length * length
    image_count = slot_image.shape[0]
    slot_ids = lax.axis_index("dp") * slot_count + jnp.arange(slot_count, dtype=jnp.int32)
    choose = (slot_ids[:, None] == jnp.arange(image_count, dtype=jnp.int32)[None, :]).astype(
        jnp.int32
    )
    picked = jnp.sum(choose * slot_image[None, :], axis=1)
    owners = (picked[:, None] == jnp.arange(image_count, dtype=jnp.int32)[None, :]).astype(
        jnp.int32
    )
    heights = jnp.sum(owners * image_sizes[None, :, 0], axis=1)
    widths = jnp.sum(owners * image_sizes[None, :, 1], axis=1)
    offsets = jnp.arange(length, dtype=jnp.int32)
    inside = (
        (offsets[None, :, None] < heights[:, None, None])
        & (offsets[None, None, :] < widths[:, None, None])
    ).astype(jnp.float32)
    masked_in = images.astype(jnp.float32) * inside[:, None]
    mixed_out, mixer_pull = jax.vjp(
        mixer,
        masked_in,
        rows_rate,
        rows_freq,
        rows_real,
        rows_imag,
        cols_rate,
        cols_freq,
        cols_real,
        cols_imag,
        skip_gain,
    )
    mixed_low = mixed_out.astype(jnp.bfloat16).reshape(slot_count, chan_count, pixels)
    mask_flat = inside.reshape(slot_count, 1, pixels)
    residual = images.astype(jnp.float32).reshape(slot_count, chan_count, pixels)
    grad_out = cotangent.astype(jnp.float32).reshape(slot_count, chan_count, pixels) * mask_flat
    chan_offset = lax.axis_index("chan") * chan_count
    all_channels = norm_gain.shape[0]
    slot_item = 0
    gathered = lax.all_gather(mixed_low[slot_item], "chan", axis=0, tiled=True)
    normed, scaled, inverse = normalize(gathered.astype(jnp.float32), norm_gain, norm_bias)
    normed_low = normed.astype(jnp.bfloat16)
    before = (
        jnp.einsum("cf,cp->fp", weight_in, normed_low, preferred_element_type=jnp.float32)
        + bias_in.astype(jnp.float32)[:, None]
    )
    active = gelu_exact(before).astype(jnp.bfloat16)

    def project(first_row, row_count, active=active):
        return jnp.einsum("fc,fp->cp", weight_out, active, preferred_element_type=jnp.float32)

    branch_list = [
        lax.psum_scatter(
            project(jnp.int32(0), chan_count * lax.axis_size("chan")),
            "chan",
            scatter_dimension=0,
            tiled=True,
        )
    ]
    scaled_part = lax.dynamic_slice_in_dim(scaled, chan_offset, chan_count, 0)
    stored = [(normed_low, before, active, scaled_part, inverse)]
    branch_all = jnp.stack(branch_list)
    shifted = branch_all + bias_out[None, :, None]
    output = (
        (mask_flat * (residual + layer_scale[None, :, None] * shifted))
        .astype(jnp.bfloat16)
        .reshape(images.shape)
    )
    scale_grad = jnp.sum(grad_out * shifted, axis=(0, 2))
    branch_grad = layer_scale[None, :, None] * grad_out
    bias_out_grad = jnp.sum(branch_grad, axis=(0, 2))
    branch_low = branch_grad.astype(jnp.bfloat16)
    hidden_count = weight_in.shape[1]
    out_weight_grad = jnp.zeros((hidden_count, all_channels), jnp.float32)
    gain_shard = lax.dynamic_slice_in_dim(norm_gain, chan_offset, chan_count, 0)
    slot_item = 0
    normed_low, before, active, scaled_part, inverse = stored[slot_item]

    def absorb(totals, shard_rows, first_row, active=active):
        hidden_grad = jnp.einsum(
            "fc,cp->fp", weight_out, shard_rows, preferred_element_type=jnp.float32
        )
        product_part = jnp.einsum(
            "fp,cp->fc", active, shard_rows, preferred_element_type=jnp.float32
        )
        return (hidden_grad, product_part)

    hidden_start = jnp.zeros((hidden_count, pixels), jnp.float32)
    hidden_grad, out_weight_grad = absorb(
        (hidden_start, out_weight_grad),
        lax.all_gather(branch_low[slot_item], "chan", axis=0, tiled=True),
        jnp.int32(0),
    )
    gelu_pull = jax.vjp(gelu_exact, before)[1]
    before_grad = gelu_pull(hidden_grad)[0].astype(jnp.bfloat16)
    in_weight_grad = jnp.einsum(
        "cp,fp->cf", normed_low, before_grad, preferred_element_type=jnp.float32
    )
    in_bias_grad = jnp.sum(before_grad.astype(jnp.float32), axis=1)

    def spread_back(first_row, row_count, before_grad=before_grad):
        return jnp.einsum("cf,fp->cp", weight_in, before_grad, preferred_element_type=jnp.float32)

    normed_grad = lax.psum_scatter(
        spread_back(jnp.int32(0), chan_count * lax.axis_size("chan")),
        "chan",
        scatter_dimension=0,
        tiled=True,
    )
    weighted = normed_grad * gain_shard[:, None]
    pixel_sums = (
        lax.psum(jnp.sum(weighted, axis=0).astype(jnp.bfloat16), "chan").astype(jnp.float32),
        lax.psum(jnp.sum(weighted * scaled_part, axis=0).astype(jnp.bfloat16), "chan").astype(
            jnp.float32
        ),
    )
    mixed_grads = [
        inverse
        * (
            weighted
            - pixel_sums[0][None, :] / all_channels
            - scaled_part * pixel_sums[1][None, :] / all_channels
        )
    ]
    gain_part = jnp.sum(normed_grad * scaled_part, axis=1)
    shift_part = jnp.sum(normed_grad, axis=1)
    mixed_grad_all = jnp.stack(mixed_grads)
    gain_grad = lax.dynamic_update_slice_in_dim(
        jnp.zeros((all_channels,), jnp.float32), gain_part, chan_offset, 0
    )
    shift_grad = lax.dynamic_update_slice_in_dim(
        jnp.zeros((all_channels,), jnp.float32), shift_part, chan_offset, 0
    )
    pulled = mixer_pull(mixed_grad_all.reshape(images.shape))
    input_grad = inside[:, None] * (cotangent.astype(jnp.float32) + pulled[0])
    summed = lax.psum(
        (
            in_weight_grad,
            out_weight_grad,
            in_bias_grad,
            bias_out_grad,
            scale_grad,
            pulled[1],
            pulled[2],
            pulled[3],
            pulled[4],
            pulled[5],
            pulled[6],
            pulled[7],
            pulled[8],
            pulled[9],
        ),
        "dp",
    )
    norm_sums = lax.psum((gain_grad, shift_grad), ("dp", "chan"))
    return (
        output,
        input_grad,
        summed[5],
        summed[6],
        summed[7],
        summed[8],
        summed[9],
        summed[10],
        summed[11],
        summed[12],
        summed[13],
        norm_sums[0],
        norm_sums[1],
        summed[0],
        summed[2],
        summed[1],
        summed[3],
        summed[4],
    )


MESH = pl.DeviceIdType.MESH
GROUP = 16
ABREAST = 2
LINES = 4
STEP_HIDDEN = 512
mebi = 1024 * 1024


def dot_nn(left, right):
    return lax.dot_general(left, right, (((1,), (0,)), ((), ())), preferred_element_type=jnp.float32)


def dot_nt(left, right):
    return lax.dot_general(left, right, (((1,), (1,)), ((), ())), preferred_element_type=jnp.float32)


def dot_tn(left, right):
    return lax.dot_general(left, right, (((0,), (0,)), ((), ())), preferred_element_type=jnp.float32)


def split_low(values):
    high = values.astype(jnp.bfloat16)
    return high, (values - high.astype(jnp.float32)).astype(jnp.bfloat16)


def lag_matrix(line, side, keep):
    spread = pltpu.roll(jnp.broadcast_to(line, (side, side)), 0, 1, stride=1, stride_axis=0)
    return jnp.where(keep, spread, 0.0)


def lag_sums(matrix, side, keep):
    turned = pltpu.roll(jnp.where(keep, matrix, 0.0), 0, 1, stride=1, stride_axis=0)
    return jnp.sum(turned, axis=0, keepdims=True)


cos_terms = (
    1.0, -19.7392087, 64.9393891, -85.4566583, 60.242131, -26.4046662, 7.8001253, -1.45310477
)
sin_terms = (6.2831853, -41.3417004, 81.6051314, -76.703015, 42.0259236, -14.8998335, 3.23811835)


def polynomial(terms, at):
    value = terms[-1]
    for term in terms[-2::-1]:
        value = value * at + term
    return value


TILE = 16


def power(rate, freq, lag):
    angle = freq * 0.15915494309189535 * lag
    angle = angle - jnp.floor(angle + 0.5)
    square = angle * angle
    decay = jnp.exp(-rate * lag)
    return decay * polynomial(cos_terms, square), decay * (angle * polynomial(sin_terms, square))


def product(left, right):
    return left[0] * right[0] - left[1] * right[1], left[0] * right[1] + left[1] * right[0]


def taps_lines(rate, freq, real, imag, side, store):
    first = power(rate, freq, 1.0)

    @pl.loop(0, side // TILE)
    def _(tile):
        state = product((real, imag), power(rate, freq, (tile * TILE).astype(jnp.float32)))
        for step in range(TILE):
            store(tile * TILE + step, jnp.sum(state[0], axis=0, keepdims=True))
            state = product(state, first)


def taps_adjoint(rate, freq, real, imag, side, load):
    first = power(rate, freq, 1.0)

    def tile_sums(tile, totals):
        state = power(rate, freq, (tile * TILE).astype(jnp.float32))
        even, odd, even_lag, odd_lag = totals
        for step in range(TILE):
            grad = load(tile * TILE + step)
            late = grad * (tile * TILE + step).astype(jnp.float32)
            even = even + grad * state[0]
            odd = odd + grad * state[1]
            even_lag = even_lag + late * state[0]
            odd_lag = odd_lag + late * state[1]
            state = product(state, first)
        return even, odd, even_lag, odd_lag

    zero = jnp.zeros_like(rate)
    even, odd, even_lag, odd_lag = lax.fori_loop(0, side // TILE, tile_sums, (zero,) * 4)
    return imag * odd_lag - real * even_lag, -real * odd_lag - imag * even_lag, even, -odd


def lane_sums(values):
    ones = jnp.ones((8, values.shape[1]), jnp.bfloat16)
    high, rest = split_low(values)
    low = (values - high.astype(jnp.float32) - rest.astype(jnp.float32)).astype(jnp.bfloat16)
    return dot_nt(ones, high) + dot_nt(ones, rest) + dot_nt(ones, low)


def meet(n, shares):
    me, share = lax.axis_index("chan"), lax.axis_index("dp")
    barrier = pltpu.get_barrier_semaphore()
    for shift in range(1, n):
        pl.semaphore_signal(
            barrier, inc=1, device_id={"chan": lax.rem(me + shift, n)}, device_id_type=MESH
        )
    for shift in range(1, shares):
        pl.semaphore_signal(
            barrier, inc=1, device_id={"dp": lax.rem(share + shift, shares)}, device_id_type=MESH
        )
    pl.semaphore_wait(barrier, n + shares - 2)
    return me, share


def push(source, target, send_sem, recv_sem, **peer):
    return pltpu.make_async_remote_copy(
        src_ref=source,
        dst_ref=target,
        send_sem=send_sem,
        recv_sem=recv_sem,
        device_id=peer,
        device_id_type=MESH,
    )


def weight_rounds(n, shares, me, share, pairs, sems):
    near, far = n // 2, me // 2
    core = lax.rem(me, 2)
    own_sem, send1, recv1, send2, recv2, send3, recv3 = sems

    def own(at):
        local, whole = pairs[at]
        return pltpu.make_async_copy(local, whole.at[core, :, far], own_sem.at[at])

    def first(at, shift, back=False):
        local, whole = pairs[at]
        origin = lax.rem(far + near - shift, near) if back else far
        return push(
            local.at[share],
            whole.at[core, share, origin],
            send1.at[at, shift],
            recv1.at[at, shift],
            chan=lax.rem(far + shift, near) * 2 + core,
        )

    def second(at, shift, turn, back=False):
        whole = pairs[at][1]
        origin = lax.rem(far + near - shift, near)
        holder = lax.rem(share + shares - turn, shares) if back else share
        return push(
            whole.at[core, share, origin],
            whole.at[core, holder, origin],
            send2.at[at, shift, turn],
            recv2.at[at, shift, turn],
            dp=lax.rem(share + turn, shares),
        )

    def third(at, back=False):
        whole = pairs[at][1]
        return push(
            whole.at[core], whole.at[1 - core if back else core], send3.at[at], recv3.at[at], chan=far * 2 + 1 - core
        )

    both = range(len(pairs))

    def start_first():
        for at in both:
            own(at).start()
            for shift in range(1, near):
                first(at, shift).start()

    def start_second():
        for at in both:
            for shift in range(1, near):
                first(at, shift, True).wait_recv()
                for turn in range(1, shares):
                    second(at, shift, turn).start()

    def start_third():
        for at in both:
            own(at).wait()
            for shift in range(1, near):
                for turn in range(1, shares):
                    second(at, shift, turn, True).wait_recv()
            third(at).start()

    def finish():
        for at in both:
            third(at, True).wait_recv()
            third(at).wait_send()
            for shift in range(1, near):
                first(at, shift).wait_send()
                for turn in range(1, shares):
                    second(at, shift, turn).wait_send()

    return start_first, start_second, start_third, finish


def send_part(stage, target, me, peer, part, send_sem, recv_sem, shift):
    return pltpu.make_async_remote_copy(
        src_ref=stage.at[peer, part],
        dst_ref=target.at[me, part],
        send_sem=send_sem.at[shift],
        recv_sem=recv_sem.at[shift],
        device_id={"chan": peer},
        device_id_type=MESH,
    )


def wait_parts(stage, target, me, n, send_sem, recv_sem):
    for shift in range(1, n):
        peer = lax.rem(me + shift, n)
        origin = lax.rem(me + n - shift, n)
        pltpu.make_async_remote_copy(
            src_ref=stage.at[peer],
            dst_ref=target.at[origin],
            send_sem=send_sem.at[shift],
            recv_sem=recv_sem.at[shift],
            device_id={"chan": peer},
            device_id_type=MESH,
        ).wait()


def mixer_kernel(
    n,
    shares,
    sizes_ref,
    image_ref,
    cot_ref,
    skip_ref,
    scale_ref,
    *rest,
):
    mixer_body(n, shares, sizes_ref, image_ref, cot_ref, skip_ref, scale_ref, rest[:8], *rest[8:])


def mixer_body(
    n,
    shares,
    sizes_ref,
    image_ref,
    cot_ref,
    skip_ref,
    scale_ref,
    param_refs,
    in_part_ref,
    out_part_ref,
    mixed_ref,
    first_ref,
    back_ref,
    in_whole_ref,
    out_whole_ref,
    sums_ref,
    rows_back_ref,
    rows_ref,
    cols_back_ref,
    cols_ref,
    mixed_stage,
    back_stage,
    wide,
    taps,
    params_got,
    params_sem,
    send_m,
    recv_m,
    send_b,
    recv_b,
    own_sem,
    keep_sem,
    *weight_sems,
):
    count, side, _ = image_ref.shape
    parts = count // GROUP
    block = side // n
    me, share = meet(n, shares)
    start_first, start_second, start_third, finish = weight_rounds(
        n, shares, me, share, ((in_part_ref, in_whole_ref), (out_part_ref, out_whole_ref)), weight_sems
    )
    start_first()
    param_copies = [
        pltpu.make_async_copy(ref, params_got.at[at], params_sem.at[at]) for at, ref in enumerate(param_refs)
    ]
    for copy in param_copies:
        copy.start()
    taps[...] = jnp.zeros_like(taps)
    row_at = lax.broadcasted_iota(jnp.int32, (side, side), 0)
    col_at = lax.broadcasted_iota(jnp.int32, (side, side), 1)
    inside = (row_at < sizes_ref[0]) & (col_at < sizes_ref[1])
    lower = row_at >= col_at
    upper = row_at <= col_at

    def turn(stage, part):
        @pl.loop(0, n)
        def _(owner):
            for line in range(block):
                tile = wide[pl.ds(owner * block + line, GROUP, stride=side), :]
                stage[owner, part, line] = tile.astype(jnp.bfloat16)

    def send(stage, target, part, send_sem, recv_sem):
        for shift in range(1, n):
            send_part(stage, target, me, lax.rem(me + shift, n), part, send_sem, recv_sem, shift).start()

    def own_back(part):
        return pltpu.make_async_copy(back_stage.at[:, part], back_ref.at[:, part], keep_sem.at[part])

    def first_push(shift, back=False):
        peer = lax.rem(me + shift, n)
        return push(
            back_stage.at[peer, :, pl.ds(0, LINES)],
            first_ref.at[lax.rem(me + n - shift, n) if back else me],
            send_b.at[shift],
            recv_b.at[shift],
            chan=peer,
        )

    for copy in param_copies:
        copy.wait()
    for axis, (back_out, out) in enumerate(((rows_back_ref, rows_ref), (cols_back_ref, cols_ref))):

        def store(lag, line):
            taps[0, pl.ds(lax.rem(side - lag, side), 1), :count] = line
            taps[1, pl.ds(lag, 1), :count] = line

        taps_lines(*(params_got[4 * axis + at] for at in range(4)), side, store)
        back_out[...] = taps[0].T[:count]
        out[...] = taps[1].T[:count]


    @pl.loop(0, parts)
    def _(part):
        pl.when(part == parts // 2)(start_second)

        def one_channel(item):
            chan = part * GROUP + item
            masked = jnp.where(inside, image_ref[chan].astype(jnp.float32), 0.0)
            masked_low = masked.astype(jnp.bfloat16)
            rows_high, rows_low = split_low(lag_matrix(rows_back_ref[pl.ds(chan, 1), :], side, lower))
            cols_high, cols_low = split_low(lag_matrix(cols_ref[pl.ds(chan, 1), :], side, upper))
            along = dot_nn(
                jnp.concatenate([rows_high, rows_low], axis=1),
                jnp.concatenate([masked_low, masked_low], axis=0),
            )
            along_high, along_low = split_low(along)
            mixed = dot_nn(
                jnp.concatenate([along_high, along_low], axis=1),
                jnp.concatenate([cols_high, cols_high], axis=0),
            ) + dot_nn(along_high, cols_low)
            mixed = mixed + skip_ref[chan] * masked
            wide[pl.ds(pl.multiple_of(item * side, side), side), :] = mixed

        @pl.loop(0, GROUP // ABREAST)
        def _(few):
            for at in range(ABREAST):
                one_channel(few * ABREAST + at)

        turn(mixed_stage, part)
        send(mixed_stage, mixed_ref, part, send_m, recv_m)

    @pl.loop(0, parts)
    def _(part):
        @pl.loop(0, GROUP)
        def _(item):
            chan = part * GROUP + item
            grad_out = jnp.where(inside, cot_ref[chan].astype(jnp.float32), 0.0)
            scaled = grad_out * scale_ref[chan]
            sums_ref[pl.ds(chan, 1), :] = jnp.sum(scaled, axis=0, keepdims=True)
            wide[pl.ds(pl.multiple_of(item * side, side), side), :] = scaled

        turn(back_stage, part)
        own_back(part).start()

    for shift in range(1, n):
        first_push(shift).start()
    own_b = pltpu.make_async_copy(back_stage.at[me, :, pl.ds(0, LINES)], first_ref.at[me], own_sem.at[0])
    own_m = pltpu.make_async_copy(mixed_stage.at[me], mixed_ref.at[me], own_sem.at[1])
    own_b.start()
    own_m.start()
    start_third()
    for part in range(parts):
        own_back(part).wait()
    own_b.wait()
    own_m.wait()
    wait_parts(mixed_stage, mixed_ref, me, n, send_m, recv_m)
    for shift in range(1, n):
        first_push(shift, True).wait_recv()
        first_push(shift).wait_send()
    finish()


def mixer_forward(n, shares, sizes, images, cotangent, skip, scale, params, in_part, out_part):
    near = n // 2
    smem = pl.BlockSpec(memory_space=pltpu.SMEM)
    count, side, _ = images.shape
    line = jax.ShapeDtypeStruct((count, side), jnp.float32)
    shape = (n, count // GROUP, side // n, GROUP, side)
    first_shape = (n, count // GROUP, LINES, GROUP, side)
    vmem = pl.BlockSpec(memory_space=pltpu.VMEM)
    hbm = pl.BlockSpec(memory_space=pl.ANY)
    return pl.pallas_call(
        functools.partial(mixer_kernel, n, shares),
        out_shape=(
            jax.ShapeDtypeStruct(shape, jnp.bfloat16),
            jax.ShapeDtypeStruct(first_shape, jnp.bfloat16),
            jax.ShapeDtypeStruct(shape, jnp.bfloat16),
        )
        + tuple(
            jax.ShapeDtypeStruct((2, shares, near, *part.shape[1:]), jnp.bfloat16)
            for part in (in_part, out_part)
        )
        + (line,) * 5,
        in_specs=[smem] + [vmem] * 2 + [smem] * 2 + [hbm] * 10,
        out_specs=(hbm,) * 5 + (vmem,) * 5,
        scratch_shapes=[
            pltpu.VMEM(shape, jnp.bfloat16),
            pltpu.VMEM(shape, jnp.bfloat16),
            pltpu.VMEM((GROUP * side, side), jnp.float32),
            pltpu.VMEM((2, side, side), jnp.float32),
            pltpu.VMEM((8, *params[0].shape), jnp.float32),
            pltpu.SemaphoreType.DMA((8,)),
            pltpu.SemaphoreType.DMA((n,)),
            pltpu.SemaphoreType.DMA((n,)),
            pltpu.SemaphoreType.DMA((n,)),
            pltpu.SemaphoreType.DMA((n,)),
            pltpu.SemaphoreType.DMA((2,)),
            pltpu.SemaphoreType.DMA((count // GROUP,)),
            pltpu.SemaphoreType.DMA((2,)),
            pltpu.SemaphoreType.DMA((2, near)),
            pltpu.SemaphoreType.DMA((2, near)),
            pltpu.SemaphoreType.DMA((2, near, shares)),
            pltpu.SemaphoreType.DMA((2, near, shares)),
            pltpu.SemaphoreType.DMA((2,)),
            pltpu.SemaphoreType.DMA((2,)),
        ],
        compiler_params=pltpu.CompilerParams(
            collective_id=0, has_side_effects=True, vmem_limit_bytes=40 * mebi
        ),
        name="mixer_forward",
    )(sizes, images, cotangent, skip, scale, *params, in_part, out_part)


def gelu_parts(value):
    bell = jnp.exp(-0.5 * value * value)
    inner = 1.0 / (1.0 + (0.3275911 * 0.7071067811865476) * jnp.abs(value))
    series = 1.061405429 * inner - 1.453152027
    series = series * inner + 1.421413741
    series = series * inner - 0.284496736
    series = series * inner + 0.254829592
    tail = (0.5 * inner) * series * bell
    return jnp.where(value < 0.0, tail, 1.0 - tail), bell * 0.3989422804014327


def mlp_kernel(
    n,
    shares,
    mixed_ref,
    first_ref,
    in_ref,
    out_ref,
    gain_ref,
    shift_ref,
    back_ref,
    grad_ref,
    branch_sent_ref,
    branch_ref,
    active_ref,
    before_grad_ref,
    out_take_ref,
    in_half_ref,
    gain_grad_ref,
    shift_grad_ref,
    grad_stage,
    branch_stage,
    active_ring,
    before_ring,
    normed_keep,
    cots_keep,
    scaled_keep,
    inverse_keep,
    branch_sum,
    grad_sum,
    hidden_sum,
    pieces,
    rows_stage,
    out_got,
    in_got,
    back_got,
    send_g,
    recv_g,
    send_c,
    recv_c,
    send_r,
    recv_r,
    own_sem,
    ring_sem,
    piece_sem,
    send_h,
    recv_h,
    send_2,
    recv_2,
):
    side = mixed_ref.shape[-1]
    groups = mixed_ref.shape[1]
    block = mixed_ref.shape[2]
    hidden, channels = out_ref.shape
    local = channels // n
    steps = block // LINES
    width = LINES * side
    parts = hidden // STEP_HIDDEN
    ring = active_ring.shape[0]
    me, share = meet(n, shares)
    core = lax.rem(me, 2)
    sibling = me + 1 - 2 * core
    early = branch_sent_ref.shape[1]

    def cot_push(step, shift, back=False):
        peer = lax.rem(me + shift, n)
        origin = lax.rem(me + n - shift, n) if back else me
        span = pl.ds(step * LINES, LINES)
        return push(
            back_ref.at[peer, :, span],
            back_got.at[origin, :, span],
            send_c.at[step, shift],
            recv_c.at[step, shift],
            chan=peer,
        )

    def branch_push(shift, back=False):
        peer = lax.rem(me + shift, n)
        return push(
            branch_stage.at[peer, pl.ds(0, early)],
            branch_sent_ref.at[lax.rem(me + n - shift, n) if back else me],
            send_r.at[shift],
            recv_r.at[shift],
            chan=peer,
        )

    for step in range(1, steps):
        for shift in range(1, n):
            cot_push(step, shift).start()
    own_c = pltpu.make_async_copy(back_ref.at[me], back_got.at[me], own_sem.at[2])
    own_c.start()
    gain_grad_ref[...] = jnp.zeros_like(gain_grad_ref)
    shift_grad_ref[...] = jnp.zeros_like(shift_grad_ref)
    hidden_sum[...] = jnp.zeros_like(hidden_sum)

    def keeps(turn):
        slot = lax.rem(turn, ring)
        span = pl.ds(pl.multiple_of(lax.rem(turn, parts) * STEP_HIDDEN, STEP_HIDDEN), STEP_HIDDEN)
        return [
            pltpu.make_async_copy(kept.at[slot], whole.at[turn // parts, span], ring_sem.at[at, slot])
            for at, (kept, whole) in enumerate(((active_ring, active_ref), (before_ring, before_grad_ref)))
        ]

    @pl.loop(0, steps)
    def _(step):
        pl.when(step == 1)(own_c.wait)

        @pl.when(step > 0)
        def _():
            for shift in range(1, n):
                cot_push(step, shift, True).wait_recv()

        for line in range(LINES):
            row = step * LINES + line
            lanes = pl.ds(line * side, side)
            order = [(owner, group) for owner in range(n) for group in range(groups)]
            mixed = jnp.concatenate(
                [mixed_ref[owner, group, row].astype(jnp.float32) for owner, group in order], axis=0
            )
            mean = jnp.sum(mixed, axis=0, keepdims=True) * (1.0 / channels)
            center = mixed - mean
            var = jnp.sum(center * center, axis=0, keepdims=True) * (1.0 / channels)
            inverse = lax.rsqrt(var + eps_norm)
            scaled = center * inverse
            normed_keep[step, :, lanes] = (scaled * gain_ref[...] + shift_ref[...]).astype(jnp.bfloat16)
            scaled_keep[:, lanes] = scaled
            inverse_keep[:, lanes] = inverse

            @pl.when(step == 0)
            def _():
                cots_keep[step, :, lanes] = jnp.concatenate(
                    [first_ref[owner, group, line] for owner, group in order], axis=0
                )

            @pl.when(step > 0)
            def _():
                cots_keep[step, :, lanes] = jnp.concatenate(
                    [back_got[owner, group, row] for owner, group in order], axis=0
                )

        @pl.loop(0, parts)
        def _(part):
            turn = step * parts + part
            slot = lax.rem(turn, ring)

            @pl.when(turn >= ring)
            def _():
                for copy in keeps(turn - ring):
                    copy.wait()

            span = pl.ds(pl.multiple_of(part * STEP_HIDDEN, STEP_HIDDEN), STEP_HIDDEN)
            bias = in_ref[span, channels:].astype(jnp.float32)[:, :1]
            before = dot_nn(in_ref[span, :channels], normed_keep[step]) + bias
            inside, bell = gelu_parts(before)
            active = (before * inside).astype(jnp.bfloat16)
            active_grad = dot_nn(out_ref[span, :], cots_keep[step])
            before_grad = (active_grad * (inside + before * bell)).astype(jnp.bfloat16)
            active_ring[slot] = active
            before_ring[slot] = before_grad
            hidden_sum[span, :] += sum(
                before_grad[:, line * side : (line + 1) * side].astype(jnp.float32) for line in range(LINES)
            )
            branch = dot_tn(out_ref[span, :], active)
            grad = dot_tn(in_ref[span, :channels], before_grad)

            @pl.when(part == 0)
            def _():
                branch_sum[...] = branch
                grad_sum[...] = grad

            @pl.when(part > 0)
            def _():
                branch_sum[...] += branch
                grad_sum[...] += grad

            for copy in keeps(turn):
                copy.start()

        for line in range(LINES):
            lanes = pl.ds(line * side, side)
            grad = grad_sum[:, lanes]
            scaled = scaled_keep[:, lanes]
            gain_grad_ref[...] += grad * scaled
            shift_grad_ref[...] += grad
            weighted = grad * gain_ref[...]
            first = jnp.sum(weighted, axis=0, keepdims=True) * (1.0 / channels)
            second = jnp.sum(weighted * scaled, axis=0, keepdims=True) * (1.0 / channels)
            mixed_grad = (inverse_keep[:, lanes] * (weighted - first - scaled * second)).astype(jnp.bfloat16)
            branch = branch_sum[:, lanes].astype(jnp.bfloat16)
            for owner in range(n):
                grad_stage[owner, step, line] = mixed_grad[owner * local : (owner + 1) * local]
                branch_stage[owner, step, line] = branch[owner * local : (owner + 1) * local]

        for shift in range(1, n):
            send_part(grad_stage, grad_ref, me, lax.rem(me + shift, n), step, send_g, recv_g, shift).start()

    own_g = pltpu.make_async_copy(grad_stage.at[me], grad_ref.at[me], own_sem.at[0])
    own_r = pltpu.make_async_copy(branch_stage.at[:, pl.ds(early, steps - early)], branch_ref, own_sem.at[1])
    own_s = pltpu.make_async_copy(branch_stage.at[me, pl.ds(0, early)], branch_sent_ref.at[me], own_sem.at[3])
    for shift in range(1, n):
        branch_push(shift).start()
    own_g.start()
    own_r.start()
    own_s.start()
    turns = steps * parts
    for turn in range(turns - ring, turns):
        for copy in keeps(turn):
            copy.wait()

    block_rows = hidden // 2 // shares
    kinds = (
        (active_ref, cots_keep, out_got, out_take_ref),
        (before_grad_ref, normed_keep, in_got, in_half_ref),
    )

    def block_span(job, base=0):
        at = lax.rem(share + 1 + lax.rem(job, shares), shares)
        return pl.ds(pl.multiple_of(base + at * block_rows, block_rows), block_rows)

    def whole_span(job):
        owner = 1 - core if job < shares else core
        return block_span(job, owner * (hidden // 2))

    def fetch(kind, job, slot):
        return pltpu.make_async_copy(
            kinds[kind][0].at[:, whole_span(job)], pieces.at[slot], piece_sem.at[slot]
        )

    def give(kind, job):
        got = kinds[kind][2]
        return push(
            rows_stage.at[job, :, pl.ds(0, got.shape[1])],
            got.at[block_span(job)],
            send_h.at[kind, job],
            recv_h.at[kind, job],
            chan=sibling,
        )

    def second(kind, job):
        _, _, got, take = kinds[kind]
        turn = job + 1 - shares
        if kind == 1:
            at = lax.rem(share + turn, shares)
            return pltpu.make_async_copy(got.at[block_span(job)], take.at[at], send_2.at[1, turn - 1])
        if turn == shares:
            return pltpu.make_async_copy(got.at[block_span(job)], take.at[0], send_2.at[0, 0])
        return push(
            got.at[block_span(job)],
            take.at[turn],
            send_2.at[kind, turn],
            recv_2.at[kind, turn],
            dp=lax.rem(share + turn, shares),
        )

    jobs = [(kind, job) for kind in range(2) for job in range(2 * shares)]
    fetch(0, 0, 0).start()
    for at, (kind, job) in enumerate(jobs):
        slot = at % 2
        if at + 1 < len(jobs):
            fetch(*jobs[at + 1], (at + 1) % 2).start()
        fetch(kind, job, slot).wait()
        right, got = kinds[kind][1:3]
        total = dot_nt(
            jnp.concatenate([pieces[slot, step] for step in range(steps)], axis=1),
            jnp.concatenate([right[step] for step in range(steps)], axis=1),
        )
        if job < shares:
            rows_stage[job, :, :channels] = total.astype(jnp.bfloat16)
            if kind == 1:
                rows_stage[job, :, channels:] = hidden_sum[whole_span(job), :].astype(jnp.bfloat16)
            give(kind, job).start()
        else:
            give(kind, job - shares).wait()
            span = block_span(job)
            got[span, :channels] = (total + got[span, :channels].astype(jnp.float32)).astype(jnp.bfloat16)
            if kind == 1:
                got[span, channels:] = (
                    hidden_sum[whole_span(job), :] + got[span, channels:].astype(jnp.float32)
                ).astype(jnp.bfloat16)
            second(kind, job).start()
    for kind in range(2):
        for job in range(shares, 2 * shares):
            second(kind, job).wait()
    own_g.wait()
    own_r.wait()
    own_s.wait()
    wait_parts(grad_stage, grad_ref, me, n, send_g, recv_g)
    for shift in range(1, n):
        branch_push(shift, True).wait_recv()
        branch_push(shift).wait_send()
        for step in range(1, steps):
            cot_push(step, shift).wait_send()


def mlp(n, shares, mixed, first, back, in_full, out_full, gain, shift):
    _, groups, block, group, side = mixed.shape
    hidden, channels = out_full.shape
    local = channels // n
    steps = block // LINES
    width = LINES * side
    shape = (n, steps, LINES, local, side)
    ring = 4
    low = functools.partial(jax.ShapeDtypeStruct, dtype=jnp.bfloat16)
    vmem = pl.BlockSpec(memory_space=pltpu.VMEM)
    hbm = pl.BlockSpec(memory_space=pl.ANY)
    return pl.pallas_call(
        functools.partial(mlp_kernel, n, shares),
        out_shape=(
            low(shape),
            low((n, steps // 4, *shape[2:])),
            low((n, steps - steps // 4, *shape[2:])),
            low((steps, hidden, width)),
            low((steps, hidden, width)),
            low((shares, hidden // 2 // shares, channels)),
            low((shares, hidden // 2 // shares, channels + side)),
            jax.ShapeDtypeStruct((channels, side), jnp.float32),
            jax.ShapeDtypeStruct((channels, side), jnp.float32),
        ),
        in_specs=[vmem] * 6 + [hbm],
        out_specs=(hbm,) * 7 + (vmem, vmem),
        scratch_shapes=[
            pltpu.VMEM(shape, jnp.bfloat16),
            pltpu.VMEM(shape, jnp.bfloat16),
            pltpu.VMEM((ring, STEP_HIDDEN, width), jnp.bfloat16),
            pltpu.VMEM((ring, STEP_HIDDEN, width), jnp.bfloat16),
            pltpu.VMEM((steps, channels, width), jnp.bfloat16),
            pltpu.VMEM((steps, channels, width), jnp.bfloat16),
            pltpu.VMEM((channels, width), jnp.float32),
            pltpu.VMEM((1, width), jnp.float32),
            pltpu.VMEM((channels, width), jnp.float32),
            pltpu.VMEM((channels, width), jnp.float32),
            pltpu.VMEM((hidden, side), jnp.float32),
            pltpu.VMEM((2, steps, hidden // 2 // shares, width), jnp.bfloat16),
            pltpu.VMEM((shares, hidden // 2 // shares, channels + side), jnp.bfloat16),
            pltpu.VMEM((hidden // 2, channels), jnp.bfloat16),
            pltpu.VMEM((hidden // 2, channels + side), jnp.bfloat16),
            pltpu.VMEM(back.shape, jnp.bfloat16),
            pltpu.SemaphoreType.DMA((n,)),
            pltpu.SemaphoreType.DMA((n,)),
            pltpu.SemaphoreType.DMA((steps, n)),
            pltpu.SemaphoreType.DMA((steps, n)),
            pltpu.SemaphoreType.DMA((n,)),
            pltpu.SemaphoreType.DMA((n,)),
            pltpu.SemaphoreType.DMA((4,)),
            pltpu.SemaphoreType.DMA((2, ring)),
            pltpu.SemaphoreType.DMA((2,)),
            pltpu.SemaphoreType.DMA((2, shares)),
            pltpu.SemaphoreType.DMA((2, shares)),
            pltpu.SemaphoreType.DMA((2, shares)),
            pltpu.SemaphoreType.DMA((2, shares)),
        ],
        compiler_params=pltpu.CompilerParams(
            collective_id=1, has_side_effects=True, vmem_limit_bytes=63 * mebi
        ),
        name="mlp",
    )(mixed, first, in_full, out_full, gain, shift, back)


def sum_rounds(n, shares, me, share, part, final, stage3, take3, keep3, keep4, send3, recv3, send4, recv4, own_sem):
    near, far = n // 2, me // 2
    core = lax.rem(me, 2)

    def third(turn):
        peer = lax.rem(far + turn, near)
        return push(stage3.at[peer], take3.at[turn], send3.at[turn], recv3.at[turn], chan=peer * 2 + core)

    def fourth(turn, back=False):
        holder = lax.rem(share + shares - turn, shares) if back else share
        peer = lax.rem(share + turn, shares)
        return push(keep4, final.at[holder], send4.at[turn], recv4.at[turn], dp=peer)

    def mine():
        return pltpu.make_async_copy(keep4, final.at[share], own_sem.at[0])

    def start_third():
        for at in range(near):
            total = part(at)
            stage3[at] = total.astype(jnp.bfloat16)

            @pl.when(far == at)
            def _():
                keep3[...] = total

        for turn in range(1, near):
            third(turn).start()

    def start_fourth():
        for turn in range(1, near):
            third(turn).wait()
        total = keep3[...]
        for turn in range(1, near):
            total = total + take3[turn].astype(jnp.float32)
        keep4[...] = total.astype(jnp.bfloat16)
        mine().start()
        for turn in range(1, shares):
            fourth(turn).start()

    def finish():
        mine().wait()
        for turn in range(1, shares):
            fourth(turn, True).wait_recv()
            fourth(turn).wait_send()

    return start_third, start_fourth, finish


def back_kernel(
    n,
    shares,
    sizes_ref,
    image_ref,
    cot_ref,
    grad_ref,
    branch_sent_ref,
    branch_ref,
    rows_back_ref,
    rows_ref,
    cols_back_ref,
    skip_ref,
    scale_ref,
    bias_ref,
    bias_sums_ref,
    gain_sums_ref,
    shift_sums_ref,
    out_take_ref,
    in_half_ref,
    output_ref,
    input_grad_ref,
    small_ref,
    late_ref,
    norm_ref,
    out_final_ref,
    in_final_ref,
    wide,
    branch_got,
    rows_sums,
    cols_sums,
    skip_sums,
    scale_sums,
    small_own,
    small_got,
    late_own,
    late_got,
    norm_own,
    norm_near,
    norm_mid,
    norm_far,
    in_take,
    out_stage3,
    out_take3,
    out_keep3,
    out_keep4,
    in_stage3,
    in_take3,
    in_keep3,
    in_keep4,
    send_sem,
    recv_sem,
    own_sem,
    send_2,
    recv_2,
    send_s,
    recv_s,
    send_l,
    recv_l,
    send_n,
    recv_n,
    send_f,
    recv_f,
    *round_sems,
):
    count, side, _ = image_ref.shape
    late, lines = branch_ref.shape[1], branch_ref.shape[2]
    early = branch_sent_ref.shape[1]
    near = n // 2
    rows = in_keep3.shape[0]
    me, share = meet(n, shares)

    def summed(take):
        return lambda at: sum(take[turn, at * rows : (at + 1) * rows].astype(jnp.float32) for turn in range(shares))

    out_third, out_fourth, out_finish = sum_rounds(
        n, shares, me, share, summed(out_take_ref), out_final_ref, out_stage3, out_take3, out_keep3, out_keep4, *round_sems[:5]
    )
    in_third, in_fourth, in_finish = sum_rounds(
        n, shares, me, share, summed(in_take), in_final_ref, in_stage3, in_take3, in_keep3, in_keep4, *round_sems[5:]
    )

    def in_second(turn):
        peer = lax.rem(share + turn, shares)
        if turn == 0:
            return pltpu.make_async_copy(in_half_ref.at[peer], in_take.at[0], send_2.at[0])
        return push(in_half_ref.at[peer], in_take.at[turn], send_2.at[turn], recv_2.at[turn], dp=peer)

    def branch_push(step, shift, back=False):
        peer = lax.rem(me + shift, n)
        return push(
            branch_ref.at[peer, step],
            branch_got.at[lax.rem(me + n - shift, n) if back else me, step],
            send_sem.at[step, shift],
            recv_sem.at[step, shift],
            chan=peer,
        )

    def start_branch(step):
        for shift in range(1, n):
            branch_push(step, shift).start()

    def norm_first(turn):
        peer = lax.rem(share + turn, shares)
        return push(norm_own, norm_near.at[turn], send_n.at[turn], recv_n.at[turn], dp=peer)

    def norm_second(turn):
        peer = lax.rem(me + turn, n)
        return push(norm_mid, norm_far.at[turn], send_f.at[turn], recv_f.at[turn], chan=peer)

    def small_push(turn):
        peer = lax.rem(share + turn, shares)
        return push(small_own, small_got.at[turn], send_s.at[turn], recv_s.at[turn], dp=peer)

    def late_push(turn):
        peer = lax.rem(share + turn, shares)
        return push(late_own, late_got.at[turn], send_l.at[turn], recv_l.at[turn], dp=peer)

    def norm_pass():
        total = norm_own[...]
        for turn in range(1, shares):
            norm_first(turn).wait()
            total = total + norm_near[turn]
        norm_mid[...] = total
        for turn in range(1, n):
            norm_second(turn).start()

    def in_pass():
        for turn in range(shares):
            in_second(turn).wait()
        in_third()
        for step in range(1, late):
            start_branch(step)

    top = lax.broadcasted_iota(jnp.int32, norm_own.shape, 0) == 0
    norm_own[...] = jnp.where(top, lane_sums(gain_sums_ref[...]), lane_sums(shift_sums_ref[...]))
    for turn in range(1, shares):
        norm_first(turn).start()
    for turn in range(shares):
        in_second(turn).start()
    out_third()
    start_branch(0)
    own = pltpu.make_async_copy(branch_ref.at[me], branch_got.at[me], own_sem.at[0])
    own.start()
    row_at = lax.broadcasted_iota(jnp.int32, (side, side), 0)
    col_at = lax.broadcasted_iota(jnp.int32, (side, side), 1)
    inside = (row_at < sizes_ref[0]) & (col_at < sizes_ref[1])
    lower = row_at >= col_at
    upper = row_at <= col_at
    flip = (row_at + col_at == side - 1).astype(jnp.bfloat16)

    @pl.loop(0, side)
    def _(row):
        span = pl.ds(pl.multiple_of(row * count, count), count)
        wide[span, :] = grad_ref[row].astype(jnp.float32)

    def one_channel(chan):
        one = pl.ds(chan, 1)
        grad = wide[pl.ds(chan, side, stride=count), :]
        image = image_ref[chan].astype(jnp.float32)
        grad_out = jnp.where(inside, cot_ref[chan].astype(jnp.float32), 0.0)
        masked = jnp.where(inside, image, 0.0)
        skip_sums[one, :] = jnp.sum(grad * masked, axis=0, keepdims=True)
        masked_low = masked.astype(jnp.bfloat16)
        grad_low = grad.astype(jnp.bfloat16)
        grad_turned = dot_nt(flip, grad_low).astype(jnp.bfloat16)
        masked_turned = dot_nn(flip, masked_low).astype(jnp.bfloat16)
        rows_high, rows_low = split_low(lag_matrix(rows_back_ref[one, :], side, lower))
        turned_high, turned_low = split_low(lag_matrix(rows_ref[one, :], side, upper))
        cols_high, cols_low = split_low(lag_matrix(cols_back_ref[one, :], side, lower))
        along = dot_nn(
            jnp.concatenate([rows_high, rows_low], axis=1),
            jnp.concatenate([masked_low, masked_low], axis=0),
        )
        along_grad = dot_nn(
            jnp.concatenate([grad_low, grad_low], axis=1),
            jnp.concatenate([cols_high, cols_low], axis=0),
        )
        along_high, along_low = split_low(along)
        grad_high, grad_rest = split_low(along_grad)
        cols_grad = dot_nn(
            jnp.concatenate([grad_turned, grad_turned], axis=1),
            jnp.concatenate([along_high, along_low], axis=0),
        )
        rows_grad = dot_nt(
            jnp.concatenate([grad_high, grad_rest], axis=1),
            jnp.concatenate([masked_turned, masked_turned], axis=1),
        )
        masked_grad = dot_nn(
            jnp.concatenate([turned_high, turned_low], axis=1),
            jnp.concatenate([grad_high, grad_high], axis=0),
        ) + dot_nn(turned_high, grad_rest)
        masked_grad = masked_grad + skip_ref[chan] * grad
        input_grad_ref[chan] = jnp.where(inside, grad_out + masked_grad, 0.0)
        rows_sums[one, :] = lag_sums(rows_grad, side, row_at + col_at >= side - 1)
        cols_sums[one, :] = lag_sums(cols_grad, side, row_at + col_at <= side - 1)

    @pl.loop(0, count // ABREAST)
    def _(few):
        pl.when(few == count // ABREAST // 2)(in_pass)
        pl.when(few == count // ABREAST * 5 // 8)(out_fourth)
        pl.when(few == count // ABREAST * 5 // 8)(norm_pass)
        for at in range(ABREAST):
            one_channel(few * ABREAST + at)

    small_own[:, :side] = rows_sums[...]
    small_own[:, side : 2 * side] = cols_sums[...]
    lane = lax.broadcasted_iota(jnp.int32, (count, side), 1)
    last = jnp.zeros((count, side), jnp.float32)
    for at, sums in enumerate((skip_sums, bias_sums_ref)):
        last = jnp.where(lane == at, jnp.sum(sums[...], axis=1, keepdims=True), last)
    small_own[:, 2 * side :] = last
    for turn in range(1, shares):
        small_push(turn).start()
    in_fourth()
    own.wait()
    for step in range(late):
        for shift in range(1, n):
            branch_push(step, shift, True).wait_recv()
            branch_push(step, shift).wait_send()

    @pl.loop(0, n)
    def _(owner):
        for step in range(early + late):
            part = branch_sent_ref.at[owner, step] if step < early else branch_got.at[owner, step - early]
            for line in range(lines):
                row = (owner * (early + late) + step) * lines + line
                wide[pl.ds(pl.multiple_of(row * count, count), count), :] = part[line].astype(jnp.float32)

    @pl.loop(0, count)
    def _(chan):
        one = pl.ds(chan, 1)
        shifted = wide[pl.ds(chan, side, stride=count), :] + bias_ref[chan]
        image = image_ref[chan].astype(jnp.float32)
        grad_out = jnp.where(inside, cot_ref[chan].astype(jnp.float32), 0.0)
        output_ref[chan] = jnp.where(inside, image + scale_ref[chan] * shifted, 0.0).astype(jnp.bfloat16)
        scale_sums[one, :] = jnp.sum(grad_out * shifted, axis=0, keepdims=True)

    late_own[...] = jnp.zeros_like(late_own)
    late_own[:, :count] = lane_sums(scale_sums[...])
    for turn in range(1, shares):
        late_push(turn).start()
    total = norm_mid[...]
    for turn in range(1, n):
        norm_second(turn).wait()
        total = total + norm_far[turn]
    norm_ref[...] = total
    out_finish()
    in_finish()
    total = small_own[...]
    for turn in range(1, shares):
        small_push(turn).wait()
        total = total + small_got[turn]
    small_ref[...] = total
    total = late_own[...]
    for turn in range(1, shares):
        late_push(turn).wait()
        total = total + late_got[turn]
    late_ref[...] = total


def mixer_back(n, shares, sizes, images, cotangent, grad, branch_sent, branch, lines, vectors, norms, sums):
    count, side, _ = images.shape
    near = n // 2
    block, channels = sums[0].shape[1:]
    rows = block // near
    wide = sums[1].shape[2]
    line = pltpu.VMEM((count, side), jnp.float32)
    norm = pltpu.VMEM((8, channels), jnp.float32)
    vmem = pl.BlockSpec(memory_space=pltpu.VMEM)
    hbm = pl.BlockSpec(memory_space=pl.ANY)
    full = functools.partial(jax.ShapeDtypeStruct, dtype=jnp.float32)
    return pl.pallas_call(
        functools.partial(back_kernel, n, shares),
        out_shape=(
            jax.ShapeDtypeStruct(images.shape, jnp.bfloat16),
            full(images.shape),
            full((count, 3 * side)),
            full((8, side)),
            full((8, channels)),
            jax.ShapeDtypeStruct((shares, rows, channels), jnp.bfloat16),
            jax.ShapeDtypeStruct((shares, rows, wide), jnp.bfloat16),
        ),
        in_specs=[pl.BlockSpec(memory_space=pltpu.SMEM)]
        + [vmem] * 4
        + [hbm]
        + [vmem] * len(lines)
        + [pl.BlockSpec(memory_space=pltpu.SMEM)] * len(vectors)
        + [vmem] * (len(norms) + 1)
        + [hbm],
        out_specs=(vmem,) * 5 + (hbm,) * 2,
        scratch_shapes=[
            pltpu.VMEM((count * side, side), jnp.float32),
            pltpu.VMEM(branch.shape, jnp.bfloat16),
            line,
            line,
            line,
            line,
            pltpu.VMEM((count, 3 * side), jnp.float32),
            pltpu.VMEM((shares, count, 3 * side), jnp.float32),
            pltpu.VMEM((8, side), jnp.float32),
            pltpu.VMEM((shares, 8, side), jnp.float32),
            norm,
            pltpu.VMEM((shares, 8, channels), jnp.float32),
            norm,
            pltpu.VMEM((n, 8, channels), jnp.float32),
            pltpu.VMEM(sums[1].shape, jnp.bfloat16),
        ]
        + [
            kind
            for columns in (channels, wide)
            for kind in (
                pltpu.VMEM((near, rows, columns), jnp.bfloat16),
                pltpu.VMEM((near, rows, columns), jnp.bfloat16),
                pltpu.VMEM((rows, columns), jnp.float32),
                pltpu.VMEM((rows, columns), jnp.bfloat16),
            )
        ]
        + [
            pltpu.SemaphoreType.DMA(size if isinstance(size, tuple) else (size,))
            for size in ((branch.shape[1], n), (branch.shape[1], n), 1, *(shares,) * 8, n, n)
            + (near, near, shares, shares, 1) * 2
        ],
        compiler_params=pltpu.CompilerParams(
            collective_id=2, has_side_effects=True, vmem_limit_bytes=62 * mebi
        ),
        name="mixer_back",
    )(sizes, images, cotangent, grad, branch_sent, branch, *lines, *vectors, *norms, *sums)


def taps_kernel(small_ref, *refs):
    params, (*grads, rest_ref), wide, turned = refs[:8], refs[8:17], refs[17], refs[18]
    count = small_ref.shape[0]
    side = wide.shape[0]
    wide[...] = jnp.zeros_like(wide)

    def turn(at):
        wide[:count, :] = small_ref[:, at * side : (at + 1) * side]
        turned[...] = wide[...].T

    def rows_load(lag):
        return turned[pl.ds(lax.rem(lag + side - 1, side), 1), :count]

    def cols_load(lag):
        return turned[pl.ds(side - 1 - lag, 1), :count]

    for at, load in enumerate((rows_load, cols_load)):
        turn(at)
        found = taps_adjoint(*(ref[...] for ref in params[4 * at : 4 * at + 4]), side, load)
        for ref, grad in zip(grads[4 * at : 4 * at + 4], found):
            ref[...] = grad
    turn(2)
    rest_ref[...] = turned[:8, :count]


def taps_back(small, params, side):
    modes, count = params[0].shape
    full = functools.partial(jax.ShapeDtypeStruct, dtype=jnp.float32)
    vmem = pl.BlockSpec(memory_space=pltpu.VMEM)
    return pl.pallas_call(
        taps_kernel,
        out_shape=(full((modes, count)),) * 8 + (full((8, count)),),
        in_specs=[vmem] * 9,
        out_specs=(vmem,) * 9,
        scratch_shapes=[pltpu.VMEM((side, side), jnp.float32), pltpu.VMEM((side, side), jnp.float32)],
        name="taps_back",
    )(small, *params)


def pixel_body(
    n,
    images,
    cotangent,
    image_sizes,
    slot_image,
    rows_rate,
    rows_freq,
    rows_real,
    rows_imag,
    cols_rate,
    cols_freq,
    cols_real,
    cols_imag,
    skip_gain,
    norm_gain,
    norm_bias,
    weight_in,
    bias_in,
    weight_out,
    bias_out,
    layer_scale,
):
    _, count, side, _ = images.shape
    channels = norm_gain.shape[0]
    picked = slot_image[lax.axis_index("dp")]
    sizes = image_sizes[picked]
    image, cot = images[0], cotangent[0]

    params = tuple(
        param.T
        for param in (
            rows_rate,
            rows_freq,
            rows_real,
            rows_imag,
            cols_rate,
            cols_freq,
            cols_real,
            cols_imag,
        )
    )
    shares = lax.axis_size("dp")
    hidden = weight_out.shape[0]
    spread = jnp.broadcast_to(bias_in[:, None], (hidden, side))
    in_part = jnp.concatenate([weight_in.T, spread], axis=1).reshape(shares, -1, channels + side)
    out_part = weight_out.reshape(shares, -1, channels)
    mixed, first, back, in_whole, out_whole, bias_out_sums, rows_back, rows, cols_back, _ = mixer_forward(
        n, shares, sizes, image, cot, skip_gain, layer_scale, params, in_part, out_part
    )
    grad, branch_sent, branch, _, _, *sums, gain_sums, shift_sums = mlp(
        n,
        shares,
        mixed,
        first,
        back,
        in_whole.reshape(-1, channels + side),
        out_whole.reshape(-1, channels),
        jnp.broadcast_to(norm_gain[:, None], (channels, side)),
        jnp.broadcast_to(norm_bias[:, None], (channels, side)),
    )
    output, input_grad, small, late, norms, out_final, in_final = mixer_back(
        n,
        shares,
        sizes,
        image,
        cot,
        grad.reshape(side, count, side),
        branch_sent,
        branch,
        (rows_back, rows, cols_back),
        (skip_gain, layer_scale, bias_out),
        (bias_out_sums, gain_sums, shift_sums),
        sums,
    )
    *params_grad, rest = taps_back(small, params, side)
    in_final = in_final.reshape(hidden, channels + side).astype(jnp.float32)
    return (
        output[None],
        input_grad[None],
        *(grad.T for grad in params_grad),
        rest[0],
        norms[0],
        norms[1],
        in_final[:, :channels].T,
        jnp.sum(in_final[:, channels:], axis=1),
        out_final.reshape(hidden, channels).astype(jnp.float32),
        rest[1],
        late[0, :count],
    )


def choose_body(n, images, *rest):
    slots, count, side, _ = images.shape
    fits = (
        slots == 1
        and side == 128
        and count <= side
        and count % GROUP == 0
        and side % (4 * n * LINES) == 0
        and n % 2 == 0
        and (rest[15].shape[0] * n) % (2 * STEP_HIDDEN) == 0
        and rest[15].shape[0] % (16 * lax.axis_size("dp")) == 0
        and lax.axis_size("dp") > 1
    )
    return pixel_body(n, images, *rest) if fits else plain_body(images, *rest)


def solution(mesh):
    in_specs = (
        P("dp", "chan", None, None),
        P("dp", "chan", None, None),
        P(),
        P(),
        P("chan", None),
        P("chan", None),
        P("chan", None),
        P("chan", None),
        P("chan", None),
        P("chan", None),
        P("chan", None),
        P("chan", None),
        P("chan"),
        P(),
        P(),
        P(None, "chan"),
        P("chan"),
        P("chan", None),
        P("chan"),
        P("chan"),
    )
    out_specs = (
        P("dp", "chan", None, None),
        P("dp", "chan", None, None),
        P("chan", None),
        P("chan", None),
        P("chan", None),
        P("chan", None),
        P("chan", None),
        P("chan", None),
        P("chan", None),
        P("chan", None),
        P("chan"),
        P(),
        P(),
        P(None, "chan"),
        P("chan"),
        P("chan", None),
        P("chan"),
        P("chan"),
    )
    return jax.shard_map(functools.partial(choose_body, mesh.shape["chan"]), mesh=mesh, in_specs=in_specs, out_specs=out_specs, check_vma=False)
```

```python
import functools

import jax
import jax.numpy as jnp
from jax import lax
from jax.experimental import pallas as pl
from jax.experimental.pallas import tpu as pltpu
from jax.sharding import PartitionSpec as P

eps_norm = 1e-06
highest = lax.Precision.HIGHEST


def kernel_taps(rate_vals, freq_vals, real_part, imag_part, length):
    offsets = jnp.arange(length, dtype=jnp.float32)
    decays = jnp.exp(-rate_vals[:, :, None] * offsets)
    angles = freq_vals[:, :, None] * offsets
    return jnp.sum(
        decays
        * (real_part[:, :, None] * jnp.cos(angles) - imag_part[:, :, None] * jnp.sin(angles)),
        axis=1,
    )


def toeplitz(filter_taps):
    length = filter_taps.shape[1]
    offsets = jnp.arange(length, dtype=jnp.int32)
    lag_index = offsets[:, None] - offsets[None, :]
    return jnp.where(lag_index[None] >= 0, filter_taps[:, jnp.maximum(lag_index, 0)], 0.0)


def mixer(
    masked_in,
    rows_rate,
    rows_freq,
    rows_real,
    rows_imag,
    cols_rate,
    cols_freq,
    cols_real,
    cols_imag,
    skip_gain,
):
    rows_op = toeplitz(kernel_taps(rows_rate, rows_freq, rows_real, rows_imag, masked_in.shape[2]))
    cols_op = toeplitz(kernel_taps(cols_rate, cols_freq, cols_real, cols_imag, masked_in.shape[3]))
    along_rows = jnp.einsum("chi,ncij->nchj", rows_op, masked_in, precision=highest)
    return (
        jnp.einsum("nchj,cwj->nchw", along_rows, cols_op, precision=highest)
        + skip_gain[None, :, None, None] * masked_in
    )


def normalize(values, norm_gain, norm_bias):
    center = values - jnp.mean(values, axis=-2, keepdims=True)
    inverse = lax.rsqrt(jnp.mean(center * center, axis=-2, keepdims=True) + eps_norm)
    scaled = center * inverse
    return (scaled * norm_gain[:, None] + norm_bias[:, None], scaled, inverse)


def gelu_exact(values):
    return jax.nn.gelu(values, approximate=False)


def plain_body(
    images,
    cotangent,
    image_sizes,
    slot_image,
    rows_rate,
    rows_freq,
    rows_real,
    rows_imag,
    cols_rate,
    cols_freq,
    cols_real,
    cols_imag,
    skip_gain,
    norm_gain,
    norm_bias,
    weight_in,
    bias_in,
    weight_out,
    bias_out,
    layer_scale,
):
    slot_count, chan_count, length = (images.shape[0], images.shape[1], images.shape[2])
    pixels = length * length
    image_count = slot_image.shape[0]
    slot_ids = lax.axis_index("dp") * slot_count + jnp.arange(slot_count, dtype=jnp.int32)
    choose = (slot_ids[:, None] == jnp.arange(image_count, dtype=jnp.int32)[None, :]).astype(
        jnp.int32
    )
    picked = jnp.sum(choose * slot_image[None, :], axis=1)
    owners = (picked[:, None] == jnp.arange(image_count, dtype=jnp.int32)[None, :]).astype(
        jnp.int32
    )
    heights = jnp.sum(owners * image_sizes[None, :, 0], axis=1)
    widths = jnp.sum(owners * image_sizes[None, :, 1], axis=1)
    offsets = jnp.arange(length, dtype=jnp.int32)
    inside = (
        (offsets[None, :, None] < heights[:, None, None])
        & (offsets[None, None, :] < widths[:, None, None])
    ).astype(jnp.float32)
    masked_in = images.astype(jnp.float32) * inside[:, None]
    mixed_out, mixer_pull = jax.vjp(
        mixer,
        masked_in,
        rows_rate,
        rows_freq,
        rows_real,
        rows_imag,
        cols_rate,
        cols_freq,
        cols_real,
        cols_imag,
        skip_gain,
    )
    mixed_low = mixed_out.astype(jnp.bfloat16).reshape(slot_count, chan_count, pixels)
    mask_flat = inside.reshape(slot_count, 1, pixels)
    residual = images.astype(jnp.float32).reshape(slot_count, chan_count, pixels)
    grad_out = cotangent.astype(jnp.float32).reshape(slot_count, chan_count, pixels) * mask_flat
    chan_offset = lax.axis_index("chan") * chan_count
    all_channels = norm_gain.shape[0]
    slot_item = 0
    gathered = lax.all_gather(mixed_low[slot_item], "chan", axis=0, tiled=True)
    normed, scaled, inverse = normalize(gathered.astype(jnp.float32), norm_gain, norm_bias)
    normed_low = normed.astype(jnp.bfloat16)
    before = (
        jnp.einsum("cf,cp->fp", weight_in, normed_low, preferred_element_type=jnp.float32)
        + bias_in.astype(jnp.float32)[:, None]
    )
    active = gelu_exact(before).astype(jnp.bfloat16)

    def project(first_row, row_count, active=active):
        return jnp.einsum("fc,fp->cp", weight_out, active, preferred_element_type=jnp.float32)

    branch_list = [
        lax.psum_scatter(
            project(jnp.int32(0), chan_count * lax.axis_size("chan")),
            "chan",
            scatter_dimension=0,
            tiled=True,
        )
    ]
    scaled_part = lax.dynamic_slice_in_dim(scaled, chan_offset, chan_count, 0)
    stored = [(normed_low, before, active, scaled_part, inverse)]
    branch_all = jnp.stack(branch_list)
    shifted = branch_all + bias_out[None, :, None]
    output = (
        (mask_flat * (residual + layer_scale[None, :, None] * shifted))
        .astype(jnp.bfloat16)
        .reshape(images.shape)
    )
    scale_grad = jnp.sum(grad_out * shifted, axis=(0, 2))
    branch_grad = layer_scale[None, :, None] * grad_out
    bias_out_grad = jnp.sum(branch_grad, axis=(0, 2))
    branch_low = branch_grad.astype(jnp.bfloat16)
    hidden_count = weight_in.shape[1]
    out_weight_grad = jnp.zeros((hidden_count, all_channels), jnp.float32)
    gain_shard = lax.dynamic_slice_in_dim(norm_gain, chan_offset, chan_count, 0)
    slot_item = 0
    normed_low, before, active, scaled_part, inverse = stored[slot_item]

    def absorb(totals, shard_rows, first_row, active=active):
        hidden_grad = jnp.einsum(
            "fc,cp->fp", weight_out, shard_rows, preferred_element_type=jnp.float32
        )
        product_part = jnp.einsum(
            "fp,cp->fc", active, shard_rows, preferred_element_type=jnp.float32
        )
        return (hidden_grad, product_part)

    hidden_start = jnp.zeros((hidden_count, pixels), jnp.float32)
    hidden_grad, out_weight_grad = absorb(
        (hidden_start, out_weight_grad),
        lax.all_gather(branch_low[slot_item], "chan", axis=0, tiled=True),
        jnp.int32(0),
    )
    gelu_pull = jax.vjp(gelu_exact, before)[1]
    before_grad = gelu_pull(hidden_grad)[0].astype(jnp.bfloat16)
    in_weight_grad = jnp.einsum(
        "cp,fp->cf", normed_low, before_grad, preferred_element_type=jnp.float32
    )
    in_bias_grad = jnp.sum(before_grad.astype(jnp.float32), axis=1)

    def spread_back(first_row, row_count, before_grad=before_grad):
        return jnp.einsum("cf,fp->cp", weight_in, before_grad, preferred_element_type=jnp.float32)

    normed_grad = lax.psum_scatter(
        spread_back(jnp.int32(0), chan_count * lax.axis_size("chan")),
        "chan",
        scatter_dimension=0,
        tiled=True,
    )
    weighted = normed_grad * gain_shard[:, None]
    pixel_sums = (
        lax.psum(jnp.sum(weighted, axis=0).astype(jnp.bfloat16), "chan").astype(jnp.float32),
        lax.psum(jnp.sum(weighted * scaled_part, axis=0).astype(jnp.bfloat16), "chan").astype(
            jnp.float32
        ),
    )
    mixed_grads = [
        inverse
        * (
            weighted
            - pixel_sums[0][None, :] / all_channels
            - scaled_part * pixel_sums[1][None, :] / all_channels
        )
    ]
    gain_part = jnp.sum(normed_grad * scaled_part, axis=1)
    shift_part = jnp.sum(normed_grad, axis=1)
    mixed_grad_all = jnp.stack(mixed_grads)
    gain_grad = lax.dynamic_update_slice_in_dim(
        jnp.zeros((all_channels,), jnp.float32), gain_part, chan_offset, 0
    )
    shift_grad = lax.dynamic_update_slice_in_dim(
        jnp.zeros((all_channels,), jnp.float32), shift_part, chan_offset, 0
    )
    pulled = mixer_pull(mixed_grad_all.reshape(images.shape))
    input_grad = inside[:, None] * (cotangent.astype(jnp.float32) + pulled[0])
    summed = lax.psum(
        (
            in_weight_grad,
            out_weight_grad,
            in_bias_grad,
            bias_out_grad,
            scale_grad,
            pulled[1],
            pulled[2],
            pulled[3],
            pulled[4],
            pulled[5],
            pulled[6],
            pulled[7],
            pulled[8],
            pulled[9],
        ),
        "dp",
    )
    norm_sums = lax.psum((gain_grad, shift_grad), ("dp", "chan"))
    return (
        output,
        input_grad,
        summed[5],
        summed[6],
        summed[7],
        summed[8],
        summed[9],
        summed[10],
        summed[11],
        summed[12],
        summed[13],
        norm_sums[0],
        norm_sums[1],
        summed[0],
        summed[2],
        summed[1],
        summed[3],
        summed[4],
    )


MESH = pl.DeviceIdType.MESH
GROUP = 16
ABREAST = 2
LINES = 4
STEP_HIDDEN = 512
mebi = 1024 * 1024


def dot_nn(left, right):
    return lax.dot_general(left, right, (((1,), (0,)), ((), ())), preferred_element_type=jnp.float32)


def dot_nt(left, right):
    return lax.dot_general(left, right, (((1,), (1,)), ((), ())), preferred_element_type=jnp.float32)


def dot_tn(left, right):
    return lax.dot_general(left, right, (((0,), (0,)), ((), ())), preferred_element_type=jnp.float32)


def split_low(values):
    high = values.astype(jnp.bfloat16)
    return high, (values - high.astype(jnp.float32)).astype(jnp.bfloat16)


def lag_matrix(line, side, keep):
    spread = pltpu.roll(jnp.broadcast_to(line, (side, side)), 0, 1, stride=1, stride_axis=0)
    return jnp.where(keep, spread, 0.0)


def lag_sums(matrix, side, keep):
    turned = pltpu.roll(jnp.where(keep, matrix, 0.0), 0, 1, stride=1, stride_axis=0)
    return jnp.sum(turned, axis=0, keepdims=True)


cos_terms = (
    1.0, -19.7392087, 64.9393891, -85.4566583, 60.242131, -26.4046662, 7.8001253, -1.45310477
)
sin_terms = (6.2831853, -41.3417004, 81.6051314, -76.703015, 42.0259236, -14.8998335, 3.23811835)


def polynomial(terms, at):
    value = terms[-1]
    for term in terms[-2::-1]:
        value = value * at + term
    return value


TILE = 16


def power(rate, freq, lag):
    angle = freq * 0.15915494309189535 * lag
    angle = angle - jnp.floor(angle + 0.5)
    square = angle * angle
    decay = jnp.exp(-rate * lag)
    return decay * polynomial(cos_terms, square), decay * (angle * polynomial(sin_terms, square))


def product(left, right):
    return left[0] * right[0] - left[1] * right[1], left[0] * right[1] + left[1] * right[0]


def taps_lines(rate, freq, real, imag, side, store):
    first = power(rate, freq, 1.0)

    @pl.loop(0, side // TILE)
    def _(tile):
        state = product((real, imag), power(rate, freq, (tile * TILE).astype(jnp.float32)))
        for step in range(TILE):
            store(tile * TILE + step, jnp.sum(state[0], axis=0, keepdims=True))
            state = product(state, first)


def taps_adjoint(rate, freq, real, imag, side, load):
    first = power(rate, freq, 1.0)

    def tile_sums(tile, totals):
        state = power(rate, freq, (tile * TILE).astype(jnp.float32))
        even, odd, even_lag, odd_lag = totals
        for step in range(TILE):
            grad = load(tile * TILE + step)
            late = grad * (tile * TILE + step).astype(jnp.float32)
            even = even + grad * state[0]
            odd = odd + grad * state[1]
            even_lag = even_lag + late * state[0]
            odd_lag = odd_lag + late * state[1]
            state = product(state, first)
        return even, odd, even_lag, odd_lag

    zero = jnp.zeros_like(rate)
    even, odd, even_lag, odd_lag = lax.fori_loop(0, side // TILE, tile_sums, (zero,) * 4)
    return imag * odd_lag - real * even_lag, -real * odd_lag - imag * even_lag, even, -odd


def lane_sums(values):
    ones = jnp.ones((8, values.shape[1]), jnp.bfloat16)
    high, rest = split_low(values)
    low = (values - high.astype(jnp.float32) - rest.astype(jnp.float32)).astype(jnp.bfloat16)
    return dot_nt(ones, high) + dot_nt(ones, rest) + dot_nt(ones, low)


def meet(n, shares):
    me, share = lax.axis_index("chan"), lax.axis_index("dp")
    barrier = pltpu.get_barrier_semaphore()
    for shift in range(1, n):
        pl.semaphore_signal(
            barrier, inc=1, device_id={"chan": lax.rem(me + shift, n)}, device_id_type=MESH
        )
    for shift in range(1, shares):
        pl.semaphore_signal(
            barrier, inc=1, device_id={"dp": lax.rem(share + shift, shares)}, device_id_type=MESH
        )
    pl.semaphore_wait(barrier, n + shares - 2)
    return me, share


def push(source, target, send_sem, recv_sem, **peer):
    return pltpu.make_async_remote_copy(
        src_ref=source,
        dst_ref=target,
        send_sem=send_sem,
        recv_sem=recv_sem,
        device_id=peer,
        device_id_type=MESH,
    )


def weight_rounds(n, shares, me, share, pairs, sems):
    near, far = n // 2, me // 2
    core = lax.rem(me, 2)
    own_sem, send1, recv1, send2, recv2, send3, recv3 = sems

    def own(at):
        local, whole = pairs[at]
        return pltpu.make_async_copy(local, whole.at[core, :, far], own_sem.at[at])

    def first(at, shift, back=False):
        local, whole = pairs[at]
        origin = lax.rem(far + near - shift, near) if back else far
        return push(
            local.at[share],
            whole.at[core, share, origin],
            send1.at[at, shift],
            recv1.at[at, shift],
            chan=lax.rem(far + shift, near) * 2 + core,
        )

    def second(at, shift, turn, back=False):
        whole = pairs[at][1]
        origin = lax.rem(far + near - shift, near)
        holder = lax.rem(share + shares - turn, shares) if back else share
        return push(
            whole.at[core, share, origin],
            whole.at[core, holder, origin],
            send2.at[at, shift, turn],
            recv2.at[at, shift, turn],
            dp=lax.rem(share + turn, shares),
        )

    def third(at, back=False):
        whole = pairs[at][1]
        return push(
            whole.at[core], whole.at[1 - core if back else core], send3.at[at], recv3.at[at], chan=far * 2 + 1 - core
        )

    both = range(len(pairs))

    def start_first():
        for at in both:
            own(at).start()
            for shift in range(1, near):
                first(at, shift).start()

    def start_second():
        for at in both:
            for shift in range(1, near):
                first(at, shift, True).wait_recv()
                for turn in range(1, shares):
                    second(at, shift, turn).start()

    def start_third():
        for at in both:
            own(at).wait()
            for shift in range(1, near):
                for turn in range(1, shares):
                    second(at, shift, turn, True).wait_recv()
            third(at).start()

    def finish():
        for at in both:
            third(at, True).wait_recv()
            third(at).wait_send()
            for shift in range(1, near):
                first(at, shift).wait_send()
                for turn in range(1, shares):
                    second(at, shift, turn).wait_send()

    return start_first, start_second, start_third, finish


def send_part(stage, target, me, peer, part, send_sem, recv_sem, shift):
    return pltpu.make_async_remote_copy(
        src_ref=stage.at[peer, part],
        dst_ref=target.at[me, part],
        send_sem=send_sem.at[shift],
        recv_sem=recv_sem.at[shift],
        device_id={"chan": peer},
        device_id_type=MESH,
    )


def wait_parts(stage, target, me, n, send_sem, recv_sem):
    for shift in range(1, n):
        peer = lax.rem(me + shift, n)
        origin = lax.rem(me + n - shift, n)
        pltpu.make_async_remote_copy(
            src_ref=stage.at[peer],
            dst_ref=target.at[origin],
            send_sem=send_sem.at[shift],
            recv_sem=recv_sem.at[shift],
            device_id={"chan": peer},
            device_id_type=MESH,
        ).wait()


def mixer_kernel(
    n,
    shares,
    sizes_ref,
    image_ref,
    cot_ref,
    skip_ref,
    scale_ref,
    *rest,
):
    mixer_body(n, shares, sizes_ref, image_ref, cot_ref, skip_ref, scale_ref, rest[:8], *rest[8:])


def mixer_body(
    n,
    shares,
    sizes_ref,
    image_ref,
    cot_ref,
    skip_ref,
    scale_ref,
    param_refs,
    in_part_ref,
    out_part_ref,
    mixed_ref,
    first_ref,
    back_ref,
    in_whole_ref,
    out_whole_ref,
    sums_ref,
    rows_back_ref,
    rows_ref,
    cols_back_ref,
    cols_ref,
    mixed_stage,
    back_stage,
    wide,
    taps,
    params_got,
    params_sem,
    send_m,
    recv_m,
    send_b,
    recv_b,
    own_sem,
    keep_sem,
    *weight_sems,
):
    count, side, _ = image_ref.shape
    parts = count // GROUP
    block = side // n
    me, share = meet(n, shares)
    start_first, start_second, start_third, finish = weight_rounds(
        n, shares, me, share, ((in_part_ref, in_whole_ref), (out_part_ref, out_whole_ref)), weight_sems
    )
    start_first()
    param_copies = [
        pltpu.make_async_copy(ref, params_got.at[at], params_sem.at[at]) for at, ref in enumerate(param_refs)
    ]
    for copy in param_copies:
        copy.start()
    taps[...] = jnp.zeros_like(taps)
    row_at = lax.broadcasted_iota(jnp.int32, (side, side), 0)
    col_at = lax.broadcasted_iota(jnp.int32, (side, side), 1)
    inside = (row_at < sizes_ref[0]) & (col_at < sizes_ref[1])
    lower = row_at >= col_at
    upper = row_at <= col_at

    def turn(stage, part):
        @pl.loop(0, n)
        def _(owner):
            for line in range(block):
                tile = wide[pl.ds(owner * block + line, GROUP, stride=side), :]
                stage[owner, part, line] = tile.astype(jnp.bfloat16)

    def send(stage, target, part, send_sem, recv_sem):
        for shift in range(1, n):
            send_part(stage, target, me, lax.rem(me + shift, n), part, send_sem, recv_sem, shift).start()

    def own_back(part):
        return pltpu.make_async_copy(back_stage.at[:, part], back_ref.at[:, part], keep_sem.at[part])

    def first_push(shift, back=False):
        peer = lax.rem(me + shift, n)
        return push(
            back_stage.at[peer, :, pl.ds(0, LINES)],
            first_ref.at[lax.rem(me + n - shift, n) if back else me],
            send_b.at[shift],
            recv_b.at[shift],
            chan=peer,
        )

    for copy in param_copies:
        copy.wait()
    for axis, (back_out, out) in enumerate(((rows_back_ref, rows_ref), (cols_back_ref, cols_ref))):

        def store(lag, line):
            taps[0, pl.ds(lax.rem(side - lag, side), 1), :count] = line
            taps[1, pl.ds(lag, 1), :count] = line

        taps_lines(*(params_got[4 * axis + at] for at in range(4)), side, store)
        back_out[...] = taps[0].T[:count]
        out[...] = taps[1].T[:count]


    @pl.loop(0, parts)
    def _(part):
        pl.when(part == parts // 2)(start_second)

        def one_channel(item):
            chan = part * GROUP + item
            masked = jnp.where(inside, image_ref[chan].astype(jnp.float32), 0.0)
            masked_low = masked.astype(jnp.bfloat16)
            rows_high, rows_low = split_low(lag_matrix(rows_back_ref[pl.ds(chan, 1), :], side, lower))
            cols_high, cols_low = split_low(lag_matrix(cols_ref[pl.ds(chan, 1), :], side, upper))
            along = dot_nn(
                jnp.concatenate([rows_high, rows_low], axis=1),
                jnp.concatenate([masked_low, masked_low], axis=0),
            )
            along_high, along_low = split_low(along)
            mixed = dot_nn(
                jnp.concatenate([along_high, along_low], axis=1),
                jnp.concatenate([cols_high, cols_high], axis=0),
            ) + dot_nn(along_high, cols_low)
            mixed = mixed + skip_ref[chan] * masked
            wide[pl.ds(pl.multiple_of(item * side, side), side), :] = mixed

        @pl.loop(0, GROUP // ABREAST)
        def _(few):
            for at in range(ABREAST):
                one_channel(few * ABREAST + at)

        turn(mixed_stage, part)
        send(mixed_stage, mixed_ref, part, send_m, recv_m)

    @pl.loop(0, parts)
    def _(part):
        @pl.loop(0, GROUP)
        def _(item):
            chan = part * GROUP + item
            grad_out = jnp.where(inside, cot_ref[chan].astype(jnp.float32), 0.0)
            scaled = grad_out * scale_ref[chan]
            sums_ref[pl.ds(chan, 1), :] = jnp.sum(scaled, axis=0, keepdims=True)
            wide[pl.ds(pl.multiple_of(item * side, side), side), :] = scaled

        turn(back_stage, part)
        own_back(part).start()

    for shift in range(1, n):
        first_push(shift).start()
    own_b = pltpu.make_async_copy(back_stage.at[me, :, pl.ds(0, LINES)], first_ref.at[me], own_sem.at[0])
    own_m = pltpu.make_async_copy(mixed_stage.at[me], mixed_ref.at[me], own_sem.at[1])
    own_b.start()
    own_m.start()
    start_third()
    for part in range(parts):
        own_back(part).wait()
    own_b.wait()
    own_m.wait()
    wait_parts(mixed_stage, mixed_ref, me, n, send_m, recv_m)
    for shift in range(1, n):
        first_push(shift, True).wait_recv()
        first_push(shift).wait_send()
    finish()


def mixer_forward(n, shares, sizes, images, cotangent, skip, scale, params, in_part, out_part):
    near = n // 2
    smem = pl.BlockSpec(memory_space=pltpu.SMEM)
    count, side, _ = images.shape
    line = jax.ShapeDtypeStruct((count, side), jnp.float32)
    shape = (n, count // GROUP, side // n, GROUP, side)
    first_shape = (n, count // GROUP, LINES, GROUP, side)
    vmem = pl.BlockSpec(memory_space=pltpu.VMEM)
    hbm = pl.BlockSpec(memory_space=pl.ANY)
    return pl.pallas_call(
        functools.partial(mixer_kernel, n, shares),
        out_shape=(
            jax.ShapeDtypeStruct(shape, jnp.bfloat16),
            jax.ShapeDtypeStruct(first_shape, jnp.bfloat16),
            jax.ShapeDtypeStruct(shape, jnp.bfloat16),
        )
        + tuple(
            jax.ShapeDtypeStruct((2, shares, near, *part.shape[1:]), jnp.bfloat16)
            for part in (in_part, out_part)
        )
        + (line,) * 5,
        in_specs=[smem] + [vmem] * 2 + [smem] * 2 + [hbm] * 10,
        out_specs=(hbm,) * 5 + (vmem,) * 5,
        scratch_shapes=[
            pltpu.VMEM(shape, jnp.bfloat16),
            pltpu.VMEM(shape, jnp.bfloat16),
            pltpu.VMEM((GROUP * side, side), jnp.float32),
            pltpu.VMEM((2, side, side), jnp.float32),
            pltpu.VMEM((8, *params[0].shape), jnp.float32),
            pltpu.SemaphoreType.DMA((8,)),
            pltpu.SemaphoreType.DMA((n,)),
            pltpu.SemaphoreType.DMA((n,)),
            pltpu.SemaphoreType.DMA((n,)),
            pltpu.SemaphoreType.DMA((n,)),
            pltpu.SemaphoreType.DMA((2,)),
            pltpu.SemaphoreType.DMA((count // GROUP,)),
            pltpu.SemaphoreType.DMA((2,)),
            pltpu.SemaphoreType.DMA((2, near)),
            pltpu.SemaphoreType.DMA((2, near)),
            pltpu.SemaphoreType.DMA((2, near, shares)),
            pltpu.SemaphoreType.DMA((2, near, shares)),
            pltpu.SemaphoreType.DMA((2,)),
            pltpu.SemaphoreType.DMA((2,)),
        ],
        compiler_params=pltpu.CompilerParams(
            collective_id=0, has_side_effects=True, vmem_limit_bytes=40 * mebi
        ),
        name="mixer_forward",
    )(sizes, images, cotangent, skip, scale, *params, in_part, out_part)


def gelu_parts(value):
    bell = jnp.exp(-0.5 * value * value)
    inner = 1.0 / (1.0 + (0.3275911 * 0.7071067811865476) * jnp.abs(value))
    series = 1.061405429 * inner - 1.453152027
    series = series * inner + 1.421413741
    series = series * inner - 0.284496736
    series = series * inner + 0.254829592
    tail = (0.5 * inner) * series * bell
    return jnp.where(value < 0.0, tail, 1.0 - tail), bell * 0.3989422804014327


def mlp_kernel(
    n,
    shares,
    mixed_hbm,
    first_hbm,
    in_hbm,
    out_hbm,
    gain_ref,
    shift_ref,
    back_ref,
    grad_ref,
    branch_sent_ref,
    branch_ref,
    active_ref,
    before_grad_ref,
    out_take_ref,
    in_half_ref,
    gain_grad_ref,
    shift_grad_ref,
    grad_stage,
    branch_stage,
    active_ring,
    before_ring,
    normed_keep,
    cots_keep,
    scaled_keep,
    inverse_keep,
    branch_sum,
    grad_sum,
    hidden_sum,
    pieces,
    rows_stage,
    out_got,
    in_got,
    back_got,
    mixed_ref,
    first_ref,
    in_ref,
    out_ref,
    load_sem,
    send_g,
    recv_g,
    send_c,
    recv_c,
    send_r,
    recv_r,
    own_sem,
    ring_sem,
    piece_sem,
    send_h,
    recv_h,
    send_2,
    recv_2,
):
    loads = [
        pltpu.make_async_copy(whole, here, load_sem.at[at])
        for at, (whole, here) in enumerate(
            ((mixed_hbm, mixed_ref), (first_hbm, first_ref), (in_hbm, in_ref), (out_hbm, out_ref))
        )
    ]
    for copy in loads:
        copy.start()
    side = mixed_ref.shape[-1]
    groups = mixed_ref.shape[1]
    block = mixed_ref.shape[2]
    hidden, channels = out_ref.shape
    local = channels // n
    steps = block // LINES
    width = LINES * side
    parts = hidden // STEP_HIDDEN
    ring = active_ring.shape[0]
    me, share = meet(n, shares)
    core = lax.rem(me, 2)
    sibling = me + 1 - 2 * core
    early = branch_sent_ref.shape[1]

    def cot_push(step, shift, back=False):
        peer = lax.rem(me + shift, n)
        origin = lax.rem(me + n - shift, n) if back else me
        span = pl.ds(step * LINES, LINES)
        return push(
            back_ref.at[peer, :, span],
            back_got.at[origin, :, span],
            send_c.at[step, shift],
            recv_c.at[step, shift],
            chan=peer,
        )

    def branch_push(shift, back=False):
        peer = lax.rem(me + shift, n)
        return push(
            branch_stage.at[peer, pl.ds(0, early)],
            branch_sent_ref.at[lax.rem(me + n - shift, n) if back else me],
            send_r.at[shift],
            recv_r.at[shift],
            chan=peer,
        )

    for step in range(1, steps):
        for shift in range(1, n):
            cot_push(step, shift).start()
    own_c = pltpu.make_async_copy(back_ref.at[me], back_got.at[me], own_sem.at[2])
    own_c.start()
    for copy in loads:
        copy.wait()
    gain_grad_ref[...] = jnp.zeros_like(gain_grad_ref)
    shift_grad_ref[...] = jnp.zeros_like(shift_grad_ref)
    hidden_sum[...] = jnp.zeros_like(hidden_sum)

    def keeps(turn):
        slot = lax.rem(turn, ring)
        span = pl.ds(pl.multiple_of(lax.rem(turn, parts) * STEP_HIDDEN, STEP_HIDDEN), STEP_HIDDEN)
        return [
            pltpu.make_async_copy(kept.at[slot], whole.at[turn // parts, span], ring_sem.at[at, slot])
            for at, (kept, whole) in enumerate(((active_ring, active_ref), (before_ring, before_grad_ref)))
        ]

    @pl.loop(0, steps)
    def _(step):
        pl.when(step == 1)(own_c.wait)

        @pl.when(step > 0)
        def _():
            for shift in range(1, n):
                cot_push(step, shift, True).wait_recv()

        for line in range(LINES):
            row = step * LINES + line
            lanes = pl.ds(line * side, side)
            order = [(owner, group) for owner in range(n) for group in range(groups)]
            mixed = jnp.concatenate(
                [mixed_ref[owner, group, row].astype(jnp.float32) for owner, group in order], axis=0
            )
            mean = jnp.sum(mixed, axis=0, keepdims=True) * (1.0 / channels)
            center = mixed - mean
            var = jnp.sum(center * center, axis=0, keepdims=True) * (1.0 / channels)
            inverse = lax.rsqrt(var + eps_norm)
            scaled = center * inverse
            normed_keep[step, :, lanes] = (scaled * gain_ref[...] + shift_ref[...]).astype(jnp.bfloat16)
            scaled_keep[:, lanes] = scaled
            inverse_keep[:, lanes] = inverse

            @pl.when(step == 0)
            def _():
                cots_keep[step, :, lanes] = jnp.concatenate(
                    [first_ref[owner, group, line] for owner, group in order], axis=0
                )

            @pl.when(step > 0)
            def _():
                cots_keep[step, :, lanes] = jnp.concatenate(
                    [back_got[owner, group, row] for owner, group in order], axis=0
                )

        @pl.loop(0, parts)
        def _(part):
            turn = step * parts + part
            slot = lax.rem(turn, ring)

            @pl.when(turn >= ring)
            def _():
                for copy in keeps(turn - ring):
                    copy.wait()

            span = pl.ds(pl.multiple_of(part * STEP_HIDDEN, STEP_HIDDEN), STEP_HIDDEN)
            bias = in_ref[span, channels:].astype(jnp.float32)[:, :1]
            before = dot_nn(in_ref[span, :channels], normed_keep[step]) + bias
            inside, bell = gelu_parts(before)
            active = (before * inside).astype(jnp.bfloat16)
            active_grad = dot_nn(out_ref[span, :], cots_keep[step])
            before_grad = (active_grad * (inside + before * bell)).astype(jnp.bfloat16)
            active_ring[slot] = active
            before_ring[slot] = before_grad
            hidden_sum[span, :] += sum(
                before_grad[:, line * side : (line + 1) * side].astype(jnp.float32) for line in range(LINES)
            )
            branch = dot_tn(out_ref[span, :], active)
            grad = dot_tn(in_ref[span, :channels], before_grad)

            @pl.when(part == 0)
            def _():
                branch_sum[...] = branch
                grad_sum[...] = grad

            @pl.when(part > 0)
            def _():
                branch_sum[...] += branch
                grad_sum[...] += grad

            for copy in keeps(turn):
                copy.start()

        for line in range(LINES):
            lanes = pl.ds(line * side, side)
            grad = grad_sum[:, lanes]
            scaled = scaled_keep[:, lanes]
            gain_grad_ref[...] += grad * scaled
            shift_grad_ref[...] += grad
            weighted = grad * gain_ref[...]
            first = jnp.sum(weighted, axis=0, keepdims=True) * (1.0 / channels)
            second = jnp.sum(weighted * scaled, axis=0, keepdims=True) * (1.0 / channels)
            mixed_grad = (inverse_keep[:, lanes] * (weighted - first - scaled * second)).astype(jnp.bfloat16)
            branch = branch_sum[:, lanes].astype(jnp.bfloat16)
            for owner in range(n):
                grad_stage[owner, step, line] = mixed_grad[owner * local : (owner + 1) * local]
                branch_stage[owner, step, line] = branch[owner * local : (owner + 1) * local]

        for shift in range(1, n):
            send_part(grad_stage, grad_ref, me, lax.rem(me + shift, n), step, send_g, recv_g, shift).start()

    own_g = pltpu.make_async_copy(grad_stage.at[me], grad_ref.at[me], own_sem.at[0])
    own_r = pltpu.make_async_copy(branch_stage.at[:, pl.ds(early, steps - early)], branch_ref, own_sem.at[1])
    own_s = pltpu.make_async_copy(branch_stage.at[me, pl.ds(0, early)], branch_sent_ref.at[me], own_sem.at[3])
    for shift in range(1, n):
        branch_push(shift).start()
    own_g.start()
    own_r.start()
    own_s.start()
    turns = steps * parts
    for turn in range(turns - ring, turns):
        for copy in keeps(turn):
            copy.wait()

    block_rows = hidden // 2 // shares
    kinds = (
        (active_ref, cots_keep, out_got, out_take_ref),
        (before_grad_ref, normed_keep, in_got, in_half_ref),
    )

    def block_span(job, base=0):
        at = lax.rem(share + 1 + lax.rem(job, shares), shares)
        return pl.ds(pl.multiple_of(base + at * block_rows, block_rows), block_rows)

    def whole_span(job):
        owner = 1 - core if job < shares else core
        return block_span(job, owner * (hidden // 2))

    def fetch(kind, job, slot):
        return pltpu.make_async_copy(
            kinds[kind][0].at[:, whole_span(job)], pieces.at[slot], piece_sem.at[slot]
        )

    def give(kind, job):
        got = kinds[kind][2]
        return push(
            rows_stage.at[job, :, pl.ds(0, got.shape[1])],
            got.at[block_span(job)],
            send_h.at[kind, job],
            recv_h.at[kind, job],
            chan=sibling,
        )

    def second(kind, job):
        _, _, got, take = kinds[kind]
        turn = job + 1 - shares
        if kind == 1:
            at = lax.rem(share + turn, shares)
            return pltpu.make_async_copy(got.at[block_span(job)], take.at[at], send_2.at[1, turn - 1])
        if turn == shares:
            return pltpu.make_async_copy(got.at[block_span(job)], take.at[0], send_2.at[0, 0])
        return push(
            got.at[block_span(job)],
            take.at[turn],
            send_2.at[kind, turn],
            recv_2.at[kind, turn],
            dp=lax.rem(share + turn, shares),
        )

    jobs = [(kind, job) for kind in range(2) for job in range(2 * shares)]
    fetch(0, 0, 0).start()
    for at, (kind, job) in enumerate(jobs):
        slot = at % 2
        if at + 1 < len(jobs):
            fetch(*jobs[at + 1], (at + 1) % 2).start()
        fetch(kind, job, slot).wait()
        right, got = kinds[kind][1:3]
        total = dot_nt(
            jnp.concatenate([pieces[slot, step] for step in range(steps)], axis=1),
            jnp.concatenate([right[step] for step in range(steps)], axis=1),
        )
        if job < shares:
            rows_stage[job, :, :channels] = total.astype(jnp.bfloat16)
            if kind == 1:
                rows_stage[job, :, channels:] = hidden_sum[whole_span(job), :].astype(jnp.bfloat16)
            give(kind, job).start()
        else:
            give(kind, job - shares).wait()
            span = block_span(job)
            got[span, :channels] = (total + got[span, :channels].astype(jnp.float32)).astype(jnp.bfloat16)
            if kind == 1:
                got[span, channels:] = (
                    hidden_sum[whole_span(job), :] + got[span, channels:].astype(jnp.float32)
                ).astype(jnp.bfloat16)
            second(kind, job).start()
    for kind in range(2):
        for job in range(shares, 2 * shares):
            second(kind, job).wait()
    own_g.wait()
    own_r.wait()
    own_s.wait()
    wait_parts(grad_stage, grad_ref, me, n, send_g, recv_g)
    for shift in range(1, n):
        branch_push(shift, True).wait_recv()
        branch_push(shift).wait_send()
        for step in range(1, steps):
            cot_push(step, shift).wait_send()


def mlp(n, shares, mixed, first, back, in_full, out_full, gain, shift):
    _, groups, block, group, side = mixed.shape
    hidden, channels = out_full.shape
    local = channels // n
    steps = block // LINES
    width = LINES * side
    shape = (n, steps, LINES, local, side)
    ring = 4
    low = functools.partial(jax.ShapeDtypeStruct, dtype=jnp.bfloat16)
    vmem = pl.BlockSpec(memory_space=pltpu.VMEM)
    hbm = pl.BlockSpec(memory_space=pl.ANY)
    return pl.pallas_call(
        functools.partial(mlp_kernel, n, shares),
        out_shape=(
            low(shape),
            low((n, steps // 4, *shape[2:])),
            low((n, steps - steps // 4, *shape[2:])),
            low((steps, hidden, width)),
            low((steps, hidden, width)),
            low((shares, hidden // 2 // shares, channels)),
            low((shares, hidden // 2 // shares, channels + side)),
            jax.ShapeDtypeStruct((channels, side), jnp.float32),
            jax.ShapeDtypeStruct((channels, side), jnp.float32),
        ),
        in_specs=[hbm] * 4 + [vmem] * 2 + [hbm],
        out_specs=(hbm,) * 7 + (vmem, vmem),
        scratch_shapes=[
            pltpu.VMEM(shape, jnp.bfloat16),
            pltpu.VMEM(shape, jnp.bfloat16),
            pltpu.VMEM((ring, STEP_HIDDEN, width), jnp.bfloat16),
            pltpu.VMEM((ring, STEP_HIDDEN, width), jnp.bfloat16),
            pltpu.VMEM((steps, channels, width), jnp.bfloat16),
            pltpu.VMEM((steps, channels, width), jnp.bfloat16),
            pltpu.VMEM((channels, width), jnp.float32),
            pltpu.VMEM((1, width), jnp.float32),
            pltpu.VMEM((channels, width), jnp.float32),
            pltpu.VMEM((channels, width), jnp.float32),
            pltpu.VMEM((hidden, side), jnp.float32),
            pltpu.VMEM((2, steps, hidden // 2 // shares, width), jnp.bfloat16),
            pltpu.VMEM((shares, hidden // 2 // shares, channels + side), jnp.bfloat16),
            pltpu.VMEM((hidden // 2, channels), jnp.bfloat16),
            pltpu.VMEM((hidden // 2, channels + side), jnp.bfloat16),
            pltpu.VMEM(back.shape, jnp.bfloat16),
            *(pltpu.VMEM(whole.shape, whole.dtype) for whole in (mixed, first, in_full, out_full)),
            pltpu.SemaphoreType.DMA((4,)),
            pltpu.SemaphoreType.DMA((n,)),
            pltpu.SemaphoreType.DMA((n,)),
            pltpu.SemaphoreType.DMA((steps, n)),
            pltpu.SemaphoreType.DMA((steps, n)),
            pltpu.SemaphoreType.DMA((n,)),
            pltpu.SemaphoreType.DMA((n,)),
            pltpu.SemaphoreType.DMA((4,)),
            pltpu.SemaphoreType.DMA((2, ring)),
            pltpu.SemaphoreType.DMA((2,)),
            pltpu.SemaphoreType.DMA((2, shares)),
            pltpu.SemaphoreType.DMA((2, shares)),
            pltpu.SemaphoreType.DMA((2, shares)),
            pltpu.SemaphoreType.DMA((2, shares)),
        ],
        compiler_params=pltpu.CompilerParams(
            collective_id=1, has_side_effects=True, vmem_limit_bytes=63 * mebi
        ),
        name="mlp",
    )(mixed, first, in_full, out_full, gain, shift, back)


def sum_rounds(n, shares, me, share, part, final, stage3, take3, keep3, keep4, send3, recv3, send4, recv4, own_sem):
    near, far = n // 2, me // 2
    core = lax.rem(me, 2)

    def third(turn):
        peer = lax.rem(far + turn, near)
        return push(stage3.at[peer], take3.at[turn], send3.at[turn], recv3.at[turn], chan=peer * 2 + core)

    def fourth(turn, back=False):
        holder = lax.rem(share + shares - turn, shares) if back else share
        peer = lax.rem(share + turn, shares)
        return push(keep4, final.at[holder], send4.at[turn], recv4.at[turn], dp=peer)

    def mine():
        return pltpu.make_async_copy(keep4, final.at[share], own_sem.at[0])

    def start_third():
        for at in range(near):
            total = part(at)
            stage3[at] = total.astype(jnp.bfloat16)

            @pl.when(far == at)
            def _():
                keep3[...] = total

        for turn in range(1, near):
            third(turn).start()

    def start_fourth():
        for turn in range(1, near):
            third(turn).wait()
        total = keep3[...]
        for turn in range(1, near):
            total = total + take3[turn].astype(jnp.float32)
        keep4[...] = total.astype(jnp.bfloat16)
        mine().start()
        for turn in range(1, shares):
            fourth(turn).start()

    def finish():
        mine().wait()
        for turn in range(1, shares):
            fourth(turn, True).wait_recv()
            fourth(turn).wait_send()

    return start_third, start_fourth, finish


def back_kernel(
    n,
    shares,
    sizes_ref,
    image_hbm,
    cot_hbm,
    grad_hbm,
    branch_sent_hbm,
    branch_ref,
    rows_back_ref,
    rows_ref,
    cols_back_ref,
    skip_ref,
    scale_ref,
    bias_ref,
    bias_sums_ref,
    gain_sums_ref,
    shift_sums_ref,
    out_take_hbm,
    in_half_ref,
    output_ref,
    input_grad_ref,
    small_ref,
    late_ref,
    norm_ref,
    out_final_ref,
    in_final_ref,
    wide,
    branch_got,
    rows_sums,
    cols_sums,
    skip_sums,
    scale_sums,
    small_own,
    small_got,
    late_own,
    late_got,
    norm_own,
    norm_near,
    norm_mid,
    norm_far,
    in_take,
    image_ref,
    cot_ref,
    grad_ref,
    branch_sent_ref,
    out_take_ref,
    load_sem,
    out_stage3,
    out_take3,
    out_keep3,
    out_keep4,
    in_stage3,
    in_take3,
    in_keep3,
    in_keep4,
    send_sem,
    recv_sem,
    own_sem,
    send_2,
    recv_2,
    send_s,
    recv_s,
    send_l,
    recv_l,
    send_n,
    recv_n,
    send_f,
    recv_f,
    *round_sems,
):
    loads = [
        pltpu.make_async_copy(whole, here, load_sem.at[at])
        for at, (whole, here) in enumerate(
            (
                (out_take_hbm, out_take_ref),
                (grad_hbm, grad_ref),
                (image_hbm, image_ref),
                (cot_hbm, cot_ref),
                (branch_sent_hbm, branch_sent_ref),
            )
        )
    ]
    for copy in loads:
        copy.start()
    count, side, _ = image_ref.shape
    late, lines = branch_ref.shape[1], branch_ref.shape[2]
    early = branch_sent_ref.shape[1]
    near = n // 2
    rows = in_keep3.shape[0]
    me, share = meet(n, shares)

    def summed(take):
        return lambda at: sum(take[turn, at * rows : (at + 1) * rows].astype(jnp.float32) for turn in range(shares))

    out_third, out_fourth, out_finish = sum_rounds(
        n, shares, me, share, summed(out_take_ref), out_final_ref, out_stage3, out_take3, out_keep3, out_keep4, *round_sems[:5]
    )
    in_third, in_fourth, in_finish = sum_rounds(
        n, shares, me, share, summed(in_take), in_final_ref, in_stage3, in_take3, in_keep3, in_keep4, *round_sems[5:]
    )

    def in_second(turn):
        peer = lax.rem(share + turn, shares)
        if turn == 0:
            return pltpu.make_async_copy(in_half_ref.at[peer], in_take.at[0], send_2.at[0])
        return push(in_half_ref.at[peer], in_take.at[turn], send_2.at[turn], recv_2.at[turn], dp=peer)

    def branch_push(step, shift, back=False):
        peer = lax.rem(me + shift, n)
        return push(
            branch_ref.at[peer, step],
            branch_got.at[lax.rem(me + n - shift, n) if back else me, step],
            send_sem.at[step, shift],
            recv_sem.at[step, shift],
            chan=peer,
        )

    def start_branch(step):
        for shift in range(1, n):
            branch_push(step, shift).start()

    def norm_first(turn):
        peer = lax.rem(share + turn, shares)
        return push(norm_own, norm_near.at[turn], send_n.at[turn], recv_n.at[turn], dp=peer)

    def norm_second(turn):
        peer = lax.rem(me + turn, n)
        return push(norm_mid, norm_far.at[turn], send_f.at[turn], recv_f.at[turn], chan=peer)

    def small_push(turn):
        peer = lax.rem(share + turn, shares)
        return push(small_own, small_got.at[turn], send_s.at[turn], recv_s.at[turn], dp=peer)

    def late_push(turn):
        peer = lax.rem(share + turn, shares)
        return push(late_own, late_got.at[turn], send_l.at[turn], recv_l.at[turn], dp=peer)

    def norm_pass():
        total = norm_own[...]
        for turn in range(1, shares):
            norm_first(turn).wait()
            total = total + norm_near[turn]
        norm_mid[...] = total
        for turn in range(1, n):
            norm_second(turn).start()

    def in_pass():
        for turn in range(shares):
            in_second(turn).wait()
        in_third()
        start_branch(late - 1)

    top = lax.broadcasted_iota(jnp.int32, norm_own.shape, 0) == 0
    norm_own[...] = jnp.where(top, lane_sums(gain_sums_ref[...]), lane_sums(shift_sums_ref[...]))
    for turn in range(1, shares):
        norm_first(turn).start()
    for turn in range(shares):
        in_second(turn).start()
    loads[0].wait()
    out_third()
    for step in range(late - 1):
        start_branch(step)
    for copy in loads[1:]:
        copy.wait()
    own = pltpu.make_async_copy(branch_ref.at[me], branch_got.at[me], own_sem.at[0])
    own.start()
    row_at = lax.broadcasted_iota(jnp.int32, (side, side), 0)
    col_at = lax.broadcasted_iota(jnp.int32, (side, side), 1)
    inside = (row_at < sizes_ref[0]) & (col_at < sizes_ref[1])
    lower = row_at >= col_at
    upper = row_at <= col_at
    flip = (row_at + col_at == side - 1).astype(jnp.bfloat16)

    @pl.loop(0, side)
    def _(row):
        span = pl.ds(pl.multiple_of(row * count, count), count)
        wide[span, :] = grad_ref[row].astype(jnp.float32)

    def one_channel(chan):
        one = pl.ds(chan, 1)
        grad = wide[pl.ds(chan, side, stride=count), :]
        image = image_ref[chan].astype(jnp.float32)
        grad_out = jnp.where(inside, cot_ref[chan].astype(jnp.float32), 0.0)
        masked = jnp.where(inside, image, 0.0)
        skip_sums[one, :] = jnp.sum(grad * masked, axis=0, keepdims=True)
        masked_low = masked.astype(jnp.bfloat16)
        grad_low = grad.astype(jnp.bfloat16)
        grad_turned = dot_nt(flip, grad_low).astype(jnp.bfloat16)
        masked_turned = dot_nn(flip, masked_low).astype(jnp.bfloat16)
        rows_high, rows_low = split_low(lag_matrix(rows_back_ref[one, :], side, lower))
        turned_high, turned_low = split_low(lag_matrix(rows_ref[one, :], side, upper))
        cols_high, cols_low = split_low(lag_matrix(cols_back_ref[one, :], side, lower))
        along = dot_nn(
            jnp.concatenate([rows_high, rows_low], axis=1),
            jnp.concatenate([masked_low, masked_low], axis=0),
        )
        along_grad = dot_nn(
            jnp.concatenate([grad_low, grad_low], axis=1),
            jnp.concatenate([cols_high, cols_low], axis=0),
        )
        along_high, along_low = split_low(along)
        grad_high, grad_rest = split_low(along_grad)
        cols_grad = dot_nn(
            jnp.concatenate([grad_turned, grad_turned], axis=1),
            jnp.concatenate([along_high, along_low], axis=0),
        )
        rows_grad = dot_nt(
            jnp.concatenate([grad_high, grad_rest], axis=1),
            jnp.concatenate([masked_turned, masked_turned], axis=1),
        )
        masked_grad = dot_nn(
            jnp.concatenate([turned_high, turned_low], axis=1),
            jnp.concatenate([grad_high, grad_high], axis=0),
        ) + dot_nn(turned_high, grad_rest)
        masked_grad = masked_grad + skip_ref[chan] * grad
        input_grad_ref[chan] = jnp.where(inside, grad_out + masked_grad, 0.0)
        rows_sums[one, :] = lag_sums(rows_grad, side, row_at + col_at >= side - 1)
        cols_sums[one, :] = lag_sums(cols_grad, side, row_at + col_at <= side - 1)

    @pl.loop(0, count // ABREAST)
    def _(few):
        pl.when(few == count // ABREAST * 7 // 8)(in_pass)
        pl.when(few == count // ABREAST * 7 // 8)(out_fourth)
        pl.when(few == count // ABREAST * 7 // 8)(norm_pass)
        for at in range(ABREAST):
            one_channel(few * ABREAST + at)

    small_own[:, :side] = rows_sums[...]
    small_own[:, side : 2 * side] = cols_sums[...]
    lane = lax.broadcasted_iota(jnp.int32, (count, side), 1)
    last = jnp.zeros((count, side), jnp.float32)
    for at, sums in enumerate((skip_sums, bias_sums_ref)):
        last = jnp.where(lane == at, jnp.sum(sums[...], axis=1, keepdims=True), last)
    small_own[:, 2 * side :] = last
    for turn in range(1, shares):
        small_push(turn).start()
    in_fourth()
    def widen(step):
        part = branch_sent_ref if step < early else branch_got
        at = step if step < early else step - early

        @pl.loop(0, n)
        def _(owner):
            for line in range(lines):
                row = (owner * (early + late) + step) * lines + line
                wide[pl.ds(pl.multiple_of(row * count, count), count), :] = part[owner, at, line].astype(jnp.float32)

    own.wait()
    for step in range(early):
        widen(step)
    for step in range(late):
        for shift in range(1, n):
            branch_push(step, shift, True).wait_recv()
            branch_push(step, shift).wait_send()
        widen(early + step)

    @pl.loop(0, count // 4)
    def _(few):
        for at in range(4):
            chan = few * 4 + at
            shifted = wide[pl.ds(chan, side, stride=count), :] + bias_ref[chan]
            image = image_ref[chan].astype(jnp.float32)
            grad_out = jnp.where(inside, cot_ref[chan].astype(jnp.float32), 0.0)
            output_ref[chan] = jnp.where(inside, image + scale_ref[chan] * shifted, 0.0).astype(jnp.bfloat16)
            scale_sums[pl.ds(chan, 1), :] = jnp.sum(grad_out * shifted, axis=0, keepdims=True)

    late_own[...] = jnp.zeros_like(late_own)
    late_own[:, :count] = lane_sums(scale_sums[...])
    for turn in range(1, shares):
        late_push(turn).start()
    total = norm_mid[...]
    for turn in range(1, n):
        norm_second(turn).wait()
        total = total + norm_far[turn]
    norm_ref[...] = total
    out_finish()
    in_finish()
    total = small_own[...]
    for turn in range(1, shares):
        small_push(turn).wait()
        total = total + small_got[turn]
    small_ref[...] = total
    total = late_own[...]
    for turn in range(1, shares):
        late_push(turn).wait()
        total = total + late_got[turn]
    late_ref[...] = total


def mixer_back(n, shares, sizes, images, cotangent, grad, branch_sent, branch, lines, vectors, norms, sums):
    count, side, _ = images.shape
    near = n // 2
    block, channels = sums[0].shape[1:]
    rows = block // near
    wide = sums[1].shape[2]
    line = pltpu.VMEM((count, side), jnp.float32)
    norm = pltpu.VMEM((8, channels), jnp.float32)
    vmem = pl.BlockSpec(memory_space=pltpu.VMEM)
    hbm = pl.BlockSpec(memory_space=pl.ANY)
    full = functools.partial(jax.ShapeDtypeStruct, dtype=jnp.float32)
    return pl.pallas_call(
        functools.partial(back_kernel, n, shares),
        out_shape=(
            jax.ShapeDtypeStruct(images.shape, jnp.bfloat16),
            full(images.shape),
            full((count, 3 * side)),
            full((8, side)),
            full((8, channels)),
            jax.ShapeDtypeStruct((shares, rows, channels), jnp.bfloat16),
            jax.ShapeDtypeStruct((shares, rows, wide), jnp.bfloat16),
        ),
        in_specs=[pl.BlockSpec(memory_space=pltpu.SMEM)]
        + [hbm] * 5
        + [vmem] * len(lines)
        + [pl.BlockSpec(memory_space=pltpu.SMEM)] * len(vectors)
        + [vmem] * len(norms)
        + [hbm] * 2,
        out_specs=(vmem,) * 5 + (hbm,) * 2,
        scratch_shapes=[
            pltpu.VMEM((count * side, side), jnp.float32),
            pltpu.VMEM(branch.shape, jnp.bfloat16),
            line,
            line,
            line,
            line,
            pltpu.VMEM((count, 3 * side), jnp.float32),
            pltpu.VMEM((shares, count, 3 * side), jnp.float32),
            pltpu.VMEM((8, side), jnp.float32),
            pltpu.VMEM((shares, 8, side), jnp.float32),
            norm,
            pltpu.VMEM((shares, 8, channels), jnp.float32),
            norm,
            pltpu.VMEM((n, 8, channels), jnp.float32),
            pltpu.VMEM(sums[1].shape, jnp.bfloat16),
            *(pltpu.VMEM(whole.shape, whole.dtype) for whole in (images, cotangent, grad, branch_sent, sums[0])),
            pltpu.SemaphoreType.DMA((5,)),
        ]
        + [
            kind
            for columns in (channels, wide)
            for kind in (
                pltpu.VMEM((near, rows, columns), jnp.bfloat16),
                pltpu.VMEM((near, rows, columns), jnp.bfloat16),
                pltpu.VMEM((rows, columns), jnp.float32),
                pltpu.VMEM((rows, columns), jnp.bfloat16),
            )
        ]
        + [
            pltpu.SemaphoreType.DMA(size if isinstance(size, tuple) else (size,))
            for size in ((branch.shape[1], n), (branch.shape[1], n), 1, *(shares,) * 8, n, n)
            + (near, near, shares, shares, 1) * 2
        ],
        compiler_params=pltpu.CompilerParams(
            collective_id=2, has_side_effects=True, vmem_limit_bytes=62 * mebi
        ),
        name="mixer_back",
    )(sizes, images, cotangent, grad, branch_sent, branch, *lines, *vectors, *norms, *sums)


def taps_kernel(small_ref, *refs):
    params, (*grads, rest_ref), wide, turned = refs[:8], refs[8:17], refs[17], refs[18]
    count = small_ref.shape[0]
    side = wide.shape[0]
    wide[...] = jnp.zeros_like(wide)

    def turn(at):
        wide[:count, :] = small_ref[:, at * side : (at + 1) * side]
        turned[...] = wide[...].T

    def rows_load(lag):
        return turned[pl.ds(lax.rem(lag + side - 1, side), 1), :count]

    def cols_load(lag):
        return turned[pl.ds(side - 1 - lag, 1), :count]

    for at, load in enumerate((rows_load, cols_load)):
        turn(at)
        found = taps_adjoint(*(ref[...] for ref in params[4 * at : 4 * at + 4]), side, load)
        for ref, grad in zip(grads[4 * at : 4 * at + 4], found):
            ref[...] = grad
    turn(2)
    rest_ref[...] = turned[:8, :count]


def taps_back(small, params, side):
    modes, count = params[0].shape
    full = functools.partial(jax.ShapeDtypeStruct, dtype=jnp.float32)
    vmem = pl.BlockSpec(memory_space=pltpu.VMEM)
    return pl.pallas_call(
        taps_kernel,
        out_shape=(full((modes, count)),) * 8 + (full((8, count)),),
        in_specs=[vmem] * 9,
        out_specs=(vmem,) * 9,
        scratch_shapes=[pltpu.VMEM((side, side), jnp.float32), pltpu.VMEM((side, side), jnp.float32)],
        name="taps_back",
    )(small, *params)


def pixel_body(
    n,
    images,
    cotangent,
    image_sizes,
    slot_image,
    rows_rate,
    rows_freq,
    rows_real,
    rows_imag,
    cols_rate,
    cols_freq,
    cols_real,
    cols_imag,
    skip_gain,
    norm_gain,
    norm_bias,
    weight_in,
    bias_in,
    weight_out,
    bias_out,
    layer_scale,
):
    _, count, side, _ = images.shape
    channels = norm_gain.shape[0]
    picked = slot_image[lax.axis_index("dp")]
    sizes = image_sizes[picked]
    image, cot = images[0], cotangent[0]

    params = tuple(
        param.T
        for param in (
            rows_rate,
            rows_freq,
            rows_real,
            rows_imag,
            cols_rate,
            cols_freq,
            cols_real,
            cols_imag,
        )
    )
    shares = lax.axis_size("dp")
    hidden = weight_out.shape[0]
    spread = jnp.broadcast_to(bias_in[:, None], (hidden, side))
    in_part = jnp.concatenate([weight_in.T, spread], axis=1).reshape(shares, -1, channels + side)
    out_part = weight_out.reshape(shares, -1, channels)
    mixed, first, back, in_whole, out_whole, bias_out_sums, rows_back, rows, cols_back, _ = mixer_forward(
        n, shares, sizes, image, cot, skip_gain, layer_scale, params, in_part, out_part
    )
    grad, branch_sent, branch, _, _, *sums, gain_sums, shift_sums = mlp(
        n,
        shares,
        mixed,
        first,
        back,
        in_whole.reshape(-1, channels + side),
        out_whole.reshape(-1, channels),
        jnp.broadcast_to(norm_gain[:, None], (channels, side)),
        jnp.broadcast_to(norm_bias[:, None], (channels, side)),
    )
    output, input_grad, small, late, norms, out_final, in_final = mixer_back(
        n,
        shares,
        sizes,
        image,
        cot,
        grad.reshape(side, count, side),
        branch_sent,
        branch,
        (rows_back, rows, cols_back),
        (skip_gain, layer_scale, bias_out),
        (bias_out_sums, gain_sums, shift_sums),
        sums,
    )
    *params_grad, rest = taps_back(small, params, side)
    in_final = in_final.reshape(hidden, channels + side).astype(jnp.float32)
    return (
        output[None],
        input_grad[None],
        *(grad.T for grad in params_grad),
        rest[0],
        norms[0],
        norms[1],
        in_final[:, :channels].T,
        jnp.sum(in_final[:, channels:], axis=1),
        out_final.reshape(hidden, channels).astype(jnp.float32),
        rest[1],
        late[0, :count],
    )


def choose_body(n, images, *rest):
    slots, count, side, _ = images.shape
    fits = (
        slots == 1
        and side == 128
        and count <= side
        and count % GROUP == 0
        and side % (4 * n * LINES) == 0
        and n % 2 == 0
        and (rest[15].shape[0] * n) % STEP_HIDDEN == 0
        and rest[15].shape[0] % (16 * lax.axis_size("dp")) == 0
        and lax.axis_size("dp") > 1
    )
    return pixel_body(n, images, *rest) if fits else plain_body(images, *rest)


def solution(mesh):
    in_specs = (
        P("dp", "chan", None, None),
        P("dp", "chan", None, None),
        P(),
        P(),
        P("chan", None),
        P("chan", None),
        P("chan", None),
        P("chan", None),
        P("chan", None),
        P("chan", None),
        P("chan", None),
        P("chan", None),
        P("chan"),
        P(),
        P(),
        P(None, "chan"),
        P("chan"),
        P("chan", None),
        P("chan"),
        P("chan"),
    )
    out_specs = (
        P("dp", "chan", None, None),
        P("dp", "chan", None, None),
        P("chan", None),
        P("chan", None),
        P("chan", None),
        P("chan", None),
        P("chan", None),
        P("chan", None),
        P("chan", None),
        P("chan", None),
        P("chan"),
        P(),
        P(),
        P(None, "chan"),
        P("chan"),
        P("chan", None),
        P("chan"),
        P("chan"),
    )
    return jax.shard_map(functools.partial(choose_body, mesh.shape["chan"]), mesh=mesh, in_specs=in_specs, out_specs=out_specs, check_vma=False)
```

```python
import functools

import jax
import jax.numpy as jnp
from jax import lax
from jax.experimental import pallas as pl
from jax.experimental.pallas import tpu as pltpu
from jax.sharding import PartitionSpec as P

eps_norm = 1e-06
highest = lax.Precision.HIGHEST


def kernel_taps(rate_vals, freq_vals, real_part, imag_part, length):
    offsets = jnp.arange(length, dtype=jnp.float32)
    decays = jnp.exp(-rate_vals[:, :, None] * offsets)
    angles = freq_vals[:, :, None] * offsets
    return jnp.sum(
        decays
        * (real_part[:, :, None] * jnp.cos(angles) - imag_part[:, :, None] * jnp.sin(angles)),
        axis=1,
    )


def toeplitz(filter_taps):
    length = filter_taps.shape[1]
    offsets = jnp.arange(length, dtype=jnp.int32)
    lag_index = offsets[:, None] - offsets[None, :]
    return jnp.where(lag_index[None] >= 0, filter_taps[:, jnp.maximum(lag_index, 0)], 0.0)


def mixer(
    masked_in,
    rows_rate,
    rows_freq,
    rows_real,
    rows_imag,
    cols_rate,
    cols_freq,
    cols_real,
    cols_imag,
    skip_gain,
):
    rows_op = toeplitz(kernel_taps(rows_rate, rows_freq, rows_real, rows_imag, masked_in.shape[2]))
    cols_op = toeplitz(kernel_taps(cols_rate, cols_freq, cols_real, cols_imag, masked_in.shape[3]))
    along_rows = jnp.einsum("chi,ncij->nchj", rows_op, masked_in, precision=highest)
    return (
        jnp.einsum("nchj,cwj->nchw", along_rows, cols_op, precision=highest)
        + skip_gain[None, :, None, None] * masked_in
    )


def normalize(values, norm_gain, norm_bias):
    center = values - jnp.mean(values, axis=-2, keepdims=True)
    inverse = lax.rsqrt(jnp.mean(center * center, axis=-2, keepdims=True) + eps_norm)
    scaled = center * inverse
    return (scaled * norm_gain[:, None] + norm_bias[:, None], scaled, inverse)


def gelu_exact(values):
    return jax.nn.gelu(values, approximate=False)


def plain_body(
    images,
    cotangent,
    image_sizes,
    slot_image,
    rows_rate,
    rows_freq,
    rows_real,
    rows_imag,
    cols_rate,
    cols_freq,
    cols_real,
    cols_imag,
    skip_gain,
    norm_gain,
    norm_bias,
    weight_in,
    bias_in,
    weight_out,
    bias_out,
    layer_scale,
):
    slot_count, chan_count, length = (images.shape[0], images.shape[1], images.shape[2])
    pixels = length * length
    image_count = slot_image.shape[0]
    slot_ids = lax.axis_index("dp") * slot_count + jnp.arange(slot_count, dtype=jnp.int32)
    choose = (slot_ids[:, None] == jnp.arange(image_count, dtype=jnp.int32)[None, :]).astype(
        jnp.int32
    )
    picked = jnp.sum(choose * slot_image[None, :], axis=1)
    owners = (picked[:, None] == jnp.arange(image_count, dtype=jnp.int32)[None, :]).astype(
        jnp.int32
    )
    heights = jnp.sum(owners * image_sizes[None, :, 0], axis=1)
    widths = jnp.sum(owners * image_sizes[None, :, 1], axis=1)
    offsets = jnp.arange(length, dtype=jnp.int32)
    inside = (
        (offsets[None, :, None] < heights[:, None, None])
        & (offsets[None, None, :] < widths[:, None, None])
    ).astype(jnp.float32)
    masked_in = images.astype(jnp.float32) * inside[:, None]
    mixed_out, mixer_pull = jax.vjp(
        mixer,
        masked_in,
        rows_rate,
        rows_freq,
        rows_real,
        rows_imag,
        cols_rate,
        cols_freq,
        cols_real,
        cols_imag,
        skip_gain,
    )
    mixed_low = mixed_out.astype(jnp.bfloat16).reshape(slot_count, chan_count, pixels)
    mask_flat = inside.reshape(slot_count, 1, pixels)
    residual = images.astype(jnp.float32).reshape(slot_count, chan_count, pixels)
    grad_out = cotangent.astype(jnp.float32).reshape(slot_count, chan_count, pixels) * mask_flat
    chan_offset = lax.axis_index("chan") * chan_count
    all_channels = norm_gain.shape[0]
    slot_item = 0
    gathered = lax.all_gather(mixed_low[slot_item], "chan", axis=0, tiled=True)
    normed, scaled, inverse = normalize(gathered.astype(jnp.float32), norm_gain, norm_bias)
    normed_low = normed.astype(jnp.bfloat16)
    before = (
        jnp.einsum("cf,cp->fp", weight_in, normed_low, preferred_element_type=jnp.float32)
        + bias_in.astype(jnp.float32)[:, None]
    )
    active = gelu_exact(before).astype(jnp.bfloat16)

    def project(first_row, row_count, active=active):
        return jnp.einsum("fc,fp->cp", weight_out, active, preferred_element_type=jnp.float32)

    branch_list = [
        lax.psum_scatter(
            project(jnp.int32(0), chan_count * lax.axis_size("chan")),
            "chan",
            scatter_dimension=0,
            tiled=True,
        )
    ]
    scaled_part = lax.dynamic_slice_in_dim(scaled, chan_offset, chan_count, 0)
    stored = [(normed_low, before, active, scaled_part, inverse)]
    branch_all = jnp.stack(branch_list)
    shifted = branch_all + bias_out[None, :, None]
    output = (
        (mask_flat * (residual + layer_scale[None, :, None] * shifted))
        .astype(jnp.bfloat16)
        .reshape(images.shape)
    )
    scale_grad = jnp.sum(grad_out * shifted, axis=(0, 2))
    branch_grad = layer_scale[None, :, None] * grad_out
    bias_out_grad = jnp.sum(branch_grad, axis=(0, 2))
    branch_low = branch_grad.astype(jnp.bfloat16)
    hidden_count = weight_in.shape[1]
    out_weight_grad = jnp.zeros((hidden_count, all_channels), jnp.float32)
    gain_shard = lax.dynamic_slice_in_dim(norm_gain, chan_offset, chan_count, 0)
    slot_item = 0
    normed_low, before, active, scaled_part, inverse = stored[slot_item]

    def absorb(totals, shard_rows, first_row, active=active):
        hidden_grad = jnp.einsum(
            "fc,cp->fp", weight_out, shard_rows, preferred_element_type=jnp.float32
        )
        product_part = jnp.einsum(
            "fp,cp->fc", active, shard_rows, preferred_element_type=jnp.float32
        )
        return (hidden_grad, product_part)

    hidden_start = jnp.zeros((hidden_count, pixels), jnp.float32)
    hidden_grad, out_weight_grad = absorb(
        (hidden_start, out_weight_grad),
        lax.all_gather(branch_low[slot_item], "chan", axis=0, tiled=True),
        jnp.int32(0),
    )
    gelu_pull = jax.vjp(gelu_exact, before)[1]
    before_grad = gelu_pull(hidden_grad)[0].astype(jnp.bfloat16)
    in_weight_grad = jnp.einsum(
        "cp,fp->cf", normed_low, before_grad, preferred_element_type=jnp.float32
    )
    in_bias_grad = jnp.sum(before_grad.astype(jnp.float32), axis=1)

    def spread_back(first_row, row_count, before_grad=before_grad):
        return jnp.einsum("cf,fp->cp", weight_in, before_grad, preferred_element_type=jnp.float32)

    normed_grad = lax.psum_scatter(
        spread_back(jnp.int32(0), chan_count * lax.axis_size("chan")),
        "chan",
        scatter_dimension=0,
        tiled=True,
    )
    weighted = normed_grad * gain_shard[:, None]
    pixel_sums = (
        lax.psum(jnp.sum(weighted, axis=0).astype(jnp.bfloat16), "chan").astype(jnp.float32),
        lax.psum(jnp.sum(weighted * scaled_part, axis=0).astype(jnp.bfloat16), "chan").astype(
            jnp.float32
        ),
    )
    mixed_grads = [
        inverse
        * (
            weighted
            - pixel_sums[0][None, :] / all_channels
            - scaled_part * pixel_sums[1][None, :] / all_channels
        )
    ]
    gain_part = jnp.sum(normed_grad * scaled_part, axis=1)
    shift_part = jnp.sum(normed_grad, axis=1)
    mixed_grad_all = jnp.stack(mixed_grads)
    gain_grad = lax.dynamic_update_slice_in_dim(
        jnp.zeros((all_channels,), jnp.float32), gain_part, chan_offset, 0
    )
    shift_grad = lax.dynamic_update_slice_in_dim(
        jnp.zeros((all_channels,), jnp.float32), shift_part, chan_offset, 0
    )
    pulled = mixer_pull(mixed_grad_all.reshape(images.shape))
    input_grad = inside[:, None] * (cotangent.astype(jnp.float32) + pulled[0])
    summed = lax.psum(
        (
            in_weight_grad,
            out_weight_grad,
            in_bias_grad,
            bias_out_grad,
            scale_grad,
            pulled[1],
            pulled[2],
            pulled[3],
            pulled[4],
            pulled[5],
            pulled[6],
            pulled[7],
            pulled[8],
            pulled[9],
        ),
        "dp",
    )
    norm_sums = lax.psum((gain_grad, shift_grad), ("dp", "chan"))
    return (
        output,
        input_grad,
        summed[5],
        summed[6],
        summed[7],
        summed[8],
        summed[9],
        summed[10],
        summed[11],
        summed[12],
        summed[13],
        norm_sums[0],
        norm_sums[1],
        summed[0],
        summed[2],
        summed[1],
        summed[3],
        summed[4],
    )


MESH = pl.DeviceIdType.MESH
GROUP = 16
ABREAST = 2
LINES = 4
STEP_HIDDEN = 512
mebi = 1024 * 1024


def dot_nn(left, right):
    return lax.dot_general(left, right, (((1,), (0,)), ((), ())), preferred_element_type=jnp.float32)


def dot_nt(left, right):
    return lax.dot_general(left, right, (((1,), (1,)), ((), ())), preferred_element_type=jnp.float32)


def dot_tn(left, right):
    return lax.dot_general(left, right, (((0,), (0,)), ((), ())), preferred_element_type=jnp.float32)


def split_low(values):
    high = values.astype(jnp.bfloat16)
    return high, (values - high.astype(jnp.float32)).astype(jnp.bfloat16)


def lag_matrix(line, side, keep):
    spread = pltpu.roll(jnp.broadcast_to(line, (side, side)), 0, 1, stride=1, stride_axis=0)
    return jnp.where(keep, spread, 0.0)


def lag_sums(matrix, side, keep):
    turned = pltpu.roll(jnp.where(keep, matrix, 0.0), 0, 1, stride=1, stride_axis=0)
    return jnp.sum(turned, axis=0, keepdims=True)


cos_terms = (
    1.0, -19.7392087, 64.9393891, -85.4566583, 60.242131, -26.4046662, 7.8001253, -1.45310477
)
sin_terms = (6.2831853, -41.3417004, 81.6051314, -76.703015, 42.0259236, -14.8998335, 3.23811835)


def polynomial(terms, at):
    value = terms[-1]
    for term in terms[-2::-1]:
        value = value * at + term
    return value


TILE = 16


def power(rate, freq, lag):
    angle = freq * 0.15915494309189535 * lag
    angle = angle - jnp.floor(angle + 0.5)
    square = angle * angle
    decay = jnp.exp(-rate * lag)
    return decay * polynomial(cos_terms, square), decay * (angle * polynomial(sin_terms, square))


def product(left, right):
    return left[0] * right[0] - left[1] * right[1], left[0] * right[1] + left[1] * right[0]


def taps_lines(rate, freq, real, imag, side, store):
    first = power(rate, freq, 1.0)

    @pl.loop(0, side // TILE)
    def _(tile):
        state = product((real, imag), power(rate, freq, (tile * TILE).astype(jnp.float32)))
        for step in range(TILE):
            store(tile * TILE + step, jnp.sum(state[0], axis=0, keepdims=True))
            state = product(state, first)


def taps_adjoint(rate, freq, real, imag, side, load):
    first = power(rate, freq, 1.0)

    def tile_sums(tile, totals):
        state = power(rate, freq, (tile * TILE).astype(jnp.float32))
        even, odd, even_lag, odd_lag = totals
        for step in range(TILE):
            grad = load(tile * TILE + step)
            late = grad * (tile * TILE + step).astype(jnp.float32)
            even = even + grad * state[0]
            odd = odd + grad * state[1]
            even_lag = even_lag + late * state[0]
            odd_lag = odd_lag + late * state[1]
            state = product(state, first)
        return even, odd, even_lag, odd_lag

    zero = jnp.zeros_like(rate)
    even, odd, even_lag, odd_lag = lax.fori_loop(0, side // TILE, tile_sums, (zero,) * 4)
    return imag * odd_lag - real * even_lag, -real * odd_lag - imag * even_lag, even, -odd


def lane_sums(values):
    ones = jnp.ones((8, values.shape[1]), jnp.bfloat16)
    high, rest = split_low(values)
    low = (values - high.astype(jnp.float32) - rest.astype(jnp.float32)).astype(jnp.bfloat16)
    return dot_nt(ones, high) + dot_nt(ones, rest) + dot_nt(ones, low)


def meet(n, shares):
    me, share = lax.axis_index("chan"), lax.axis_index("dp")
    barrier = pltpu.get_barrier_semaphore()
    for shift in range(1, n):
        pl.semaphore_signal(
            barrier, inc=1, device_id={"chan": lax.rem(me + shift, n)}, device_id_type=MESH
        )
    for shift in range(1, shares):
        pl.semaphore_signal(
            barrier, inc=1, device_id={"dp": lax.rem(share + shift, shares)}, device_id_type=MESH
        )
    pl.semaphore_wait(barrier, n + shares - 2)
    return me, share


def push(source, target, send_sem, recv_sem, **peer):
    return pltpu.make_async_remote_copy(
        src_ref=source,
        dst_ref=target,
        send_sem=send_sem,
        recv_sem=recv_sem,
        device_id=peer,
        device_id_type=MESH,
    )


def weight_rounds(n, shares, me, share, pairs, sems):
    far = me // 2
    core = lax.rem(me, 2)
    mate = far + 1 - 2 * lax.rem(far, 2)
    mine = far // 2 * 2
    beyond = 2 - mine
    inner = lax.rem(far + 1, 4) >= 2
    own_sem, send1, recv1, send2, recv2, send3, recv3 = sems
    both = range(len(pairs))
    origins = (mate, beyond, beyond + 1)

    def own(at):
        local, whole = pairs[at]
        return pltpu.make_async_copy(local, whole.at[core, :, far], own_sem.at[at])

    def first(at, back=False):
        local, whole = pairs[at]
        return push(
            local.at[share],
            whole.at[core, share, mate if back else far],
            send1.at[at, 0],
            recv1.at[at, 0],
            chan=mate * 2 + core,
        )

    def across(at, half, back=False):
        whole = pairs[at][1]
        return push(
            whole.at[core, share, mine + half],
            whole.at[core, share, (beyond if back else mine) + half],
            send1.at[at, 1 + half],
            recv1.at[at, 1 + half],
            chan=(3 - far) * 2 + core,
        )

    def onward(at, half):
        block = pairs[at][1].at[core, share, beyond + half]
        return push(block, block, send1.at[at, 3 + half], recv1.at[at, 1 + half], chan=mate * 2 + core)

    def second(at, place, turn, back=False):
        whole = pairs[at][1]
        holder = lax.rem(share + shares - turn, shares) if back else share
        return push(
            whole.at[core, share, origins[place]],
            whole.at[core, holder, origins[place]],
            send2.at[at, place, turn],
            recv2.at[at, place, turn],
            dp=lax.rem(share + turn, shares),
        )

    def third(at, back=False):
        whole = pairs[at][1]
        return push(
            whole.at[core], whole.at[1 - core if back else core], send3.at[at], recv3.at[at], chan=far * 2 + 1 - core
        )

    def start_second(at, place):
        for turn in range(1, shares):
            second(at, place, turn).start()

    def start_first():
        for at in both:
            own(at).start()
            first(at).start()

    def start_across():
        for at in both:
            own(at).wait()
            first(at, True).wait_recv()

            @pl.when(inner)
            def _():
                for half in range(2):
                    across(at, half).start()

            start_second(at, 0)

    def start_onward():
        @pl.when(inner)
        def _():
            for at in both:
                for half in range(2):
                    across(at, half, True).wait_recv()
                    onward(at, half).start()
                    start_second(at, 1 + half)

    def start_last():
        @pl.when(jnp.logical_not(inner))
        def _():
            for at in both:
                for half in range(2):
                    across(at, half, True).wait_recv()
                    start_second(at, 1 + half)

    def start_third():
        for at in both:
            for place in range(3):
                for turn in range(1, shares):
                    second(at, place, turn, True).wait_recv()
            third(at).start()

    def finish():
        for at in both:
            third(at, True).wait_recv()
            third(at).wait_send()
            first(at).wait_send()
            for place in range(3):
                for turn in range(1, shares):
                    second(at, place, turn).wait_send()

            @pl.when(inner)
            def _():
                for half in range(2):
                    across(at, half).wait_send()
                    onward(at, half).wait_send()

    return start_first, start_across, start_onward, start_last, start_third, finish


def send_part(stage, target, me, peer, part, send_sem, recv_sem, shift):
    return pltpu.make_async_remote_copy(
        src_ref=stage.at[peer, part],
        dst_ref=target.at[me, part],
        send_sem=send_sem.at[shift],
        recv_sem=recv_sem.at[shift],
        device_id={"chan": peer},
        device_id_type=MESH,
    )


def wait_parts(stage, target, me, n, send_sem, recv_sem):
    for shift in range(1, n):
        peer = lax.rem(me + shift, n)
        origin = lax.rem(me + n - shift, n)
        pltpu.make_async_remote_copy(
            src_ref=stage.at[peer],
            dst_ref=target.at[origin],
            send_sem=send_sem.at[shift],
            recv_sem=recv_sem.at[shift],
            device_id={"chan": peer},
            device_id_type=MESH,
        ).wait()


def mixer_kernel(
    n,
    shares,
    sizes_ref,
    image_ref,
    cot_ref,
    skip_ref,
    scale_ref,
    *rest,
):
    mixer_body(n, shares, sizes_ref, image_ref, cot_ref, skip_ref, scale_ref, rest[:8], *rest[8:])


def mixer_body(
    n,
    shares,
    sizes_ref,
    image_ref,
    cot_ref,
    skip_ref,
    scale_ref,
    param_refs,
    in_part_ref,
    out_part_ref,
    mixed_ref,
    first_ref,
    back_ref,
    in_whole_ref,
    out_whole_ref,
    sums_ref,
    rows_back_ref,
    rows_ref,
    cols_back_ref,
    cols_ref,
    mixed_stage,
    back_stage,
    wide,
    taps,
    params_got,
    params_sem,
    send_m,
    recv_m,
    send_b,
    recv_b,
    own_sem,
    keep_sem,
    *weight_sems,
):
    count, side, _ = image_ref.shape
    parts = count // GROUP
    block = side // n
    me, share = meet(n, shares)
    start_first, start_across, start_onward, start_last, start_third, finish = weight_rounds(
        n, shares, me, share, ((in_part_ref, in_whole_ref), (out_part_ref, out_whole_ref)), weight_sems
    )
    start_first()
    param_copies = [
        pltpu.make_async_copy(ref, params_got.at[at], params_sem.at[at]) for at, ref in enumerate(param_refs)
    ]
    for copy in param_copies:
        copy.start()
    taps[...] = jnp.zeros_like(taps)
    row_at = lax.broadcasted_iota(jnp.int32, (side, side), 0)
    col_at = lax.broadcasted_iota(jnp.int32, (side, side), 1)
    inside = (row_at < sizes_ref[0]) & (col_at < sizes_ref[1])
    lower = row_at >= col_at
    upper = row_at <= col_at

    def turn(stage, part):
        @pl.loop(0, n)
        def _(owner):
            for line in range(block):
                tile = wide[pl.ds(owner * block + line, GROUP, stride=side), :]
                stage[owner, part, line] = tile.astype(jnp.bfloat16)

    def send(stage, target, part, send_sem, recv_sem):
        for shift in range(1, n):
            send_part(stage, target, me, lax.rem(me + shift, n), part, send_sem, recv_sem, shift).start()

    def own_back(part):
        return pltpu.make_async_copy(back_stage.at[:, part], back_ref.at[:, part], keep_sem.at[part])

    def first_push(shift, back=False):
        peer = lax.rem(me + shift, n)
        return push(
            back_stage.at[peer, :, pl.ds(0, LINES)],
            first_ref.at[lax.rem(me + n - shift, n) if back else me],
            send_b.at[shift],
            recv_b.at[shift],
            chan=peer,
        )

    for copy in param_copies:
        copy.wait()
    for axis, (back_out, out) in enumerate(((rows_back_ref, rows_ref), (cols_back_ref, cols_ref))):

        def store(lag, line):
            taps[0, pl.ds(lax.rem(side - lag, side), 1), :count] = line
            taps[1, pl.ds(lag, 1), :count] = line

        taps_lines(*(params_got[4 * axis + at] for at in range(4)), side, store)
        back_out[...] = taps[0].T[:count]
        out[...] = taps[1].T[:count]


    @pl.loop(0, parts)
    def _(part):
        pl.when(part == 1)(start_across)
        pl.when(part == parts * 2 // 3)(start_onward)

        def one_channel(item):
            chan = part * GROUP + item
            masked = jnp.where(inside, image_ref[chan].astype(jnp.float32), 0.0)
            masked_low = masked.astype(jnp.bfloat16)
            rows_high, rows_low = split_low(lag_matrix(rows_back_ref[pl.ds(chan, 1), :], side, lower))
            cols_high, cols_low = split_low(lag_matrix(cols_ref[pl.ds(chan, 1), :], side, upper))
            along = dot_nn(
                jnp.concatenate([rows_high, rows_low], axis=1),
                jnp.concatenate([masked_low, masked_low], axis=0),
            )
            along_high, along_low = split_low(along)
            mixed = dot_nn(
                jnp.concatenate([along_high, along_low], axis=1),
                jnp.concatenate([cols_high, cols_high], axis=0),
            ) + dot_nn(along_high, cols_low)
            mixed = mixed + skip_ref[chan] * masked
            wide[pl.ds(pl.multiple_of(item * side, side), side), :] = mixed

        @pl.loop(0, GROUP // ABREAST)
        def _(few):
            for at in range(ABREAST):
                one_channel(few * ABREAST + at)

        turn(mixed_stage, part)
        send(mixed_stage, mixed_ref, part, send_m, recv_m)

    @pl.loop(0, parts)
    def _(part):
        @pl.loop(0, GROUP)
        def _(item):
            chan = part * GROUP + item
            grad_out = jnp.where(inside, cot_ref[chan].astype(jnp.float32), 0.0)
            scaled = grad_out * scale_ref[chan]
            sums_ref[pl.ds(chan, 1), :] = jnp.sum(scaled, axis=0, keepdims=True)
            wide[pl.ds(pl.multiple_of(item * side, side), side), :] = scaled

        turn(back_stage, part)
        own_back(part).start()

    for shift in range(1, n):
        first_push(shift).start()
    own_b = pltpu.make_async_copy(back_stage.at[me, :, pl.ds(0, LINES)], first_ref.at[me], own_sem.at[0])
    own_m = pltpu.make_async_copy(mixed_stage.at[me], mixed_ref.at[me], own_sem.at[1])
    own_b.start()
    own_m.start()
    start_last()
    start_third()
    for part in range(parts):
        own_back(part).wait()
    own_b.wait()
    own_m.wait()
    wait_parts(mixed_stage, mixed_ref, me, n, send_m, recv_m)
    for shift in range(1, n):
        first_push(shift, True).wait_recv()
        first_push(shift).wait_send()
    finish()


def mixer_forward(n, shares, sizes, images, cotangent, skip, scale, params, in_part, out_part):
    near = n // 2
    smem = pl.BlockSpec(memory_space=pltpu.SMEM)
    count, side, _ = images.shape
    line = jax.ShapeDtypeStruct((count, side), jnp.float32)
    shape = (n, count // GROUP, side // n, GROUP, side)
    first_shape = (n, count // GROUP, LINES, GROUP, side)
    vmem = pl.BlockSpec(memory_space=pltpu.VMEM)
    hbm = pl.BlockSpec(memory_space=pl.ANY)
    return pl.pallas_call(
        functools.partial(mixer_kernel, n, shares),
        out_shape=(
            jax.ShapeDtypeStruct(shape, jnp.bfloat16),
            jax.ShapeDtypeStruct(first_shape, jnp.bfloat16),
            jax.ShapeDtypeStruct(shape, jnp.bfloat16),
        )
        + tuple(
            jax.ShapeDtypeStruct((2, shares, near, *part.shape[1:]), jnp.bfloat16)
            for part in (in_part, out_part)
        )
        + (line,) * 5,
        in_specs=[smem] + [vmem] * 2 + [smem] * 2 + [hbm] * 10,
        out_specs=(hbm,) * 5 + (vmem,) * 5,
        scratch_shapes=[
            pltpu.VMEM(shape, jnp.bfloat16),
            pltpu.VMEM(shape, jnp.bfloat16),
            pltpu.VMEM((GROUP * side, side), jnp.float32),
            pltpu.VMEM((2, side, side), jnp.float32),
            pltpu.VMEM((8, *params[0].shape), jnp.float32),
            pltpu.SemaphoreType.DMA((8,)),
            pltpu.SemaphoreType.DMA((n,)),
            pltpu.SemaphoreType.DMA((n,)),
            pltpu.SemaphoreType.DMA((n,)),
            pltpu.SemaphoreType.DMA((n,)),
            pltpu.SemaphoreType.DMA((2,)),
            pltpu.SemaphoreType.DMA((count // GROUP,)),
            pltpu.SemaphoreType.DMA((2,)),
            pltpu.SemaphoreType.DMA((2, 5)),
            pltpu.SemaphoreType.DMA((2, 3)),
            pltpu.SemaphoreType.DMA((2, 3, shares)),
            pltpu.SemaphoreType.DMA((2, 3, shares)),
            pltpu.SemaphoreType.DMA((2,)),
            pltpu.SemaphoreType.DMA((2,)),
        ],
        compiler_params=pltpu.CompilerParams(
            collective_id=0, has_side_effects=True, vmem_limit_bytes=40 * mebi
        ),
        name="mixer_forward",
    )(sizes, images, cotangent, skip, scale, *params, in_part, out_part)


def gelu_parts(value):
    bell = jnp.exp(-0.5 * value * value)
    inner = 1.0 / (1.0 + (0.3275911 * 0.7071067811865476) * jnp.abs(value))
    series = 1.061405429 * inner - 1.453152027
    series = series * inner + 1.421413741
    series = series * inner - 0.284496736
    series = series * inner + 0.254829592
    tail = (0.5 * inner) * series * bell
    return jnp.where(value < 0.0, tail, 1.0 - tail), bell * 0.3989422804014327


def mlp_kernel(
    n,
    shares,
    mixed_hbm,
    first_hbm,
    in_hbm,
    out_hbm,
    gain_ref,
    shift_ref,
    back_ref,
    grad_ref,
    branch_sent_ref,
    branch_ref,
    active_ref,
    before_grad_ref,
    out_take_ref,
    in_half_ref,
    gain_grad_ref,
    shift_grad_ref,
    grad_stage,
    branch_stage,
    active_ring,
    before_ring,
    normed_keep,
    cots_keep,
    scaled_keep,
    inverse_keep,
    branch_sum,
    grad_sum,
    hidden_sum,
    pieces,
    rows_stage,
    out_got,
    in_got,
    back_got,
    mixed_ref,
    first_ref,
    in_ref,
    out_ref,
    load_sem,
    send_g,
    recv_g,
    send_c,
    recv_c,
    send_r,
    recv_r,
    own_sem,
    ring_sem,
    piece_sem,
    send_h,
    recv_h,
    send_2,
    recv_2,
):
    loads = [
        pltpu.make_async_copy(whole, here, load_sem.at[at])
        for at, (whole, here) in enumerate(
            ((mixed_hbm, mixed_ref), (first_hbm, first_ref), (in_hbm, in_ref), (out_hbm, out_ref))
        )
    ]
    for copy in loads:
        copy.start()
    side = mixed_ref.shape[-1]
    groups = mixed_ref.shape[1]
    block = mixed_ref.shape[2]
    hidden, channels = out_ref.shape
    local = channels // n
    steps = block // LINES
    width = LINES * side
    parts = hidden // STEP_HIDDEN
    ring = active_ring.shape[0]
    me, share = meet(n, shares)
    core = lax.rem(me, 2)
    sibling = me + 1 - 2 * core
    early = branch_sent_ref.shape[1]

    def cot_push(step, shift, back=False):
        peer = lax.rem(me + shift, n)
        origin = lax.rem(me + n - shift, n) if back else me
        span = pl.ds(step * LINES, LINES)
        return push(
            back_ref.at[peer, :, span],
            back_got.at[origin, :, span],
            send_c.at[step, shift],
            recv_c.at[step, shift],
            chan=peer,
        )

    def branch_push(shift, back=False):
        peer = lax.rem(me + shift, n)
        return push(
            branch_stage.at[peer, pl.ds(0, early)],
            branch_sent_ref.at[lax.rem(me + n - shift, n) if back else me],
            send_r.at[shift],
            recv_r.at[shift],
            chan=peer,
        )

    for step in range(1, steps):
        for shift in range(1, n):
            cot_push(step, shift).start()
    own_c = pltpu.make_async_copy(back_ref.at[me], back_got.at[me], own_sem.at[2])
    own_c.start()
    for copy in loads:
        copy.wait()
    gain_grad_ref[...] = jnp.zeros_like(gain_grad_ref)
    shift_grad_ref[...] = jnp.zeros_like(shift_grad_ref)
    hidden_sum[...] = jnp.zeros_like(hidden_sum)

    def keeps(turn):
        slot = lax.rem(turn, ring)
        span = pl.ds(pl.multiple_of(lax.rem(turn, parts) * STEP_HIDDEN, STEP_HIDDEN), STEP_HIDDEN)
        return [
            pltpu.make_async_copy(kept.at[slot], whole.at[turn // parts, span], ring_sem.at[at, slot])
            for at, (kept, whole) in enumerate(((active_ring, active_ref), (before_ring, before_grad_ref)))
        ]

    @pl.loop(0, steps)
    def _(step):
        pl.when(step == 1)(own_c.wait)

        @pl.when(step > 0)
        def _():
            for shift in range(1, n):
                cot_push(step, shift, True).wait_recv()

        for line in range(LINES):
            row = step * LINES + line
            lanes = pl.ds(line * side, side)
            order = [(owner, group) for owner in range(n) for group in range(groups)]
            mixed = jnp.concatenate(
                [mixed_ref[owner, group, row].astype(jnp.float32) for owner, group in order], axis=0
            )
            mean = jnp.sum(mixed, axis=0, keepdims=True) * (1.0 / channels)
            center = mixed - mean
            var = jnp.sum(center * center, axis=0, keepdims=True) * (1.0 / channels)
            inverse = lax.rsqrt(var + eps_norm)
            scaled = center * inverse
            normed_keep[step, :, lanes] = (scaled * gain_ref[...] + shift_ref[...]).astype(jnp.bfloat16)
            scaled_keep[:, lanes] = scaled
            inverse_keep[:, lanes] = inverse

            @pl.when(step == 0)
            def _():
                cots_keep[step, :, lanes] = jnp.concatenate(
                    [first_ref[owner, group, line] for owner, group in order], axis=0
                )

            @pl.when(step > 0)
            def _():
                cots_keep[step, :, lanes] = jnp.concatenate(
                    [back_got[owner, group, row] for owner, group in order], axis=0
                )

        @pl.loop(0, parts)
        def _(part):
            turn = step * parts + part
            slot = lax.rem(turn, ring)

            @pl.when(turn >= ring)
            def _():
                for copy in keeps(turn - ring):
                    copy.wait()

            span = pl.ds(pl.multiple_of(part * STEP_HIDDEN, STEP_HIDDEN), STEP_HIDDEN)
            bias = in_ref[span, channels:].astype(jnp.float32)[:, :1]
            before = dot_nn(in_ref[span, :channels], normed_keep[step]) + bias
            inside, bell = gelu_parts(before)
            active = (before * inside).astype(jnp.bfloat16)
            active_grad = dot_nn(out_ref[span, :], cots_keep[step])
            before_grad = (active_grad * (inside + before * bell)).astype(jnp.bfloat16)
            active_ring[slot] = active
            before_ring[slot] = before_grad
            hidden_sum[span, :] += sum(
                before_grad[:, line * side : (line + 1) * side].astype(jnp.float32) for line in range(LINES)
            )
            branch = dot_tn(out_ref[span, :], active)
            grad = dot_tn(in_ref[span, :channels], before_grad)

            @pl.when(part == 0)
            def _():
                branch_sum[...] = branch
                grad_sum[...] = grad

            @pl.when(part > 0)
            def _():
                branch_sum[...] += branch
                grad_sum[...] += grad

            for copy in keeps(turn):
                copy.start()

        for line in range(LINES):
            lanes = pl.ds(line * side, side)
            grad = grad_sum[:, lanes]
            scaled = scaled_keep[:, lanes]
            gain_grad_ref[...] += grad * scaled
            shift_grad_ref[...] += grad
            weighted = grad * gain_ref[...]
            first = jnp.sum(weighted, axis=0, keepdims=True) * (1.0 / channels)
            second = jnp.sum(weighted * scaled, axis=0, keepdims=True) * (1.0 / channels)
            mixed_grad = (inverse_keep[:, lanes] * (weighted - first - scaled * second)).astype(jnp.bfloat16)
            branch = branch_sum[:, lanes].astype(jnp.bfloat16)
            for owner in range(n):
                grad_stage[owner, step, line] = mixed_grad[owner * local : (owner + 1) * local]
                branch_stage[owner, step, line] = branch[owner * local : (owner + 1) * local]

        for shift in range(1, n):
            send_part(grad_stage, grad_ref, me, lax.rem(me + shift, n), step, send_g, recv_g, shift).start()

    own_g = pltpu.make_async_copy(grad_stage.at[me], grad_ref.at[me], own_sem.at[0])
    own_r = pltpu.make_async_copy(branch_stage.at[:, pl.ds(early, steps - early)], branch_ref, own_sem.at[1])
    own_s = pltpu.make_async_copy(branch_stage.at[me, pl.ds(0, early)], branch_sent_ref.at[me], own_sem.at[3])
    for shift in range(1, n):
        branch_push(shift).start()
    own_g.start()
    own_r.start()
    own_s.start()
    turns = steps * parts
    for turn in range(turns - ring, turns):
        for copy in keeps(turn):
            copy.wait()

    block_rows = hidden // 2 // shares
    kinds = (
        (active_ref, cots_keep, out_got, out_take_ref),
        (before_grad_ref, normed_keep, in_got, in_half_ref),
    )

    def block_span(job, base=0):
        at = lax.rem(share + 1 + lax.rem(job, shares), shares)
        return pl.ds(pl.multiple_of(base + at * block_rows, block_rows), block_rows)

    def whole_span(job):
        owner = 1 - core if job < shares else core
        return block_span(job, owner * (hidden // 2))

    def fetch(kind, job, slot):
        return pltpu.make_async_copy(
            kinds[kind][0].at[:, whole_span(job)], pieces.at[slot], piece_sem.at[slot]
        )

    def give(kind, job):
        got = kinds[kind][2]
        return push(
            rows_stage.at[job, :, pl.ds(0, got.shape[1])],
            got.at[block_span(job)],
            send_h.at[kind, job],
            recv_h.at[kind, job],
            chan=sibling,
        )

    def second(kind, job):
        _, _, got, take = kinds[kind]
        turn = job + 1 - shares
        if kind == 1:
            at = lax.rem(share + turn, shares)
            return pltpu.make_async_copy(got.at[block_span(job)], take.at[at], send_2.at[1, turn - 1])
        if turn == shares:
            return pltpu.make_async_copy(got.at[block_span(job)], take.at[0], send_2.at[0, 0])
        return push(
            got.at[block_span(job)],
            take.at[turn],
            send_2.at[kind, turn],
            recv_2.at[kind, turn],
            dp=lax.rem(share + turn, shares),
        )

    jobs = [(kind, job) for kind in range(2) for job in range(2 * shares)]
    fetch(0, 0, 0).start()
    for at, (kind, job) in enumerate(jobs):
        slot = at % 2
        if at + 1 < len(jobs):
            fetch(*jobs[at + 1], (at + 1) % 2).start()
        fetch(kind, job, slot).wait()
        right, got = kinds[kind][1:3]
        total = dot_nt(
            jnp.concatenate([pieces[slot, step] for step in range(steps)], axis=1),
            jnp.concatenate([right[step] for step in range(steps)], axis=1),
        )
        if job < shares:
            rows_stage[job, :, :channels] = total.astype(jnp.bfloat16)
            if kind == 1:
                rows_stage[job, :, channels:] = hidden_sum[whole_span(job), :].astype(jnp.bfloat16)
            give(kind, job).start()
        else:
            give(kind, job - shares).wait()
            span = block_span(job)
            got[span, :channels] = (total + got[span, :channels].astype(jnp.float32)).astype(jnp.bfloat16)
            if kind == 1:
                got[span, channels:] = (
                    hidden_sum[whole_span(job), :] + got[span, channels:].astype(jnp.float32)
                ).astype(jnp.bfloat16)
            second(kind, job).start()
    for kind in range(2):
        for job in range(shares, 2 * shares):
            second(kind, job).wait()
    own_g.wait()
    own_r.wait()
    own_s.wait()
    wait_parts(grad_stage, grad_ref, me, n, send_g, recv_g)
    for shift in range(1, n):
        branch_push(shift, True).wait_recv()
        branch_push(shift).wait_send()
        for step in range(1, steps):
            cot_push(step, shift).wait_send()


def mlp(n, shares, mixed, first, back, in_full, out_full, gain, shift):
    _, groups, block, group, side = mixed.shape
    hidden, channels = out_full.shape
    local = channels // n
    steps = block // LINES
    width = LINES * side
    shape = (n, steps, LINES, local, side)
    ring = 4
    low = functools.partial(jax.ShapeDtypeStruct, dtype=jnp.bfloat16)
    vmem = pl.BlockSpec(memory_space=pltpu.VMEM)
    hbm = pl.BlockSpec(memory_space=pl.ANY)
    return pl.pallas_call(
        functools.partial(mlp_kernel, n, shares),
        out_shape=(
            low(shape),
            low((n, steps // 4, *shape[2:])),
            low((n, steps - steps // 4, *shape[2:])),
            low((steps, hidden, width)),
            low((steps, hidden, width)),
            low((shares, hidden // 2 // shares, channels)),
            low((shares, hidden // 2 // shares, channels + side)),
            jax.ShapeDtypeStruct((channels, side), jnp.float32),
            jax.ShapeDtypeStruct((channels, side), jnp.float32),
        ),
        in_specs=[hbm] * 4 + [vmem] * 2 + [hbm],
        out_specs=(hbm,) * 7 + (vmem, vmem),
        scratch_shapes=[
            pltpu.VMEM(shape, jnp.bfloat16),
            pltpu.VMEM(shape, jnp.bfloat16),
            pltpu.VMEM((ring, STEP_HIDDEN, width), jnp.bfloat16),
            pltpu.VMEM((ring, STEP_HIDDEN, width), jnp.bfloat16),
            pltpu.VMEM((steps, channels, width), jnp.bfloat16),
            pltpu.VMEM((steps, channels, width), jnp.bfloat16),
            pltpu.VMEM((channels, width), jnp.float32),
            pltpu.VMEM((1, width), jnp.float32),
            pltpu.VMEM((channels, width), jnp.float32),
            pltpu.VMEM((channels, width), jnp.float32),
            pltpu.VMEM((hidden, side), jnp.float32),
            pltpu.VMEM((2, steps, hidden // 2 // shares, width), jnp.bfloat16),
            pltpu.VMEM((shares, hidden // 2 // shares, channels + side), jnp.bfloat16),
            pltpu.VMEM((hidden // 2, channels), jnp.bfloat16),
            pltpu.VMEM((hidden // 2, channels + side), jnp.bfloat16),
            pltpu.VMEM(back.shape, jnp.bfloat16),
            *(pltpu.VMEM(whole.shape, whole.dtype) for whole in (mixed, first, in_full, out_full)),
            pltpu.SemaphoreType.DMA((4,)),
            pltpu.SemaphoreType.DMA((n,)),
            pltpu.SemaphoreType.DMA((n,)),
            pltpu.SemaphoreType.DMA((steps, n)),
            pltpu.SemaphoreType.DMA((steps, n)),
            pltpu.SemaphoreType.DMA((n,)),
            pltpu.SemaphoreType.DMA((n,)),
            pltpu.SemaphoreType.DMA((4,)),
            pltpu.SemaphoreType.DMA((2, ring)),
            pltpu.SemaphoreType.DMA((2,)),
            pltpu.SemaphoreType.DMA((2, shares)),
            pltpu.SemaphoreType.DMA((2, shares)),
            pltpu.SemaphoreType.DMA((2, shares)),
            pltpu.SemaphoreType.DMA((2, shares)),
        ],
        compiler_params=pltpu.CompilerParams(
            collective_id=1, has_side_effects=True, vmem_limit_bytes=63 * mebi
        ),
        name="mlp",
    )(mixed, first, in_full, out_full, gain, shift, back)


def sum_rounds(n, shares, me, share, part, final, stage3, take3, keep3, keep4, send3, recv3, send4, recv4, own_sem):
    near, far = n // 2, me // 2
    core = lax.rem(me, 2)

    def third(turn):
        peer = lax.rem(far + turn, near)
        return push(stage3.at[peer], take3.at[turn], send3.at[turn], recv3.at[turn], chan=peer * 2 + core)

    def fourth(turn, back=False):
        holder = lax.rem(share + shares - turn, shares) if back else share
        peer = lax.rem(share + turn, shares)
        return push(keep4, final.at[holder], send4.at[turn], recv4.at[turn], dp=peer)

    def mine():
        return pltpu.make_async_copy(keep4, final.at[share], own_sem.at[0])

    def start_third():
        for at in range(near):
            total = part(at)
            stage3[at] = total.astype(jnp.bfloat16)

            @pl.when(far == at)
            def _():
                keep3[...] = total

        for turn in range(1, near):
            third(turn).start()

    def start_fourth():
        for turn in range(1, near):
            third(turn).wait()
        total = keep3[...]
        for turn in range(1, near):
            total = total + take3[turn].astype(jnp.float32)
        keep4[...] = total.astype(jnp.bfloat16)
        mine().start()
        for turn in range(1, shares):
            fourth(turn).start()

    def finish():
        mine().wait()
        for turn in range(1, shares):
            fourth(turn, True).wait_recv()
            fourth(turn).wait_send()

    return start_third, start_fourth, finish


def back_kernel(
    n,
    shares,
    sizes_ref,
    image_hbm,
    cot_hbm,
    grad_hbm,
    branch_sent_hbm,
    branch_ref,
    rows_back_ref,
    rows_ref,
    cols_back_ref,
    skip_ref,
    scale_ref,
    bias_ref,
    bias_sums_ref,
    gain_sums_ref,
    shift_sums_ref,
    out_take_hbm,
    in_half_ref,
    output_ref,
    input_grad_ref,
    small_ref,
    late_ref,
    norm_ref,
    out_final_ref,
    in_final_ref,
    wide,
    branch_got,
    rows_sums,
    cols_sums,
    skip_sums,
    scale_sums,
    small_own,
    small_got,
    late_own,
    late_got,
    norm_own,
    norm_near,
    norm_mid,
    norm_far,
    in_take,
    image_ref,
    cot_ref,
    grad_ref,
    branch_sent_ref,
    out_take_ref,
    load_sem,
    out_stage3,
    out_take3,
    out_keep3,
    out_keep4,
    in_stage3,
    in_take3,
    in_keep3,
    in_keep4,
    send_sem,
    recv_sem,
    own_sem,
    send_2,
    recv_2,
    send_s,
    recv_s,
    send_l,
    recv_l,
    send_n,
    recv_n,
    send_f,
    recv_f,
    *round_sems,
):
    loads = [
        pltpu.make_async_copy(whole, here, load_sem.at[at])
        for at, (whole, here) in enumerate(
            (
                (out_take_hbm, out_take_ref),
                (grad_hbm, grad_ref),
                (image_hbm, image_ref),
                (cot_hbm, cot_ref),
                (branch_sent_hbm, branch_sent_ref),
            )
        )
    ]
    for copy in loads:
        copy.start()
    count, side, _ = image_ref.shape
    late, lines = branch_ref.shape[1], branch_ref.shape[2]
    early = branch_sent_ref.shape[1]
    near = n // 2
    rows = in_keep3.shape[0]
    me, share = meet(n, shares)

    def summed(take):
        return lambda at: sum(take[turn, at * rows : (at + 1) * rows].astype(jnp.float32) for turn in range(shares))

    out_third, out_fourth, out_finish = sum_rounds(
        n, shares, me, share, summed(out_take_ref), out_final_ref, out_stage3, out_take3, out_keep3, out_keep4, *round_sems[:5]
    )
    in_third, in_fourth, in_finish = sum_rounds(
        n, shares, me, share, summed(in_take), in_final_ref, in_stage3, in_take3, in_keep3, in_keep4, *round_sems[5:]
    )

    def in_second(turn):
        peer = lax.rem(share + turn, shares)
        if turn == 0:
            return pltpu.make_async_copy(in_half_ref.at[peer], in_take.at[0], send_2.at[0])
        return push(in_half_ref.at[peer], in_take.at[turn], send_2.at[turn], recv_2.at[turn], dp=peer)

    def branch_push(step, shift, back=False):
        peer = lax.rem(me + shift, n)
        return push(
            branch_ref.at[peer, step],
            branch_got.at[lax.rem(me + n - shift, n) if back else me, step],
            send_sem.at[step, shift],
            recv_sem.at[step, shift],
            chan=peer,
        )

    def start_branch(step):
        for shift in range(1, n):
            branch_push(step, shift).start()

    def norm_first(turn):
        peer = lax.rem(share + turn, shares)
        return push(norm_own, norm_near.at[turn], send_n.at[turn], recv_n.at[turn], dp=peer)

    def norm_second(turn):
        peer = lax.rem(me + turn, n)
        return push(norm_mid, norm_far.at[turn], send_f.at[turn], recv_f.at[turn], chan=peer)

    def small_push(turn):
        peer = lax.rem(share + turn, shares)
        return push(small_own, small_got.at[turn], send_s.at[turn], recv_s.at[turn], dp=peer)

    def late_push(turn):
        peer = lax.rem(share + turn, shares)
        return push(late_own, late_got.at[turn], send_l.at[turn], recv_l.at[turn], dp=peer)

    def norm_pass():
        total = norm_own[...]
        for turn in range(1, shares):
            norm_first(turn).wait()
            total = total + norm_near[turn]
        norm_mid[...] = total
        for turn in range(1, n):
            norm_second(turn).start()

    def in_pass():
        for turn in range(shares):
            in_second(turn).wait()
        in_third()
        start_branch(late - 1)

    top = lax.broadcasted_iota(jnp.int32, norm_own.shape, 0) == 0
    norm_own[...] = jnp.where(top, lane_sums(gain_sums_ref[...]), lane_sums(shift_sums_ref[...]))
    for turn in range(1, shares):
        norm_first(turn).start()
    for turn in range(shares):
        in_second(turn).start()
    loads[0].wait()
    out_third()
    for step in range(late - 1):
        start_branch(step)
    for copy in loads[1:]:
        copy.wait()
    own = pltpu.make_async_copy(branch_ref.at[me], branch_got.at[me], own_sem.at[0])
    own.start()
    row_at = lax.broadcasted_iota(jnp.int32, (side, side), 0)
    col_at = lax.broadcasted_iota(jnp.int32, (side, side), 1)
    inside = (row_at < sizes_ref[0]) & (col_at < sizes_ref[1])
    lower = row_at >= col_at
    upper = row_at <= col_at
    flip = (row_at + col_at == side - 1).astype(jnp.bfloat16)

    @pl.loop(0, side)
    def _(row):
        span = pl.ds(pl.multiple_of(row * count, count), count)
        wide[span, :] = grad_ref[row].astype(jnp.float32)

    def one_channel(chan):
        one = pl.ds(chan, 1)
        grad = wide[pl.ds(chan, side, stride=count), :]
        image = image_ref[chan].astype(jnp.float32)
        grad_out = jnp.where(inside, cot_ref[chan].astype(jnp.float32), 0.0)
        masked = jnp.where(inside, image, 0.0)
        skip_sums[one, :] = jnp.sum(grad * masked, axis=0, keepdims=True)
        masked_low = masked.astype(jnp.bfloat16)
        grad_low = grad.astype(jnp.bfloat16)
        grad_turned = dot_nt(flip, grad_low).astype(jnp.bfloat16)
        masked_turned = dot_nn(flip, masked_low).astype(jnp.bfloat16)
        rows_high, rows_low = split_low(lag_matrix(rows_back_ref[one, :], side, lower))
        turned_high, turned_low = split_low(lag_matrix(rows_ref[one, :], side, upper))
        cols_high, cols_low = split_low(lag_matrix(cols_back_ref[one, :], side, lower))
        along = dot_nn(
            jnp.concatenate([rows_high, rows_low], axis=1),
            jnp.concatenate([masked_low, masked_low], axis=0),
        )
        along_grad = dot_nn(
            jnp.concatenate([grad_low, grad_low], axis=1),
            jnp.concatenate([cols_high, cols_low], axis=0),
        )
        along_high, along_low = split_low(along)
        grad_high, grad_rest = split_low(along_grad)
        cols_grad = dot_nn(
            jnp.concatenate([grad_turned, grad_turned], axis=1),
            jnp.concatenate([along_high, along_low], axis=0),
        )
        rows_grad = dot_nt(
            jnp.concatenate([grad_high, grad_rest], axis=1),
            jnp.concatenate([masked_turned, masked_turned], axis=1),
        )
        masked_grad = dot_nn(
            jnp.concatenate([turned_high, turned_low], axis=1),
            jnp.concatenate([grad_high, grad_high], axis=0),
        ) + dot_nn(turned_high, grad_rest)
        masked_grad = masked_grad + skip_ref[chan] * grad
        input_grad_ref[chan] = jnp.where(inside, grad_out + masked_grad, 0.0)
        rows_sums[one, :] = lag_sums(rows_grad, side, row_at + col_at >= side - 1)
        cols_sums[one, :] = lag_sums(cols_grad, side, row_at + col_at <= side - 1)

    @pl.loop(0, count // ABREAST)
    def _(few):
        pl.when(few == count // ABREAST * 7 // 8)(in_pass)
        pl.when(few == count // ABREAST * 7 // 8)(out_fourth)
        pl.when(few == count // ABREAST * 7 // 8)(norm_pass)
        for at in range(ABREAST):
            one_channel(few * ABREAST + at)

    small_own[:, :side] = rows_sums[...]
    small_own[:, side : 2 * side] = cols_sums[...]
    lane = lax.broadcasted_iota(jnp.int32, (count, side), 1)
    last = jnp.zeros((count, side), jnp.float32)
    for at, sums in enumerate((skip_sums, bias_sums_ref)):
        last = jnp.where(lane == at, jnp.sum(sums[...], axis=1, keepdims=True), last)
    small_own[:, 2 * side :] = last
    for turn in range(1, shares):
        small_push(turn).start()
    in_fourth()
    def widen(step):
        part = branch_sent_ref if step < early else branch_got
        at = step if step < early else step - early

        @pl.loop(0, n)
        def _(owner):
            for line in range(lines):
                row = (owner * (early + late) + step) * lines + line
                wide[pl.ds(pl.multiple_of(row * count, count), count), :] = part[owner, at, line].astype(jnp.float32)

    own.wait()
    for step in range(early):
        widen(step)
    for step in range(late):
        for shift in range(1, n):
            branch_push(step, shift, True).wait_recv()
            branch_push(step, shift).wait_send()
        widen(early + step)

    @pl.loop(0, count // 4)
    def _(few):
        for at in range(4):
            chan = few * 4 + at
            shifted = wide[pl.ds(chan, side, stride=count), :] + bias_ref[chan]
            image = image_ref[chan].astype(jnp.float32)
            grad_out = jnp.where(inside, cot_ref[chan].astype(jnp.float32), 0.0)
            output_ref[chan] = jnp.where(inside, image + scale_ref[chan] * shifted, 0.0).astype(jnp.bfloat16)
            scale_sums[pl.ds(chan, 1), :] = jnp.sum(grad_out * shifted, axis=0, keepdims=True)

    late_own[...] = jnp.zeros_like(late_own)
    late_own[:, :count] = lane_sums(scale_sums[...])
    for turn in range(1, shares):
        late_push(turn).start()
    total = norm_mid[...]
    for turn in range(1, n):
        norm_second(turn).wait()
        total = total + norm_far[turn]
    norm_ref[...] = total
    out_finish()
    in_finish()
    total = small_own[...]
    for turn in range(1, shares):
        small_push(turn).wait()
        total = total + small_got[turn]
    small_ref[...] = total
    total = late_own[...]
    for turn in range(1, shares):
        late_push(turn).wait()
        total = total + late_got[turn]
    late_ref[...] = total


def mixer_back(n, shares, sizes, images, cotangent, grad, branch_sent, branch, lines, vectors, norms, sums):
    count, side, _ = images.shape
    near = n // 2
    block, channels = sums[0].shape[1:]
    rows = block // near
    wide = sums[1].shape[2]
    line = pltpu.VMEM((count, side), jnp.float32)
    norm = pltpu.VMEM((8, channels), jnp.float32)
    vmem = pl.BlockSpec(memory_space=pltpu.VMEM)
    hbm = pl.BlockSpec(memory_space=pl.ANY)
    full = functools.partial(jax.ShapeDtypeStruct, dtype=jnp.float32)
    return pl.pallas_call(
        functools.partial(back_kernel, n, shares),
        out_shape=(
            jax.ShapeDtypeStruct(images.shape, jnp.bfloat16),
            full(images.shape),
            full((count, 3 * side)),
            full((8, side)),
            full((8, channels)),
            jax.ShapeDtypeStruct((shares, rows, channels), jnp.bfloat16),
            jax.ShapeDtypeStruct((shares, rows, wide), jnp.bfloat16),
        ),
        in_specs=[pl.BlockSpec(memory_space=pltpu.SMEM)]
        + [hbm] * 5
        + [vmem] * len(lines)
        + [pl.BlockSpec(memory_space=pltpu.SMEM)] * len(vectors)
        + [vmem] * len(norms)
        + [hbm] * 2,
        out_specs=(vmem,) * 5 + (hbm,) * 2,
        scratch_shapes=[
            pltpu.VMEM((count * side, side), jnp.float32),
            pltpu.VMEM(branch.shape, jnp.bfloat16),
            line,
            line,
            line,
            line,
            pltpu.VMEM((count, 3 * side), jnp.float32),
            pltpu.VMEM((shares, count, 3 * side), jnp.float32),
            pltpu.VMEM((8, side), jnp.float32),
            pltpu.VMEM((shares, 8, side), jnp.float32),
            norm,
            pltpu.VMEM((shares, 8, channels), jnp.float32),
            norm,
            pltpu.VMEM((n, 8, channels), jnp.float32),
            pltpu.VMEM(sums[1].shape, jnp.bfloat16),
            *(pltpu.VMEM(whole.shape, whole.dtype) for whole in (images, cotangent, grad, branch_sent, sums[0])),
            pltpu.SemaphoreType.DMA((5,)),
        ]
        + [
            kind
            for columns in (channels, wide)
            for kind in (
                pltpu.VMEM((near, rows, columns), jnp.bfloat16),
                pltpu.VMEM((near, rows, columns), jnp.bfloat16),
                pltpu.VMEM((rows, columns), jnp.float32),
                pltpu.VMEM((rows, columns), jnp.bfloat16),
            )
        ]
        + [
            pltpu.SemaphoreType.DMA(size if isinstance(size, tuple) else (size,))
            for size in ((branch.shape[1], n), (branch.shape[1], n), 1, *(shares,) * 8, n, n)
            + (near, near, shares, shares, 1) * 2
        ],
        compiler_params=pltpu.CompilerParams(
            collective_id=2, has_side_effects=True, vmem_limit_bytes=62 * mebi
        ),
        name="mixer_back",
    )(sizes, images, cotangent, grad, branch_sent, branch, *lines, *vectors, *norms, *sums)


def taps_kernel(small_ref, *refs):
    params, (*grads, rest_ref), wide, turned = refs[:8], refs[8:17], refs[17], refs[18]
    count = small_ref.shape[0]
    side = wide.shape[0]
    wide[...] = jnp.zeros_like(wide)

    def turn(at):
        wide[:count, :] = small_ref[:, at * side : (at + 1) * side]
        turned[...] = wide[...].T

    def rows_load(lag):
        return turned[pl.ds(lax.rem(lag + side - 1, side), 1), :count]

    def cols_load(lag):
        return turned[pl.ds(side - 1 - lag, 1), :count]

    for at, load in enumerate((rows_load, cols_load)):
        turn(at)
        found = taps_adjoint(*(ref[...] for ref in params[4 * at : 4 * at + 4]), side, load)
        for ref, grad in zip(grads[4 * at : 4 * at + 4], found):
            ref[...] = grad
    turn(2)
    rest_ref[...] = turned[:8, :count]


def taps_back(small, params, side):
    modes, count = params[0].shape
    full = functools.partial(jax.ShapeDtypeStruct, dtype=jnp.float32)
    vmem = pl.BlockSpec(memory_space=pltpu.VMEM)
    return pl.pallas_call(
        taps_kernel,
        out_shape=(full((modes, count)),) * 8 + (full((8, count)),),
        in_specs=[vmem] * 9,
        out_specs=(vmem,) * 9,
        scratch_shapes=[pltpu.VMEM((side, side), jnp.float32), pltpu.VMEM((side, side), jnp.float32)],
        name="taps_back",
    )(small, *params)


def pixel_body(
    n,
    images,
    cotangent,
    image_sizes,
    slot_image,
    rows_rate,
    rows_freq,
    rows_real,
    rows_imag,
    cols_rate,
    cols_freq,
    cols_real,
    cols_imag,
    skip_gain,
    norm_gain,
    norm_bias,
    weight_in,
    bias_in,
    weight_out,
    bias_out,
    layer_scale,
):
    _, count, side, _ = images.shape
    channels = norm_gain.shape[0]
    picked = slot_image[lax.axis_index("dp")]
    sizes = image_sizes[picked]
    image, cot = images[0], cotangent[0]

    params = tuple(
        param.T
        for param in (
            rows_rate,
            rows_freq,
            rows_real,
            rows_imag,
            cols_rate,
            cols_freq,
            cols_real,
            cols_imag,
        )
    )
    shares = lax.axis_size("dp")
    hidden = weight_out.shape[0]
    spread = jnp.broadcast_to(bias_in[:, None], (hidden, side))
    in_part = jnp.concatenate([weight_in.T, spread], axis=1).reshape(shares, -1, channels + side)
    out_part = weight_out.reshape(shares, -1, channels)
    mixed, first, back, in_whole, out_whole, bias_out_sums, rows_back, rows, cols_back, _ = mixer_forward(
        n, shares, sizes, image, cot, skip_gain, layer_scale, params, in_part, out_part
    )
    grad, branch_sent, branch, _, _, *sums, gain_sums, shift_sums = mlp(
        n,
        shares,
        mixed,
        first,
        back,
        in_whole.reshape(-1, channels + side),
        out_whole.reshape(-1, channels),
        jnp.broadcast_to(norm_gain[:, None], (channels, side)),
        jnp.broadcast_to(norm_bias[:, None], (channels, side)),
    )
    output, input_grad, small, late, norms, out_final, in_final = mixer_back(
        n,
        shares,
        sizes,
        image,
        cot,
        grad.reshape(side, count, side),
        branch_sent,
        branch,
        (rows_back, rows, cols_back),
        (skip_gain, layer_scale, bias_out),
        (bias_out_sums, gain_sums, shift_sums),
        sums,
    )
    *params_grad, rest = taps_back(small, params, side)
    in_final = in_final.reshape(hidden, channels + side).astype(jnp.float32)
    return (
        output[None],
        input_grad[None],
        *(grad.T for grad in params_grad),
        rest[0],
        norms[0],
        norms[1],
        in_final[:, :channels].T,
        jnp.sum(in_final[:, channels:], axis=1),
        out_final.reshape(hidden, channels).astype(jnp.float32),
        rest[1],
        late[0, :count],
    )


def choose_body(n, images, *rest):
    slots, count, side, _ = images.shape
    fits = (
        slots == 1
        and side == 128
        and count <= side
        and count % GROUP == 0
        and side % (4 * n * LINES) == 0
        and n == 8
        and (rest[15].shape[0] * n) % STEP_HIDDEN == 0
        and rest[15].shape[0] % (16 * lax.axis_size("dp")) == 0
        and lax.axis_size("dp") > 1
    )
    return pixel_body(n, images, *rest) if fits else plain_body(images, *rest)


def solution(mesh):
    in_specs = (
        P("dp", "chan", None, None),
        P("dp", "chan", None, None),
        P(),
        P(),
        P("chan", None),
        P("chan", None),
        P("chan", None),
        P("chan", None),
        P("chan", None),
        P("chan", None),
        P("chan", None),
        P("chan", None),
        P("chan"),
        P(),
        P(),
        P(None, "chan"),
        P("chan"),
        P("chan", None),
        P("chan"),
        P("chan"),
    )
    out_specs = (
        P("dp", "chan", None, None),
        P("dp", "chan", None, None),
        P("chan", None),
        P("chan", None),
        P("chan", None),
        P("chan", None),
        P("chan", None),
        P("chan", None),
        P("chan", None),
        P("chan", None),
        P("chan"),
        P(),
        P(),
        P(None, "chan"),
        P("chan"),
        P("chan", None),
        P("chan"),
        P("chan"),
    )
    return jax.shard_map(functools.partial(choose_body, mesh.shape["chan"]), mesh=mesh, in_specs=in_specs, out_specs=out_specs, check_vma=False)
```

```python
import functools

import jax
import jax.numpy as jnp
from jax import lax
from jax.experimental import pallas as pl
from jax.experimental.pallas import tpu as pltpu
from jax.sharding import PartitionSpec as P

eps_norm = 1e-06
highest = lax.Precision.HIGHEST


def kernel_taps(rate_vals, freq_vals, real_part, imag_part, length):
    offsets = jnp.arange(length, dtype=jnp.float32)
    decays = jnp.exp(-rate_vals[:, :, None] * offsets)
    angles = freq_vals[:, :, None] * offsets
    return jnp.sum(
        decays
        * (real_part[:, :, None] * jnp.cos(angles) - imag_part[:, :, None] * jnp.sin(angles)),
        axis=1,
    )


def toeplitz(filter_taps):
    length = filter_taps.shape[1]
    offsets = jnp.arange(length, dtype=jnp.int32)
    lag_index = offsets[:, None] - offsets[None, :]
    return jnp.where(lag_index[None] >= 0, filter_taps[:, jnp.maximum(lag_index, 0)], 0.0)


def mixer(
    masked_in,
    rows_rate,
    rows_freq,
    rows_real,
    rows_imag,
    cols_rate,
    cols_freq,
    cols_real,
    cols_imag,
    skip_gain,
):
    rows_op = toeplitz(kernel_taps(rows_rate, rows_freq, rows_real, rows_imag, masked_in.shape[2]))
    cols_op = toeplitz(kernel_taps(cols_rate, cols_freq, cols_real, cols_imag, masked_in.shape[3]))
    along_rows = jnp.einsum("chi,ncij->nchj", rows_op, masked_in, precision=highest)
    return (
        jnp.einsum("nchj,cwj->nchw", along_rows, cols_op, precision=highest)
        + skip_gain[None, :, None, None] * masked_in
    )


def normalize(values, norm_gain, norm_bias):
    center = values - jnp.mean(values, axis=-2, keepdims=True)
    inverse = lax.rsqrt(jnp.mean(center * center, axis=-2, keepdims=True) + eps_norm)
    scaled = center * inverse
    return (scaled * norm_gain[:, None] + norm_bias[:, None], scaled, inverse)


def gelu_exact(values):
    return jax.nn.gelu(values, approximate=False)


def plain_body(
    images,
    cotangent,
    image_sizes,
    slot_image,
    rows_rate,
    rows_freq,
    rows_real,
    rows_imag,
    cols_rate,
    cols_freq,
    cols_real,
    cols_imag,
    skip_gain,
    norm_gain,
    norm_bias,
    weight_in,
    bias_in,
    weight_out,
    bias_out,
    layer_scale,
):
    slot_count, chan_count, length = (images.shape[0], images.shape[1], images.shape[2])
    pixels = length * length
    image_count = slot_image.shape[0]
    slot_ids = lax.axis_index("dp") * slot_count + jnp.arange(slot_count, dtype=jnp.int32)
    choose = (slot_ids[:, None] == jnp.arange(image_count, dtype=jnp.int32)[None, :]).astype(
        jnp.int32
    )
    picked = jnp.sum(choose * slot_image[None, :], axis=1)
    owners = (picked[:, None] == jnp.arange(image_count, dtype=jnp.int32)[None, :]).astype(
        jnp.int32
    )
    heights = jnp.sum(owners * image_sizes[None, :, 0], axis=1)
    widths = jnp.sum(owners * image_sizes[None, :, 1], axis=1)
    offsets = jnp.arange(length, dtype=jnp.int32)
    inside = (
        (offsets[None, :, None] < heights[:, None, None])
        & (offsets[None, None, :] < widths[:, None, None])
    ).astype(jnp.float32)
    masked_in = images.astype(jnp.float32) * inside[:, None]
    mixed_out, mixer_pull = jax.vjp(
        mixer,
        masked_in,
        rows_rate,
        rows_freq,
        rows_real,
        rows_imag,
        cols_rate,
        cols_freq,
        cols_real,
        cols_imag,
        skip_gain,
    )
    mixed_low = mixed_out.astype(jnp.bfloat16).reshape(slot_count, chan_count, pixels)
    mask_flat = inside.reshape(slot_count, 1, pixels)
    residual = images.astype(jnp.float32).reshape(slot_count, chan_count, pixels)
    grad_out = cotangent.astype(jnp.float32).reshape(slot_count, chan_count, pixels) * mask_flat
    chan_offset = lax.axis_index("chan") * chan_count
    all_channels = norm_gain.shape[0]
    slot_item = 0
    gathered = lax.all_gather(mixed_low[slot_item], "chan", axis=0, tiled=True)
    normed, scaled, inverse = normalize(gathered.astype(jnp.float32), norm_gain, norm_bias)
    normed_low = normed.astype(jnp.bfloat16)
    before = (
        jnp.einsum("cf,cp->fp", weight_in, normed_low, preferred_element_type=jnp.float32)
        + bias_in.astype(jnp.float32)[:, None]
    )
    active = gelu_exact(before).astype(jnp.bfloat16)

    def project(first_row, row_count, active=active):
        return jnp.einsum("fc,fp->cp", weight_out, active, preferred_element_type=jnp.float32)

    branch_list = [
        lax.psum_scatter(
            project(jnp.int32(0), chan_count * lax.axis_size("chan")),
            "chan",
            scatter_dimension=0,
            tiled=True,
        )
    ]
    scaled_part = lax.dynamic_slice_in_dim(scaled, chan_offset, chan_count, 0)
    stored = [(normed_low, before, active, scaled_part, inverse)]
    branch_all = jnp.stack(branch_list)
    shifted = branch_all + bias_out[None, :, None]
    output = (
        (mask_flat * (residual + layer_scale[None, :, None] * shifted))
        .astype(jnp.bfloat16)
        .reshape(images.shape)
    )
    scale_grad = jnp.sum(grad_out * shifted, axis=(0, 2))
    branch_grad = layer_scale[None, :, None] * grad_out
    bias_out_grad = jnp.sum(branch_grad, axis=(0, 2))
    branch_low = branch_grad.astype(jnp.bfloat16)
    hidden_count = weight_in.shape[1]
    out_weight_grad = jnp.zeros((hidden_count, all_channels), jnp.float32)
    gain_shard = lax.dynamic_slice_in_dim(norm_gain, chan_offset, chan_count, 0)
    slot_item = 0
    normed_low, before, active, scaled_part, inverse = stored[slot_item]

    def absorb(totals, shard_rows, first_row, active=active):
        hidden_grad = jnp.einsum(
            "fc,cp->fp", weight_out, shard_rows, preferred_element_type=jnp.float32
        )
        product_part = jnp.einsum(
            "fp,cp->fc", active, shard_rows, preferred_element_type=jnp.float32
        )
        return (hidden_grad, product_part)

    hidden_start = jnp.zeros((hidden_count, pixels), jnp.float32)
    hidden_grad, out_weight_grad = absorb(
        (hidden_start, out_weight_grad),
        lax.all_gather(branch_low[slot_item], "chan", axis=0, tiled=True),
        jnp.int32(0),
    )
    gelu_pull = jax.vjp(gelu_exact, before)[1]
    before_grad = gelu_pull(hidden_grad)[0].astype(jnp.bfloat16)
    in_weight_grad = jnp.einsum(
        "cp,fp->cf", normed_low, before_grad, preferred_element_type=jnp.float32
    )
    in_bias_grad = jnp.sum(before_grad.astype(jnp.float32), axis=1)

    def spread_back(first_row, row_count, before_grad=before_grad):
        return jnp.einsum("cf,fp->cp", weight_in, before_grad, preferred_element_type=jnp.float32)

    normed_grad = lax.psum_scatter(
        spread_back(jnp.int32(0), chan_count * lax.axis_size("chan")),
        "chan",
        scatter_dimension=0,
        tiled=True,
    )
    weighted = normed_grad * gain_shard[:, None]
    pixel_sums = (
        lax.psum(jnp.sum(weighted, axis=0).astype(jnp.bfloat16), "chan").astype(jnp.float32),
        lax.psum(jnp.sum(weighted * scaled_part, axis=0).astype(jnp.bfloat16), "chan").astype(
            jnp.float32
        ),
    )
    mixed_grads = [
        inverse
        * (
            weighted
            - pixel_sums[0][None, :] / all_channels
            - scaled_part * pixel_sums[1][None, :] / all_channels
        )
    ]
    gain_part = jnp.sum(normed_grad * scaled_part, axis=1)
    shift_part = jnp.sum(normed_grad, axis=1)
    mixed_grad_all = jnp.stack(mixed_grads)
    gain_grad = lax.dynamic_update_slice_in_dim(
        jnp.zeros((all_channels,), jnp.float32), gain_part, chan_offset, 0
    )
    shift_grad = lax.dynamic_update_slice_in_dim(
        jnp.zeros((all_channels,), jnp.float32), shift_part, chan_offset, 0
    )
    pulled = mixer_pull(mixed_grad_all.reshape(images.shape))
    input_grad = inside[:, None] * (cotangent.astype(jnp.float32) + pulled[0])
    summed = lax.psum(
        (
            in_weight_grad,
            out_weight_grad,
            in_bias_grad,
            bias_out_grad,
            scale_grad,
            pulled[1],
            pulled[2],
            pulled[3],
            pulled[4],
            pulled[5],
            pulled[6],
            pulled[7],
            pulled[8],
            pulled[9],
        ),
        "dp",
    )
    norm_sums = lax.psum((gain_grad, shift_grad), ("dp", "chan"))
    return (
        output,
        input_grad,
        summed[5],
        summed[6],
        summed[7],
        summed[8],
        summed[9],
        summed[10],
        summed[11],
        summed[12],
        summed[13],
        norm_sums[0],
        norm_sums[1],
        summed[0],
        summed[2],
        summed[1],
        summed[3],
        summed[4],
    )


MESH = pl.DeviceIdType.MESH
GROUP = 16
ABREAST = 4
LINES = 4
STEP_HIDDEN = 512
mebi = 1024 * 1024


def dot_nn(left, right):
    return lax.dot_general(left, right, (((1,), (0,)), ((), ())), preferred_element_type=jnp.float32)


def dot_nt(left, right):
    return lax.dot_general(left, right, (((1,), (1,)), ((), ())), preferred_element_type=jnp.float32)


def dot_tn(left, right):
    return lax.dot_general(left, right, (((0,), (0,)), ((), ())), preferred_element_type=jnp.float32)


def split_low(values):
    high = values.astype(jnp.bfloat16)
    return high, (values - high.astype(jnp.float32)).astype(jnp.bfloat16)


def lag_matrix(line, side, keep):
    spread = pltpu.roll(jnp.broadcast_to(line, (side, side)), 0, 1, stride=1, stride_axis=0)
    return jnp.where(keep, spread, 0.0)


def lag_sums(matrix, side, keep):
    turned = pltpu.roll(jnp.where(keep, matrix, 0.0), 0, 1, stride=1, stride_axis=0)
    return jnp.sum(turned, axis=0, keepdims=True)


cos_terms = (
    1.0, -19.7392087, 64.9393891, -85.4566583, 60.242131, -26.4046662, 7.8001253, -1.45310477
)
sin_terms = (6.2831853, -41.3417004, 81.6051314, -76.703015, 42.0259236, -14.8998335, 3.23811835)


def polynomial(terms, at):
    value = terms[-1]
    for term in terms[-2::-1]:
        value = value * at + term
    return value


TILE = 16


def power(rate, freq, lag):
    angle = freq * 0.15915494309189535 * lag
    angle = angle - jnp.floor(angle + 0.5)
    square = angle * angle
    decay = jnp.exp(-rate * lag)
    return decay * polynomial(cos_terms, square), decay * (angle * polynomial(sin_terms, square))


def product(left, right):
    return left[0] * right[0] - left[1] * right[1], left[0] * right[1] + left[1] * right[0]


def taps_lines(rate, freq, real, imag, side, store):
    first = power(rate, freq, 1.0)

    @pl.loop(0, side // TILE)
    def _(tile):
        state = product((real, imag), power(rate, freq, (tile * TILE).astype(jnp.float32)))
        for step in range(TILE):
            store(tile * TILE + step, jnp.sum(state[0], axis=0, keepdims=True))
            state = product(state, first)


def taps_adjoint(rate, freq, real, imag, side, load):
    first = power(rate, freq, 1.0)

    def tile_sums(tile, totals):
        state = power(rate, freq, (tile * TILE).astype(jnp.float32))
        even, odd, even_lag, odd_lag = totals
        for step in range(TILE):
            grad = load(tile * TILE + step)
            late = grad * (tile * TILE + step).astype(jnp.float32)
            even = even + grad * state[0]
            odd = odd + grad * state[1]
            even_lag = even_lag + late * state[0]
            odd_lag = odd_lag + late * state[1]
            state = product(state, first)
        return even, odd, even_lag, odd_lag

    zero = jnp.zeros_like(rate)
    even, odd, even_lag, odd_lag = lax.fori_loop(0, side // TILE, tile_sums, (zero,) * 4)
    return imag * odd_lag - real * even_lag, -real * odd_lag - imag * even_lag, even, -odd


def lane_sums(values):
    ones = jnp.ones((8, values.shape[1]), jnp.bfloat16)
    high, rest = split_low(values)
    low = (values - high.astype(jnp.float32) - rest.astype(jnp.float32)).astype(jnp.bfloat16)
    return dot_nt(ones, high) + dot_nt(ones, rest) + dot_nt(ones, low)


def meet(n, shares):
    me, share = lax.axis_index("chan"), lax.axis_index("dp")
    barrier = pltpu.get_barrier_semaphore()
    for shift in range(1, n):
        pl.semaphore_signal(
            barrier, inc=1, device_id={"chan": lax.rem(me + shift, n)}, device_id_type=MESH
        )
    for shift in range(1, shares):
        pl.semaphore_signal(
            barrier, inc=1, device_id={"dp": lax.rem(share + shift, shares)}, device_id_type=MESH
        )
    pl.semaphore_wait(barrier, n + shares - 2)
    return me, share


def push(source, target, send_sem, recv_sem, **peer):
    return pltpu.make_async_remote_copy(
        src_ref=source,
        dst_ref=target,
        send_sem=send_sem,
        recv_sem=recv_sem,
        device_id=peer,
        device_id_type=MESH,
    )


def weight_rounds(n, shares, me, share, pairs, sems):
    far = me // 2
    core = lax.rem(me, 2)
    mate = far + 1 - 2 * lax.rem(far, 2)
    mine = far // 2 * 2
    beyond = 2 - mine
    inner = lax.rem(far + 1, 4) >= 2
    own_sem, send1, recv1, send2, recv2, send3, recv3 = sems
    both = range(len(pairs))
    origins = (mate, beyond, beyond + 1)

    def own(at):
        local, whole = pairs[at]
        return pltpu.make_async_copy(local, whole.at[core, :, far], own_sem.at[at])

    def first(at, back=False):
        local, whole = pairs[at]
        return push(
            local.at[share],
            whole.at[core, share, mate if back else far],
            send1.at[at, 0],
            recv1.at[at, 0],
            chan=mate * 2 + core,
        )

    def across(at, half, back=False):
        whole = pairs[at][1]
        return push(
            whole.at[core, share, mine + half],
            whole.at[core, share, (beyond if back else mine) + half],
            send1.at[at, 1 + half],
            recv1.at[at, 1 + half],
            chan=(3 - far) * 2 + core,
        )

    def onward(at, half):
        block = pairs[at][1].at[core, share, beyond + half]
        return push(block, block, send1.at[at, 3 + half], recv1.at[at, 1 + half], chan=mate * 2 + core)

    def second(at, place, turn, back=False):
        whole = pairs[at][1]
        holder = lax.rem(share + shares - turn, shares) if back else share
        return push(
            whole.at[core, share, origins[place]],
            whole.at[core, holder, origins[place]],
            send2.at[at, place, turn],
            recv2.at[at, place, turn],
            dp=lax.rem(share + turn, shares),
        )

    def third(at, back=False):
        whole = pairs[at][1]
        return push(
            whole.at[core], whole.at[1 - core if back else core], send3.at[at], recv3.at[at], chan=far * 2 + 1 - core
        )

    def start_second(at, place):
        for turn in range(1, shares):
            second(at, place, turn).start()

    def start_first():
        for at in both:
            own(at).start()
            first(at).start()

    def start_across():
        for at in both:
            own(at).wait()
            first(at, True).wait_recv()

            @pl.when(inner)
            def _():
                for half in range(2):
                    across(at, half).start()

            start_second(at, 0)

    def start_onward():
        @pl.when(inner)
        def _():
            for at in both:
                for half in range(2):
                    across(at, half, True).wait_recv()
                    onward(at, half).start()
                    start_second(at, 1 + half)

    def start_last():
        @pl.when(jnp.logical_not(inner))
        def _():
            for at in both:
                for half in range(2):
                    across(at, half, True).wait_recv()
                    start_second(at, 1 + half)

    def start_third():
        for at in both:
            for place in range(3):
                for turn in range(1, shares):
                    second(at, place, turn, True).wait_recv()
            third(at).start()

    def finish():
        for at in both:
            third(at, True).wait_recv()
            third(at).wait_send()
            first(at).wait_send()
            for place in range(3):
                for turn in range(1, shares):
                    second(at, place, turn).wait_send()

            @pl.when(inner)
            def _():
                for half in range(2):
                    across(at, half).wait_send()
                    onward(at, half).wait_send()

    return start_first, start_across, start_onward, start_last, start_third, finish


def send_part(stage, target, me, peer, part, send_sem, recv_sem, shift):
    return pltpu.make_async_remote_copy(
        src_ref=stage.at[peer, part],
        dst_ref=target.at[me, part],
        send_sem=send_sem.at[shift],
        recv_sem=recv_sem.at[shift],
        device_id={"chan": peer},
        device_id_type=MESH,
    )


def wait_parts(stage, target, me, n, send_sem, recv_sem):
    for shift in range(1, n):
        peer = lax.rem(me + shift, n)
        origin = lax.rem(me + n - shift, n)
        pltpu.make_async_remote_copy(
            src_ref=stage.at[peer],
            dst_ref=target.at[origin],
            send_sem=send_sem.at[shift],
            recv_sem=recv_sem.at[shift],
            device_id={"chan": peer},
            device_id_type=MESH,
        ).wait()


def mixer_kernel(
    n,
    shares,
    sizes_ref,
    image_ref,
    cot_ref,
    skip_ref,
    scale_ref,
    *rest,
):
    mixer_body(n, shares, sizes_ref, image_ref, cot_ref, skip_ref, scale_ref, rest[:8], *rest[8:])


def mixer_body(
    n,
    shares,
    sizes_ref,
    image_ref,
    cot_ref,
    skip_ref,
    scale_ref,
    param_refs,
    in_part_ref,
    out_part_ref,
    mixed_ref,
    first_ref,
    back_ref,
    in_whole_ref,
    out_whole_ref,
    sums_ref,
    rows_back_ref,
    rows_ref,
    cols_back_ref,
    cols_ref,
    mixed_stage,
    back_stage,
    wide,
    taps,
    params_got,
    params_sem,
    send_m,
    recv_m,
    send_b,
    recv_b,
    own_sem,
    keep_sem,
    *weight_sems,
):
    count, side, _ = image_ref.shape
    parts = count // GROUP
    block = side // n
    me, share = meet(n, shares)
    start_first, start_across, start_onward, start_last, start_third, finish = weight_rounds(
        n, shares, me, share, ((in_part_ref, in_whole_ref), (out_part_ref, out_whole_ref)), weight_sems
    )
    start_first()
    param_copies = [
        pltpu.make_async_copy(ref, params_got.at[at], params_sem.at[at]) for at, ref in enumerate(param_refs)
    ]
    for copy in param_copies:
        copy.start()
    taps[...] = jnp.zeros_like(taps)
    row_at = lax.broadcasted_iota(jnp.int32, (side, side), 0)
    col_at = lax.broadcasted_iota(jnp.int32, (side, side), 1)
    inside = (row_at < sizes_ref[0]) & (col_at < sizes_ref[1])
    lower = row_at >= col_at
    upper = row_at <= col_at

    def turn(stage, part):
        @pl.loop(0, n)
        def _(owner):
            for line in range(block):
                tile = wide[pl.ds(owner * block + line, GROUP, stride=side), :]
                stage[owner, part, line] = tile.astype(jnp.bfloat16)

    def send(stage, target, part, send_sem, recv_sem):
        for shift in range(1, n):
            send_part(stage, target, me, lax.rem(me + shift, n), part, send_sem, recv_sem, shift).start()

    def own_back(part):
        return pltpu.make_async_copy(back_stage.at[:, part], back_ref.at[:, part], keep_sem.at[part])

    def first_push(shift, back=False):
        peer = lax.rem(me + shift, n)
        return push(
            back_stage.at[peer, :, pl.ds(0, LINES)],
            first_ref.at[lax.rem(me + n - shift, n) if back else me],
            send_b.at[shift],
            recv_b.at[shift],
            chan=peer,
        )

    for copy in param_copies:
        copy.wait()
    for axis, (back_out, out) in enumerate(((rows_back_ref, rows_ref), (cols_back_ref, cols_ref))):

        def store(lag, line):
            taps[0, pl.ds(lax.rem(side - lag, side), 1), :count] = line
            taps[1, pl.ds(lag, 1), :count] = line

        taps_lines(*(params_got[4 * axis + at] for at in range(4)), side, store)
        back_out[...] = taps[0].T[:count]
        out[...] = taps[1].T[:count]


    @pl.loop(0, parts)
    def _(part):
        pl.when(part == 1)(start_across)
        pl.when(part == parts // 2)(start_onward)

        def one_channel(item):
            chan = part * GROUP + item
            masked = jnp.where(inside, image_ref[chan].astype(jnp.float32), 0.0)
            masked_low = masked.astype(jnp.bfloat16)
            rows_high, rows_low = split_low(lag_matrix(rows_back_ref[pl.ds(chan, 1), :], side, lower))
            cols_high, cols_low = split_low(lag_matrix(cols_ref[pl.ds(chan, 1), :], side, upper))
            along = dot_nn(
                jnp.concatenate([rows_high, rows_low], axis=1),
                jnp.concatenate([masked_low, masked_low], axis=0),
            )
            along_high, along_low = split_low(along)
            mixed = dot_nn(
                jnp.concatenate([along_high, along_low], axis=1),
                jnp.concatenate([cols_high, cols_high], axis=0),
            ) + dot_nn(along_high, cols_low)
            mixed = mixed + skip_ref[chan] * masked
            wide[pl.ds(pl.multiple_of(item * side, side), side), :] = mixed

        @pl.loop(0, GROUP // ABREAST)
        def _(few):
            for at in range(ABREAST):
                one_channel(few * ABREAST + at)

        turn(mixed_stage, part)
        send(mixed_stage, mixed_ref, part, send_m, recv_m)

    start_last()

    @pl.loop(0, parts)
    def _(part):
        @pl.loop(0, GROUP)
        def _(item):
            chan = part * GROUP + item
            grad_out = jnp.where(inside, cot_ref[chan].astype(jnp.float32), 0.0)
            scaled = grad_out * scale_ref[chan]
            sums_ref[pl.ds(chan, 1), :] = jnp.sum(scaled, axis=0, keepdims=True)
            wide[pl.ds(pl.multiple_of(item * side, side), side), :] = scaled

        turn(back_stage, part)
        own_back(part).start()

    for shift in range(1, n):
        first_push(shift).start()
    own_b = pltpu.make_async_copy(back_stage.at[me, :, pl.ds(0, LINES)], first_ref.at[me], own_sem.at[0])
    own_m = pltpu.make_async_copy(mixed_stage.at[me], mixed_ref.at[me], own_sem.at[1])
    own_b.start()
    own_m.start()
    start_third()
    for part in range(parts):
        own_back(part).wait()
    own_b.wait()
    own_m.wait()
    wait_parts(mixed_stage, mixed_ref, me, n, send_m, recv_m)
    for shift in range(1, n):
        first_push(shift, True).wait_recv()
        first_push(shift).wait_send()
    finish()


def mixer_forward(n, shares, sizes, images, cotangent, skip, scale, params, in_part, out_part):
    near = n // 2
    smem = pl.BlockSpec(memory_space=pltpu.SMEM)
    count, side, _ = images.shape
    line = jax.ShapeDtypeStruct((count, side), jnp.float32)
    shape = (n, count // GROUP, side // n, GROUP, side)
    first_shape = (n, count // GROUP, LINES, GROUP, side)
    vmem = pl.BlockSpec(memory_space=pltpu.VMEM)
    hbm = pl.BlockSpec(memory_space=pl.ANY)
    return pl.pallas_call(
        functools.partial(mixer_kernel, n, shares),
        out_shape=(
            jax.ShapeDtypeStruct(shape, jnp.bfloat16),
            jax.ShapeDtypeStruct(first_shape, jnp.bfloat16),
            jax.ShapeDtypeStruct(shape, jnp.bfloat16),
        )
        + tuple(
            jax.ShapeDtypeStruct((2, shares, near, *part.shape[1:]), jnp.bfloat16)
            for part in (in_part, out_part)
        )
        + (line,) * 5,
        in_specs=[smem] + [vmem] * 2 + [smem] * 2 + [hbm] * 10,
        out_specs=(hbm,) * 5 + (vmem,) * 5,
        scratch_shapes=[
            pltpu.VMEM(shape, jnp.bfloat16),
            pltpu.VMEM(shape, jnp.bfloat16),
            pltpu.VMEM((GROUP * side, side), jnp.float32),
            pltpu.VMEM((2, side, side), jnp.float32),
            pltpu.VMEM((8, *params[0].shape), jnp.float32),
            pltpu.SemaphoreType.DMA((8,)),
            pltpu.SemaphoreType.DMA((n,)),
            pltpu.SemaphoreType.DMA((n,)),
            pltpu.SemaphoreType.DMA((n,)),
            pltpu.SemaphoreType.DMA((n,)),
            pltpu.SemaphoreType.DMA((2,)),
            pltpu.SemaphoreType.DMA((count // GROUP,)),
            pltpu.SemaphoreType.DMA((2,)),
            pltpu.SemaphoreType.DMA((2, 5)),
            pltpu.SemaphoreType.DMA((2, 3)),
            pltpu.SemaphoreType.DMA((2, 3, shares)),
            pltpu.SemaphoreType.DMA((2, 3, shares)),
            pltpu.SemaphoreType.DMA((2,)),
            pltpu.SemaphoreType.DMA((2,)),
        ],
        compiler_params=pltpu.CompilerParams(
            collective_id=0, has_side_effects=True, vmem_limit_bytes=40 * mebi
        ),
        name="mixer_forward",
    )(sizes, images, cotangent, skip, scale, *params, in_part, out_part)


def gelu_parts(value):
    bell = jnp.exp(-0.5 * value * value)
    inner = 1.0 / (1.0 + (0.3275911 * 0.7071067811865476) * jnp.abs(value))
    series = 1.061405429 * inner - 1.453152027
    series = series * inner + 1.421413741
    series = series * inner - 0.284496736
    series = series * inner + 0.254829592
    tail = (0.5 * inner) * series * bell
    return jnp.where(value < 0.0, tail, 1.0 - tail), bell * 0.3989422804014327


def mlp_kernel(
    n,
    shares,
    mixed_hbm,
    first_hbm,
    in_hbm,
    out_hbm,
    gain_ref,
    shift_ref,
    back_ref,
    grad_ref,
    branch_sent_ref,
    branch_ref,
    active_ref,
    before_grad_ref,
    out_take_ref,
    in_half_ref,
    gain_grad_ref,
    shift_grad_ref,
    grad_stage,
    branch_stage,
    active_ring,
    before_ring,
    normed_keep,
    cots_keep,
    scaled_keep,
    inverse_keep,
    branch_sum,
    grad_sum,
    hidden_sum,
    pieces,
    rows_stage,
    out_got,
    in_got,
    back_got,
    mixed_ref,
    first_ref,
    in_ref,
    out_ref,
    load_sem,
    send_g,
    recv_g,
    send_c,
    recv_c,
    send_r,
    recv_r,
    own_sem,
    ring_sem,
    piece_sem,
    send_h,
    recv_h,
    send_2,
    recv_2,
):
    loads = [
        pltpu.make_async_copy(whole, here, load_sem.at[at])
        for at, (whole, here) in enumerate(
            ((mixed_hbm, mixed_ref), (first_hbm, first_ref), (in_hbm, in_ref), (out_hbm, out_ref))
        )
    ]
    for copy in loads:
        copy.start()
    side = mixed_ref.shape[-1]
    groups = mixed_ref.shape[1]
    block = mixed_ref.shape[2]
    hidden, channels = out_ref.shape
    local = channels // n
    steps = block // LINES
    width = LINES * side
    parts = hidden // STEP_HIDDEN
    ring = active_ring.shape[0]
    me, share = meet(n, shares)
    core = lax.rem(me, 2)
    sibling = me + 1 - 2 * core
    early = branch_sent_ref.shape[1]

    def cot_push(step, shift, back=False):
        peer = lax.rem(me + shift, n)
        origin = lax.rem(me + n - shift, n) if back else me
        span = pl.ds(step * LINES, LINES)
        return push(
            back_ref.at[peer, :, span],
            back_got.at[origin, :, span],
            send_c.at[step, shift],
            recv_c.at[step, shift],
            chan=peer,
        )

    def branch_push(shift, back=False):
        peer = lax.rem(me + shift, n)
        return push(
            branch_stage.at[peer, pl.ds(0, early)],
            branch_sent_ref.at[lax.rem(me + n - shift, n) if back else me],
            send_r.at[shift],
            recv_r.at[shift],
            chan=peer,
        )

    for step in range(1, steps):
        for shift in range(1, n):
            cot_push(step, shift).start()
    own_c = pltpu.make_async_copy(back_ref.at[me], back_got.at[me], own_sem.at[2])
    own_c.start()
    for copy in loads:
        copy.wait()
    gain_grad_ref[...] = jnp.zeros_like(gain_grad_ref)
    shift_grad_ref[...] = jnp.zeros_like(shift_grad_ref)
    hidden_sum[...] = jnp.zeros_like(hidden_sum)

    def keeps(turn):
        slot = lax.rem(turn, ring)
        span = pl.ds(pl.multiple_of(lax.rem(turn, parts) * STEP_HIDDEN, STEP_HIDDEN), STEP_HIDDEN)
        return [
            pltpu.make_async_copy(kept.at[slot], whole.at[turn // parts, span], ring_sem.at[at, slot])
            for at, (kept, whole) in enumerate(((active_ring, active_ref), (before_ring, before_grad_ref)))
        ]

    @pl.loop(0, steps)
    def _(step):
        pl.when(step == 1)(own_c.wait)

        @pl.when(step > 0)
        def _():
            for shift in range(1, n):
                cot_push(step, shift, True).wait_recv()

        for line in range(LINES):
            row = step * LINES + line
            lanes = pl.ds(line * side, side)
            order = [(owner, group) for owner in range(n) for group in range(groups)]
            mixed = jnp.concatenate(
                [mixed_ref[owner, group, row].astype(jnp.float32) for owner, group in order], axis=0
            )
            mean = jnp.sum(mixed, axis=0, keepdims=True) * (1.0 / channels)
            center = mixed - mean
            var = jnp.sum(center * center, axis=0, keepdims=True) * (1.0 / channels)
            inverse = lax.rsqrt(var + eps_norm)
            scaled = center * inverse
            normed_keep[step, :, lanes] = (scaled * gain_ref[...] + shift_ref[...]).astype(jnp.bfloat16)
            scaled_keep[:, lanes] = scaled
            inverse_keep[:, lanes] = inverse

            @pl.when(step == 0)
            def _():
                cots_keep[step, :, lanes] = jnp.concatenate(
                    [first_ref[owner, group, line] for owner, group in order], axis=0
                )

            @pl.when(step > 0)
            def _():
                cots_keep[step, :, lanes] = jnp.concatenate(
                    [back_got[owner, group, row] for owner, group in order], axis=0
                )

        @pl.loop(0, parts)
        def _(part):
            turn = step * parts + part
            slot = lax.rem(turn, ring)

            @pl.when(turn >= ring)
            def _():
                for copy in keeps(turn - ring):
                    copy.wait()

            span = pl.ds(pl.multiple_of(part * STEP_HIDDEN, STEP_HIDDEN), STEP_HIDDEN)
            bias = in_ref[span, channels:].astype(jnp.float32)[:, :1]
            before = dot_nn(in_ref[span, :channels], normed_keep[step]) + bias
            inside, bell = gelu_parts(before)
            active = (before * inside).astype(jnp.bfloat16)
            active_grad = dot_nn(out_ref[span, :], cots_keep[step])
            before_grad = (active_grad * (inside + before * bell)).astype(jnp.bfloat16)
            active_ring[slot] = active
            before_ring[slot] = before_grad
            hidden_sum[span, :] += sum(
                before_grad[:, line * side : (line + 1) * side].astype(jnp.float32) for line in range(LINES)
            )
            branch = dot_tn(out_ref[span, :], active)
            grad = dot_tn(in_ref[span, :channels], before_grad)

            @pl.when(part == 0)
            def _():
                branch_sum[...] = branch
                grad_sum[...] = grad

            @pl.when(part > 0)
            def _():
                branch_sum[...] += branch
                grad_sum[...] += grad

            for copy in keeps(turn):
                copy.start()

        for line in range(LINES):
            lanes = pl.ds(line * side, side)
            grad = grad_sum[:, lanes]
            scaled = scaled_keep[:, lanes]
            gain_grad_ref[...] += grad * scaled
            shift_grad_ref[...] += grad
            weighted = grad * gain_ref[...]
            first = jnp.sum(weighted, axis=0, keepdims=True) * (1.0 / channels)
            second = jnp.sum(weighted * scaled, axis=0, keepdims=True) * (1.0 / channels)
            mixed_grad = (inverse_keep[:, lanes] * (weighted - first - scaled * second)).astype(jnp.bfloat16)
            branch = branch_sum[:, lanes].astype(jnp.bfloat16)
            for owner in range(n):
                grad_stage[owner, step, line] = mixed_grad[owner * local : (owner + 1) * local]
                branch_stage[owner, step, line] = branch[owner * local : (owner + 1) * local]

        for shift in range(1, n):
            send_part(grad_stage, grad_ref, me, lax.rem(me + shift, n), step, send_g, recv_g, shift).start()

    own_g = pltpu.make_async_copy(grad_stage.at[me], grad_ref.at[me], own_sem.at[0])
    own_r = pltpu.make_async_copy(branch_stage.at[:, pl.ds(early, steps - early)], branch_ref, own_sem.at[1])
    own_s = pltpu.make_async_copy(branch_stage.at[me, pl.ds(0, early)], branch_sent_ref.at[me], own_sem.at[3])
    for shift in range(1, n):
        branch_push(shift).start()
    own_g.start()
    own_r.start()
    own_s.start()
    turns = steps * parts
    for turn in range(turns - ring, turns):
        for copy in keeps(turn):
            copy.wait()

    block_rows = hidden // 2 // shares
    kinds = (
        (active_ref, cots_keep, out_got, out_take_ref),
        (before_grad_ref, normed_keep, in_got, in_half_ref),
    )

    def block_span(job, base=0):
        at = lax.rem(share + 1 + lax.rem(job, shares), shares)
        return pl.ds(pl.multiple_of(base + at * block_rows, block_rows), block_rows)

    def whole_span(job):
        owner = 1 - core if job < shares else core
        return block_span(job, owner * (hidden // 2))

    def fetch(kind, job, slot):
        return pltpu.make_async_copy(
            kinds[kind][0].at[:, whole_span(job)], pieces.at[slot], piece_sem.at[slot]
        )

    def give(kind, job):
        got = kinds[kind][2]
        return push(
            rows_stage.at[job, :, pl.ds(0, got.shape[1])],
            got.at[block_span(job)],
            send_h.at[kind, job],
            recv_h.at[kind, job],
            chan=sibling,
        )

    def second(kind, job):
        _, _, got, take = kinds[kind]
        turn = job + 1 - shares
        if kind == 1:
            at = lax.rem(share + turn, shares)
            return pltpu.make_async_copy(got.at[block_span(job)], take.at[at], send_2.at[1, turn - 1])
        if turn == shares:
            return pltpu.make_async_copy(got.at[block_span(job)], take.at[0], send_2.at[0, 0])
        return push(
            got.at[block_span(job)],
            take.at[turn],
            send_2.at[kind, turn],
            recv_2.at[kind, turn],
            dp=lax.rem(share + turn, shares),
        )

    jobs = [(kind, job) for kind in range(2) for job in range(2 * shares)]
    fetch(0, 0, 0).start()
    for at, (kind, job) in enumerate(jobs):
        slot = at % 2
        if at + 1 < len(jobs):
            fetch(*jobs[at + 1], (at + 1) % 2).start()
        fetch(kind, job, slot).wait()
        right, got = kinds[kind][1:3]
        total = dot_nt(
            jnp.concatenate([pieces[slot, step] for step in range(steps)], axis=1),
            jnp.concatenate([right[step] for step in range(steps)], axis=1),
        )
        if job < shares:
            rows_stage[job, :, :channels] = total.astype(jnp.bfloat16)
            if kind == 1:
                rows_stage[job, :, channels:] = hidden_sum[whole_span(job), :].astype(jnp.bfloat16)
            give(kind, job).start()
        else:
            give(kind, job - shares).wait()
            span = block_span(job)
            got[span, :channels] = (total + got[span, :channels].astype(jnp.float32)).astype(jnp.bfloat16)
            if kind == 1:
                got[span, channels:] = (
                    hidden_sum[whole_span(job), :] + got[span, channels:].astype(jnp.float32)
                ).astype(jnp.bfloat16)
            second(kind, job).start()
    for kind in range(2):
        for job in range(shares, 2 * shares):
            second(kind, job).wait()
    own_g.wait()
    own_r.wait()
    own_s.wait()
    wait_parts(grad_stage, grad_ref, me, n, send_g, recv_g)
    for shift in range(1, n):
        branch_push(shift, True).wait_recv()
        branch_push(shift).wait_send()
        for step in range(1, steps):
            cot_push(step, shift).wait_send()


def mlp(n, shares, mixed, first, back, in_full, out_full, gain, shift):
    _, groups, block, group, side = mixed.shape
    hidden, channels = out_full.shape
    local = channels // n
    steps = block // LINES
    width = LINES * side
    shape = (n, steps, LINES, local, side)
    ring = 4
    low = functools.partial(jax.ShapeDtypeStruct, dtype=jnp.bfloat16)
    vmem = pl.BlockSpec(memory_space=pltpu.VMEM)
    hbm = pl.BlockSpec(memory_space=pl.ANY)
    return pl.pallas_call(
        functools.partial(mlp_kernel, n, shares),
        out_shape=(
            low(shape),
            low((n, steps // 4, *shape[2:])),
            low((n, steps - steps // 4, *shape[2:])),
            low((steps, hidden, width)),
            low((steps, hidden, width)),
            low((shares, hidden // 2 // shares, channels)),
            low((shares, hidden // 2 // shares, channels + side)),
            jax.ShapeDtypeStruct((channels, side), jnp.float32),
            jax.ShapeDtypeStruct((channels, side), jnp.float32),
        ),
        in_specs=[hbm] * 4 + [vmem] * 2 + [hbm],
        out_specs=(hbm,) * 7 + (vmem, vmem),
        scratch_shapes=[
            pltpu.VMEM(shape, jnp.bfloat16),
            pltpu.VMEM(shape, jnp.bfloat16),
            pltpu.VMEM((ring, STEP_HIDDEN, width), jnp.bfloat16),
            pltpu.VMEM((ring, STEP_HIDDEN, width), jnp.bfloat16),
            pltpu.VMEM((steps, channels, width), jnp.bfloat16),
            pltpu.VMEM((steps, channels, width), jnp.bfloat16),
            pltpu.VMEM((channels, width), jnp.float32),
            pltpu.VMEM((1, width), jnp.float32),
            pltpu.VMEM((channels, width), jnp.float32),
            pltpu.VMEM((channels, width), jnp.float32),
            pltpu.VMEM((hidden, side), jnp.float32),
            pltpu.VMEM((2, steps, hidden // 2 // shares, width), jnp.bfloat16),
            pltpu.VMEM((shares, hidden // 2 // shares, channels + side), jnp.bfloat16),
            pltpu.VMEM((hidden // 2, channels), jnp.bfloat16),
            pltpu.VMEM((hidden // 2, channels + side), jnp.bfloat16),
            pltpu.VMEM(back.shape, jnp.bfloat16),
            *(pltpu.VMEM(whole.shape, whole.dtype) for whole in (mixed, first, in_full, out_full)),
            pltpu.SemaphoreType.DMA((4,)),
            pltpu.SemaphoreType.DMA((n,)),
            pltpu.SemaphoreType.DMA((n,)),
            pltpu.SemaphoreType.DMA((steps, n)),
            pltpu.SemaphoreType.DMA((steps, n)),
            pltpu.SemaphoreType.DMA((n,)),
            pltpu.SemaphoreType.DMA((n,)),
            pltpu.SemaphoreType.DMA((4,)),
            pltpu.SemaphoreType.DMA((2, ring)),
            pltpu.SemaphoreType.DMA((2,)),
            pltpu.SemaphoreType.DMA((2, shares)),
            pltpu.SemaphoreType.DMA((2, shares)),
            pltpu.SemaphoreType.DMA((2, shares)),
            pltpu.SemaphoreType.DMA((2, shares)),
        ],
        compiler_params=pltpu.CompilerParams(
            collective_id=1, has_side_effects=True, vmem_limit_bytes=63 * mebi
        ),
        name="mlp",
    )(mixed, first, in_full, out_full, gain, shift, back)


def sum_rounds(n, shares, me, share, part, final, stage3, take3, keep3, keep4, send3, recv3, send4, recv4, own_sem):
    near, far = n // 2, me // 2
    core = lax.rem(me, 2)

    def third(turn):
        peer = lax.rem(far + turn, near)
        return push(stage3.at[peer], take3.at[turn], send3.at[turn], recv3.at[turn], chan=peer * 2 + core)

    def fourth(turn, back=False):
        holder = lax.rem(share + shares - turn, shares) if back else share
        peer = lax.rem(share + turn, shares)
        return push(keep4, final.at[holder], send4.at[turn], recv4.at[turn], dp=peer)

    def mine():
        return pltpu.make_async_copy(keep4, final.at[share], own_sem.at[0])

    def start_third():
        for at in range(near):
            total = part(at)
            stage3[at] = total.astype(jnp.bfloat16)

            @pl.when(far == at)
            def _():
                keep3[...] = total

        for turn in range(1, near):
            third(turn).start()

    def start_fourth():
        for turn in range(1, near):
            third(turn).wait()
        total = keep3[...]
        for turn in range(1, near):
            total = total + take3[turn].astype(jnp.float32)
        keep4[...] = total.astype(jnp.bfloat16)
        mine().start()
        for turn in range(1, shares):
            fourth(turn).start()

    def finish():
        mine().wait()
        for turn in range(1, shares):
            fourth(turn, True).wait_recv()
            fourth(turn).wait_send()

    return start_third, start_fourth, finish


def back_kernel(
    n,
    shares,
    sizes_ref,
    image_hbm,
    cot_hbm,
    grad_hbm,
    branch_sent_hbm,
    branch_ref,
    rows_back_ref,
    rows_ref,
    cols_back_ref,
    skip_ref,
    scale_ref,
    bias_ref,
    bias_sums_ref,
    gain_sums_ref,
    shift_sums_ref,
    out_take_hbm,
    in_half_ref,
    output_ref,
    input_grad_ref,
    small_ref,
    late_ref,
    norm_ref,
    out_final_ref,
    in_final_ref,
    wide,
    branch_got,
    rows_sums,
    cols_sums,
    skip_sums,
    scale_sums,
    small_own,
    small_got,
    late_own,
    late_got,
    norm_own,
    norm_near,
    norm_mid,
    norm_far,
    in_take,
    image_ref,
    cot_ref,
    grad_ref,
    branch_sent_ref,
    out_take_ref,
    load_sem,
    out_stage3,
    out_take3,
    out_keep3,
    out_keep4,
    in_stage3,
    in_take3,
    in_keep3,
    in_keep4,
    send_sem,
    recv_sem,
    own_sem,
    send_2,
    recv_2,
    send_s,
    recv_s,
    send_l,
    recv_l,
    send_n,
    recv_n,
    send_f,
    recv_f,
    *round_sems,
):
    loads = [
        pltpu.make_async_copy(whole, here, load_sem.at[at])
        for at, (whole, here) in enumerate(
            (
                (out_take_hbm, out_take_ref),
                (grad_hbm, grad_ref),
                (image_hbm, image_ref),
                (cot_hbm, cot_ref),
                (branch_sent_hbm, branch_sent_ref),
            )
        )
    ]
    for copy in loads:
        copy.start()
    count, side, _ = image_ref.shape
    late, lines = branch_ref.shape[1], branch_ref.shape[2]
    early = branch_sent_ref.shape[1]
    near = n // 2
    rows = in_keep3.shape[0]
    me, share = meet(n, shares)

    def summed(take):
        return lambda at: sum(take[turn, at * rows : (at + 1) * rows].astype(jnp.float32) for turn in range(shares))

    out_third, out_fourth, out_finish = sum_rounds(
        n, shares, me, share, summed(out_take_ref), out_final_ref, out_stage3, out_take3, out_keep3, out_keep4, *round_sems[:5]
    )
    in_third, in_fourth, in_finish = sum_rounds(
        n, shares, me, share, summed(in_take), in_final_ref, in_stage3, in_take3, in_keep3, in_keep4, *round_sems[5:]
    )

    def in_second(turn):
        peer = lax.rem(share + turn, shares)
        if turn == 0:
            return pltpu.make_async_copy(in_half_ref.at[peer], in_take.at[0], send_2.at[0])
        return push(in_half_ref.at[peer], in_take.at[turn], send_2.at[turn], recv_2.at[turn], dp=peer)

    def branch_push(step, shift, back=False):
        peer = lax.rem(me + shift, n)
        return push(
            branch_ref.at[peer, step],
            branch_got.at[lax.rem(me + n - shift, n) if back else me, step],
            send_sem.at[step, shift],
            recv_sem.at[step, shift],
            chan=peer,
        )

    def start_branch(step):
        for shift in range(1, n):
            branch_push(step, shift).start()

    def norm_first(turn):
        peer = lax.rem(share + turn, shares)
        return push(norm_own, norm_near.at[turn], send_n.at[turn], recv_n.at[turn], dp=peer)

    def norm_second(turn):
        peer = lax.rem(me + turn, n)
        return push(norm_mid, norm_far.at[turn], send_f.at[turn], recv_f.at[turn], chan=peer)

    def small_push(turn):
        peer = lax.rem(share + turn, shares)
        return push(small_own, small_got.at[turn], send_s.at[turn], recv_s.at[turn], dp=peer)

    def late_push(turn):
        peer = lax.rem(share + turn, shares)
        return push(late_own, late_got.at[turn], send_l.at[turn], recv_l.at[turn], dp=peer)

    def norm_pass():
        total = norm_own[...]
        for turn in range(1, shares):
            norm_first(turn).wait()
            total = total + norm_near[turn]
        norm_mid[...] = total
        for turn in range(1, n):
            norm_second(turn).start()

    def in_pass():
        for turn in range(shares):
            in_second(turn).wait()
        in_third()
        start_branch(late - 1)

    top = lax.broadcasted_iota(jnp.int32, norm_own.shape, 0) == 0
    norm_own[...] = jnp.where(top, lane_sums(gain_sums_ref[...]), lane_sums(shift_sums_ref[...]))
    for turn in range(1, shares):
        norm_first(turn).start()
    for turn in range(shares):
        in_second(turn).start()
    loads[0].wait()
    out_third()
    for step in range(late - 1):
        start_branch(step)
    for copy in loads[1:]:
        copy.wait()
    own = pltpu.make_async_copy(branch_ref.at[me], branch_got.at[me], own_sem.at[0])
    own.start()
    row_at = lax.broadcasted_iota(jnp.int32, (side, side), 0)
    col_at = lax.broadcasted_iota(jnp.int32, (side, side), 1)
    inside = (row_at < sizes_ref[0]) & (col_at < sizes_ref[1])
    lower = row_at >= col_at
    upper = row_at <= col_at
    flip = (row_at + col_at == side - 1).astype(jnp.bfloat16)

    @pl.loop(0, side)
    def _(row):
        span = pl.ds(pl.multiple_of(row * count, count), count)
        wide[span, :] = grad_ref[row].astype(jnp.float32)

    def one_channel(chan):
        one = pl.ds(chan, 1)
        grad = wide[pl.ds(chan, side, stride=count), :]
        image = image_ref[chan].astype(jnp.float32)
        grad_out = jnp.where(inside, cot_ref[chan].astype(jnp.float32), 0.0)
        masked = jnp.where(inside, image, 0.0)
        skip_sums[one, :] = jnp.sum(grad * masked, axis=0, keepdims=True)
        masked_low = masked.astype(jnp.bfloat16)
        grad_low = grad.astype(jnp.bfloat16)
        grad_turned = dot_nt(flip, grad_low).astype(jnp.bfloat16)
        masked_turned = dot_nn(flip, masked_low).astype(jnp.bfloat16)
        rows_high, rows_low = split_low(lag_matrix(rows_back_ref[one, :], side, lower))
        turned_high, turned_low = split_low(lag_matrix(rows_ref[one, :], side, upper))
        cols_high, cols_low = split_low(lag_matrix(cols_back_ref[one, :], side, lower))
        along = dot_nn(
            jnp.concatenate([rows_high, rows_low], axis=1),
            jnp.concatenate([masked_low, masked_low], axis=0),
        )
        along_grad = dot_nn(
            jnp.concatenate([grad_low, grad_low], axis=1),
            jnp.concatenate([cols_high, cols_low], axis=0),
        )
        along_high, along_low = split_low(along)
        grad_high, grad_rest = split_low(along_grad)
        cols_grad = dot_nn(
            jnp.concatenate([grad_turned, grad_turned], axis=1),
            jnp.concatenate([along_high, along_low], axis=0),
        )
        rows_grad = dot_nt(
            jnp.concatenate([grad_high, grad_rest], axis=1),
            jnp.concatenate([masked_turned, masked_turned], axis=1),
        )
        masked_grad = dot_nn(
            jnp.concatenate([turned_high, turned_low], axis=1),
            jnp.concatenate([grad_high, grad_high], axis=0),
        ) + dot_nn(turned_high, grad_rest)
        masked_grad = masked_grad + skip_ref[chan] * grad
        input_grad_ref[chan] = jnp.where(inside, grad_out + masked_grad, 0.0)
        rows_sums[one, :] = lag_sums(rows_grad, side, row_at + col_at >= side - 1)
        cols_sums[one, :] = lag_sums(cols_grad, side, row_at + col_at <= side - 1)

    @pl.loop(0, count // ABREAST)
    def _(few):
        pl.when(few == count // ABREAST * 7 // 8)(in_pass)
        pl.when(few == count // ABREAST * 7 // 8)(out_fourth)
        pl.when(few == count // ABREAST * 7 // 8)(norm_pass)
        for at in range(ABREAST):
            one_channel(few * ABREAST + at)

    small_own[:, :side] = rows_sums[...]
    small_own[:, side : 2 * side] = cols_sums[...]
    lane = lax.broadcasted_iota(jnp.int32, (count, side), 1)
    last = jnp.zeros((count, side), jnp.float32)
    for at, sums in enumerate((skip_sums, bias_sums_ref)):
        last = jnp.where(lane == at, jnp.sum(sums[...], axis=1, keepdims=True), last)
    small_own[:, 2 * side :] = last
    for turn in range(1, shares):
        small_push(turn).start()
    in_fourth()
    def widen(step):
        part = branch_sent_ref if step < early else branch_got
        at = step if step < early else step - early

        @pl.loop(0, n)
        def _(owner):
            for line in range(lines):
                row = (owner * (early + late) + step) * lines + line
                wide[pl.ds(pl.multiple_of(row * count, count), count), :] = part[owner, at, line].astype(jnp.float32)

    own.wait()
    for step in range(early):
        widen(step)
    for step in range(late):
        for shift in range(1, n):
            branch_push(step, shift, True).wait_recv()
            branch_push(step, shift).wait_send()
        widen(early + step)

    @pl.loop(0, count // 4)
    def _(few):
        for at in range(4):
            chan = few * 4 + at
            shifted = wide[pl.ds(chan, side, stride=count), :] + bias_ref[chan]
            image = image_ref[chan].astype(jnp.float32)
            grad_out = jnp.where(inside, cot_ref[chan].astype(jnp.float32), 0.0)
            output_ref[chan] = jnp.where(inside, image + scale_ref[chan] * shifted, 0.0).astype(jnp.bfloat16)
            scale_sums[pl.ds(chan, 1), :] = jnp.sum(grad_out * shifted, axis=0, keepdims=True)

    late_own[...] = jnp.zeros_like(late_own)
    late_own[:, :count] = lane_sums(scale_sums[...])
    for turn in range(1, shares):
        late_push(turn).start()
    total = norm_mid[...]
    for turn in range(1, n):
        norm_second(turn).wait()
        total = total + norm_far[turn]
    norm_ref[...] = total
    out_finish()
    in_finish()
    total = small_own[...]
    for turn in range(1, shares):
        small_push(turn).wait()
        total = total + small_got[turn]
    small_ref[...] = total
    total = late_own[...]
    for turn in range(1, shares):
        late_push(turn).wait()
        total = total + late_got[turn]
    late_ref[...] = total


def mixer_back(n, shares, sizes, images, cotangent, grad, branch_sent, branch, lines, vectors, norms, sums):
    count, side, _ = images.shape
    near = n // 2
    block, channels = sums[0].shape[1:]
    rows = block // near
    wide = sums[1].shape[2]
    line = pltpu.VMEM((count, side), jnp.float32)
    norm = pltpu.VMEM((8, channels), jnp.float32)
    vmem = pl.BlockSpec(memory_space=pltpu.VMEM)
    hbm = pl.BlockSpec(memory_space=pl.ANY)
    full = functools.partial(jax.ShapeDtypeStruct, dtype=jnp.float32)
    return pl.pallas_call(
        functools.partial(back_kernel, n, shares),
        out_shape=(
            jax.ShapeDtypeStruct(images.shape, jnp.bfloat16),
            full(images.shape),
            full((count, 3 * side)),
            full((8, side)),
            full((8, channels)),
            jax.ShapeDtypeStruct((shares, rows, channels), jnp.bfloat16),
            jax.ShapeDtypeStruct((shares, rows, wide), jnp.bfloat16),
        ),
        in_specs=[pl.BlockSpec(memory_space=pltpu.SMEM)]
        + [hbm] * 5
        + [vmem] * len(lines)
        + [pl.BlockSpec(memory_space=pltpu.SMEM)] * len(vectors)
        + [vmem] * len(norms)
        + [hbm] * 2,
        out_specs=(vmem,) * 5 + (hbm,) * 2,
        scratch_shapes=[
            pltpu.VMEM((count * side, side), jnp.float32),
            pltpu.VMEM(branch.shape, jnp.bfloat16),
            line,
            line,
            line,
            line,
            pltpu.VMEM((count, 3 * side), jnp.float32),
            pltpu.VMEM((shares, count, 3 * side), jnp.float32),
            pltpu.VMEM((8, side), jnp.float32),
            pltpu.VMEM((shares, 8, side), jnp.float32),
            norm,
            pltpu.VMEM((shares, 8, channels), jnp.float32),
            norm,
            pltpu.VMEM((n, 8, channels), jnp.float32),
            pltpu.VMEM(sums[1].shape, jnp.bfloat16),
            *(pltpu.VMEM(whole.shape, whole.dtype) for whole in (images, cotangent, grad, branch_sent, sums[0])),
            pltpu.SemaphoreType.DMA((5,)),
        ]
        + [
            kind
            for columns in (channels, wide)
            for kind in (
                pltpu.VMEM((near, rows, columns), jnp.bfloat16),
                pltpu.VMEM((near, rows, columns), jnp.bfloat16),
                pltpu.VMEM((rows, columns), jnp.float32),
                pltpu.VMEM((rows, columns), jnp.bfloat16),
            )
        ]
        + [
            pltpu.SemaphoreType.DMA(size if isinstance(size, tuple) else (size,))
            for size in ((branch.shape[1], n), (branch.shape[1], n), 1, *(shares,) * 8, n, n)
            + (near, near, shares, shares, 1) * 2
        ],
        compiler_params=pltpu.CompilerParams(
            collective_id=2, has_side_effects=True, vmem_limit_bytes=62 * mebi
        ),
        name="mixer_back",
    )(sizes, images, cotangent, grad, branch_sent, branch, *lines, *vectors, *norms, *sums)


def taps_kernel(small_ref, *refs):
    params, (*grads, rest_ref), wide, turned = refs[:8], refs[8:17], refs[17], refs[18]
    count = small_ref.shape[0]
    side = wide.shape[0]
    wide[...] = jnp.zeros_like(wide)

    def turn(at):
        wide[:count, :] = small_ref[:, at * side : (at + 1) * side]
        turned[...] = wide[...].T

    def rows_load(lag):
        return turned[pl.ds(lax.rem(lag + side - 1, side), 1), :count]

    def cols_load(lag):
        return turned[pl.ds(side - 1 - lag, 1), :count]

    for at, load in enumerate((rows_load, cols_load)):
        turn(at)
        found = taps_adjoint(*(ref[...] for ref in params[4 * at : 4 * at + 4]), side, load)
        for ref, grad in zip(grads[4 * at : 4 * at + 4], found):
            ref[...] = grad
    turn(2)
    rest_ref[...] = turned[:8, :count]


def taps_back(small, params, side):
    modes, count = params[0].shape
    full = functools.partial(jax.ShapeDtypeStruct, dtype=jnp.float32)
    vmem = pl.BlockSpec(memory_space=pltpu.VMEM)
    return pl.pallas_call(
        taps_kernel,
        out_shape=(full((modes, count)),) * 8 + (full((8, count)),),
        in_specs=[vmem] * 9,
        out_specs=(vmem,) * 9,
        scratch_shapes=[pltpu.VMEM((side, side), jnp.float32), pltpu.VMEM((side, side), jnp.float32)],
        name="taps_back",
    )(small, *params)


def pixel_body(
    n,
    images,
    cotangent,
    image_sizes,
    slot_image,
    rows_rate,
    rows_freq,
    rows_real,
    rows_imag,
    cols_rate,
    cols_freq,
    cols_real,
    cols_imag,
    skip_gain,
    norm_gain,
    norm_bias,
    weight_in,
    bias_in,
    weight_out,
    bias_out,
    layer_scale,
):
    _, count, side, _ = images.shape
    channels = norm_gain.shape[0]
    picked = slot_image[lax.axis_index("dp")]
    sizes = image_sizes[picked]
    image, cot = images[0], cotangent[0]

    params = tuple(
        param.T
        for param in (
            rows_rate,
            rows_freq,
            rows_real,
            rows_imag,
            cols_rate,
            cols_freq,
            cols_real,
            cols_imag,
        )
    )
    shares = lax.axis_size("dp")
    hidden = weight_out.shape[0]
    spread = jnp.broadcast_to(bias_in[:, None], (hidden, side))
    in_part = jnp.concatenate([weight_in.T, spread], axis=1).reshape(shares, -1, channels + side)
    out_part = weight_out.reshape(shares, -1, channels)
    mixed, first, back, in_whole, out_whole, bias_out_sums, rows_back, rows, cols_back, _ = mixer_forward(
        n, shares, sizes, image, cot, skip_gain, layer_scale, params, in_part, out_part
    )
    grad, branch_sent, branch, _, _, *sums, gain_sums, shift_sums = mlp(
        n,
        shares,
        mixed,
        first,
        back,
        in_whole.reshape(-1, channels + side),
        out_whole.reshape(-1, channels),
        jnp.broadcast_to(norm_gain[:, None], (channels, side)),
        jnp.broadcast_to(norm_bias[:, None], (channels, side)),
    )
    output, input_grad, small, late, norms, out_final, in_final = mixer_back(
        n,
        shares,
        sizes,
        image,
        cot,
        grad.reshape(side, count, side),
        branch_sent,
        branch,
        (rows_back, rows, cols_back),
        (skip_gain, layer_scale, bias_out),
        (bias_out_sums, gain_sums, shift_sums),
        sums,
    )
    *params_grad, rest = taps_back(small, params, side)
    in_final = in_final.reshape(hidden, channels + side).astype(jnp.float32)
    return (
        output[None],
        input_grad[None],
        *(grad.T for grad in params_grad),
        rest[0],
        norms[0],
        norms[1],
        in_final[:, :channels].T,
        jnp.sum(in_final[:, channels:], axis=1),
        out_final.reshape(hidden, channels).astype(jnp.float32),
        rest[1],
        late[0, :count],
    )


def choose_body(n, images, *rest):
    slots, count, side, _ = images.shape
    fits = (
        slots == 1
        and side == 128
        and count <= side
        and count % GROUP == 0
        and side % (4 * n * LINES) == 0
        and n == 8
        and (rest[15].shape[0] * n) % STEP_HIDDEN == 0
        and rest[15].shape[0] % (16 * lax.axis_size("dp")) == 0
        and lax.axis_size("dp") > 1
    )
    return pixel_body(n, images, *rest) if fits else plain_body(images, *rest)


def solution(mesh):
    in_specs = (
        P("dp", "chan", None, None),
        P("dp", "chan", None, None),
        P(),
        P(),
        P("chan", None),
        P("chan", None),
        P("chan", None),
        P("chan", None),
        P("chan", None),
        P("chan", None),
        P("chan", None),
        P("chan", None),
        P("chan"),
        P(),
        P(),
        P(None, "chan"),
        P("chan"),
        P("chan", None),
        P("chan"),
        P("chan"),
    )
    out_specs = (
        P("dp", "chan", None, None),
        P("dp", "chan", None, None),
        P("chan", None),
        P("chan", None),
        P("chan", None),
        P("chan", None),
        P("chan", None),
        P("chan", None),
        P("chan", None),
        P("chan", None),
        P("chan"),
        P(),
        P(),
        P(None, "chan"),
        P("chan"),
        P("chan", None),
        P("chan"),
        P("chan"),
    )
    return jax.shard_map(functools.partial(choose_body, mesh.shape["chan"]), mesh=mesh, in_specs=in_specs, out_specs=out_specs, check_vma=False)
```
